32 devices in a mesh: grp: 2 (over x), cell: 16 (over z, y, core).
Axes of the slice: x: 2, y: 2, z: 4, core: 2. Of those that a mesh axis runs over, the one named last changes fastest.
Arguments:
- fields: bfloat16 [8192, 3, 8192], P(('grp', 'cell')), parts along dimension 0, may hold values from -6 to 6
- horiz: float32 [16384], P(('grp', 'cell')), parts along dimension 0, may hold values from 0.2 to 1
- vertical: float32 [16384], P(('grp', 'cell')), parts along dimension 0, may hold values from 1.5 to 6
- tilt_angle: float32 [16384], P(('grp', 'cell')), parts along dimension 0, may hold values from 0.2 to 1.4
- azimuth: float32 [16384], P(('grp', 'cell')), parts along dimension 0, may hold values from -3.140625 to 3.140625
- electrode_quads: int32 [4096, 4], P('grp'), parts along dimension 0, may hold values from 0 to 4095, as said below
Outputs:
- jacobian: bfloat16 [4096, 4, 8192], P('grp', None, 'cell'), parts along dimension 0
- coverage: float32 [16384], P(('grp', 'cell')), parts along dimension 0
The draws below stay inside these ranges and needn't reach their ends.
There are 2 independent parts, one for each index of `grp`. The reference program is written for one: setup_inputs(seed, part) draws one part's arguments, and reference() takes and returns one part's arrays. A program takes and returns all parts, laid end to end along the dimension named above; each array names one. Nothing has to cross between parts.
Inputs may be any that keep to these rules, and one draw needn't show every extreme that they name: `electrode_quads`: each row names four different electrodes.
All inputs are finite; a program needn't handle non-finite values.
Results may differ from the reference program's by a relative error of at most 0.001.
Values may be sent and summed in bfloat16 or wider, within the bound.
No kernel may reach another device: no remote copies, remote signals or barrier semaphores. Data moves between devices by JAX's collectives and lax.ppermute only.
A program may use at most 192 MiB of HBM per device.

```python
import math
import jax
import jax.numpy as jnp
from jax import lax

ELECTRODE_COUNT = 4096
QUAD_READINGS = 2048
CELL_TOTAL = 8192


def draw_electrode_quads(key, part):
    random_keys = jax.random.split(key, 4)
    base_offset = jax.random.randint(random_keys[0], (QUAD_READINGS,), 0, ELECTRODE_COUNT)
    base_offset = base_offset.at[0].set(ELECTRODE_COUNT - 1).at[1].set(0)
    quarter_size = ELECTRODE_COUNT // 4
    first_quarter = jax.random.randint(random_keys[1], (QUAD_READINGS,), 1, quarter_size)
    second_quarter = jax.random.randint(random_keys[2], (QUAD_READINGS,), quarter_size, 2 * quarter_size)
    third_quarter = jax.random.randint(random_keys[3], (QUAD_READINGS,), 2 * quarter_size, 3 * quarter_size)
    return jnp.stack([base_offset, (base_offset + first_quarter) % ELECTRODE_COUNT, (base_offset + second_quarter) % ELECTRODE_COUNT, (base_offset + third_quarter) % ELECTRODE_COUNT], axis=1).astype(jnp.int32)


def block_scale(own_key, dims, cuts, low, top_value):
    def one(dim, blocks):
        steps = jax.random.uniform(jax.random.fold_in(jax.random.fold_in(own_key, 6), dim), (blocks,), jnp.float32, low / len(cuts), top_value / len(cuts))
        return jnp.repeat(jnp.exp(steps), dims[dim] // blocks).reshape((-1,) + (1,) * (len(dims) - dim - 1))

    level = one(*cuts[0])
    for cut in cuts[1:]:
        level = level * one(*cut)
    return level


def gaussian(rng, extent, width, most, cuts=(), held_as=jnp.bfloat16):
    drawn = width * jax.random.normal(rng, extent, jnp.float32)
    if cuts:
        drawn = drawn * block_scale(rng, extent, cuts, -0.22, 0.18)
    return jnp.clip(drawn, -most, most).astype(held_as)


def setup_inputs(seed: int = 0, part: int = 0) -> dict:
    streams_of = jax.random.split(jax.random.key(seed), 7)
    part_keys = jax.random.split(jax.random.fold_in(streams_of[6], part), 7)
    fields = gaussian(part_keys[0], (ELECTRODE_COUNT, 3, CELL_TOTAL), 1.0, 6.0, ((0, 16),))
    horiz = jnp.clip(jnp.exp(math.log(1.0) - 1.609438 * jax.random.uniform(part_keys[1], (CELL_TOTAL,), jnp.float32) ** block_scale(part_keys[1], (CELL_TOTAL,), ((0, 16),), -0.2, 0.2)), 0.2, 1.0)
    vertical = jnp.clip(jnp.exp(math.log(6.0) - 1.3862944 * jax.random.uniform(part_keys[2], (CELL_TOTAL,), jnp.float32) ** block_scale(part_keys[2], (CELL_TOTAL,), ((0, 16),), -0.2, 0.2)), 1.5, 6.0)
    tilt_angle = jnp.clip(0.2 + 1.19999997 * jax.random.uniform(part_keys[3], (CELL_TOTAL,), jnp.float32) ** block_scale(part_keys[3], (CELL_TOTAL,), ((0, 16),), -0.2, 0.2), 0.2, 1.4)
    azimuth = jnp.clip(jax.random.uniform(part_keys[4], (CELL_TOTAL,), jnp.float32, -3.140625, 3.140625), -3.140625, 3.140625)
    electrode_quads = draw_electrode_quads(jax.random.fold_in(jax.random.fold_in(streams_of[6], part), 71), part)
    return {"fields": fields, "horiz": horiz, "vertical": vertical, "tilt_angle": tilt_angle, "azimuth": azimuth, "electrode_quads": electrode_quads}


def sensitivity(grads, horiz, vertical, tilt_angle, azimuth, rows):

    def pick(column):
        return jnp.take(grads, rows[:, column], axis=0).astype(jnp.float32)
    source = pick(0) - pick(1)
    receiver = pick(2) - pick(3)
    sin_t = jnp.sin(tilt_angle)
    cos_t = jnp.cos(tilt_angle)
    sin_p = jnp.sin(azimuth)
    cos_p = jnp.cos(azimuth)
    axis_dir = jnp.stack([sin_t * cos_p, sin_t * sin_p, cos_t])
    tilt_dir = jnp.stack([cos_t * cos_p, cos_t * sin_p, -sin_t])
    turn_dir = jnp.stack([-sin_t * sin_p, sin_t * cos_p, jnp.zeros_like(sin_t)])

    def along(field, direction):
        return lax.optimization_barrier(jnp.sum(field * direction[None], axis=1))
    s_axis = along(source, axis_dir)
    r_axis = along(receiver, axis_dir)
    s_tilt = along(source, tilt_dir)
    r_tilt = along(receiver, tilt_dir)
    s_turn = along(source, turn_dir)
    r_turn = along(receiver, turn_dir)
    inner = lax.optimization_barrier(jnp.sum(source * receiver, axis=1))
    contrast = vertical - horiz
    return jnp.stack([-horiz * (inner - s_axis * r_axis), -vertical * s_axis * r_axis, -contrast * (s_tilt * r_axis + s_axis * r_tilt), -contrast * (s_turn * r_axis + s_axis * r_turn)], axis=1)

def reference(fields, horiz, vertical, tilt_angle, azimuth, electrode_quads):
    block_slice = min(128, QUAD_READINGS)
    block_count = QUAD_READINGS // block_slice

    def one_block(rows):
        values = sensitivity(fields, horiz, vertical, tilt_angle, azimuth, rows)
        meansq = lax.optimization_barrier(jnp.sum(values * values, axis=(1, 2))) / (4.0 * CELL_TOTAL)
        normed = values * lax.rsqrt(meansq + 1e-06)[:, None, None]
        return (normed.astype(jnp.bfloat16), lax.optimization_barrier(jnp.sum(normed * normed, axis=(0, 1))))
    jacobian_blocks, coverage_blocks = lax.map(one_block, electrode_quads.reshape(block_count, block_slice, 4))
    return (jacobian_blocks.reshape(QUAD_READINGS, 4, CELL_TOTAL), lax.optimization_barrier(jnp.sum(coverage_blocks, axis=0)))
```

```python
import functools

import jax
import jax.numpy as jnp
from jax import lax
from jax.experimental import pallas as pl
from jax.experimental.pallas import tpu as pltpu
from jax.sharding import PartitionSpec as P

LANES = 128
SUBLANES = 8
UNROLL = 4
FILL_STEPS = 4
GROUP_ROWS = 512
PAD = 4
MIB = 1 << 20
VMEM_LIMIT = 56 * MIB


def send_order_kernel(first, fields_ref, out_ref, held, in_sems, out_sems):
    shards, _, _, width = held.shape
    cell_dev = fields_ref.shape[2] // shards
    arrive = [
        pltpu.make_async_copy(fields_ref.at[:, :, pl.ds(d * cell_dev + first, width)], held.at[d], in_sems.at[d])
        for d in range(shards)
    ]
    leave = [pltpu.make_async_copy(held.at[d], out_ref.at[d], out_sems.at[d]) for d in range(shards)]
    for copy in arrive:
        copy.start()
    for d in range(shards):
        arrive[d].wait()
        leave[d].start()
    for copy in leave:
        copy.wait()


def send_order(fields, shards, first, width):
    comps, owned, cells = fields.shape
    shape = (shards, comps, owned, width)
    return pl.pallas_call(
        functools.partial(send_order_kernel, first),
        in_specs=[pl.BlockSpec(memory_space=pl.ANY)],
        out_specs=pl.BlockSpec(memory_space=pl.ANY),
        out_shape=jax.ShapeDtypeStruct(shape, fields.dtype),
        scratch_shapes=[
            pltpu.VMEM(shape, fields.dtype),
            pltpu.SemaphoreType.DMA((shards,)),
            pltpu.SemaphoreType.DMA((shards,)),
        ],
        cost_estimate=pl.CostEstimate(flops=0, bytes_accessed=4 * comps * owned * width * shards, transcendentals=0),
        compiler_params=pltpu.CompilerParams(vmem_limit_bytes=VMEM_LIMIT),
        name="send_order",
    )(fields)


def sens_kernel(fill_steps, group_rows, rows_ref, fields_ref, coef_ref, sens_ref, sumsq_ref, table, picked, squares):
    step = pl.program_id(1)
    sources, comps, owned = fields_ref.shape[:3]

    @pl.when(step < fill_steps)
    def _():
        for source in range(sources):
            base = (step * sources + source) * (owned * PAD)
            for comp in range(comps):
                block = fields_ref[source, comp].astype(jnp.float32)
                table[pl.ds(base + comp, owned, stride=PAD), :] = block

    @pl.when(step >= fill_steps)
    def _():
        total = rows_ref.shape[0] // 4
        first = (step - fill_steps) * group_rows
        coef = [coef_ref[pl.ds(k, 1), :] for k in range(11)]
        ax, ay, az, tx, ty, tz, ux, uy, nh, nv, nc = coef

        def fetch(index):
            return table[pl.ds(pl.multiple_of(rows_ref[index], PAD), PAD), :]

        @pl.loop(0, group_rows // (SUBLANES * UNROLL))
        def _(batch):
            start = first + batch * (SUBLANES * UNROLL)
            for j in range(SUBLANES * UNROLL):
                i = start + j
                picked[pl.ds(j * 2 * PAD, PAD), :] = fetch(i) - fetch(total + i)
                picked[pl.ds(j * 2 * PAD + PAD, PAD), :] = fetch(2 * total + i) - fetch(3 * total + i)
            for g in range(UNROLL):
                spot = g * SUBLANES * 2 * PAD
                group = batch * UNROLL + g
                sx, sy, sz = (picked[pl.ds(spot + k, SUBLANES, stride=2 * PAD), :] for k in range(3))
                rx, ry, rz = (picked[pl.ds(spot + PAD + k, SUBLANES, stride=2 * PAD), :] for k in range(3))
                sn = sx * ax + sy * ay + sz * az
                rn = rx * ax + ry * ay + rz * az
                st = sx * tx + sy * ty + sz * tz
                rt = rx * tx + ry * ty + rz * tz
                sp = sx * ux + sy * uy
                rp = rx * ux + ry * uy
                dot = sx * rx + sy * ry + sz * rz
                both = sn * rn
                values = (nh * (dot - both), nv * both, nc * (st * rn + sn * rt), nc * (sp * rn + sn * rp))
                for k in range(4):
                    sens_ref[0, pl.ds(group * (SUBLANES * 4) + k, SUBLANES, stride=4), :] = values[k]
                squares[pl.ds(group * SUBLANES, SUBLANES), :] = (
                    values[0] * values[0] + values[1] * values[1] + values[2] * values[2] + values[3] * values[3]
                )

        for k in range(group_rows // LANES):
            turned = squares[pl.ds(k * LANES, LANES), :].T
            sumsq_ref[0, 0, pl.ds(k, 1), :] = jnp.sum(turned, axis=0, keepdims=True)


def sens_chunk(rows, fields, coef, group_rows, fill_steps):
    shards, comps, owned, width = fields.shape
    blocks = width // LANES
    total = rows.shape[0] // 4
    groups = total // group_rows
    return pl.pallas_call(
        functools.partial(sens_kernel, fill_steps, group_rows),
        grid=(blocks, fill_steps + groups),
        in_specs=[
            pl.BlockSpec(memory_space=pltpu.SMEM),
            pl.BlockSpec(
                (shards // fill_steps, comps, owned, LANES),
                lambda b, i: (jnp.minimum(i, fill_steps - 1), 0, 0, b),
            ),
            pl.BlockSpec((16, LANES), lambda b, i: (0, b)),
        ],
        out_specs=[
            pl.BlockSpec((1, group_rows * 4, LANES), lambda b, i: (b, jnp.maximum(i - fill_steps, 0), 0)),
            pl.BlockSpec((1, 1, group_rows // LANES, LANES), lambda b, i: (b, jnp.maximum(i - fill_steps, 0), 0, 0)),
        ],
        out_shape=[
            jax.ShapeDtypeStruct((blocks, total * 4, LANES), jnp.float32),
            jax.ShapeDtypeStruct((blocks, groups, group_rows // LANES, LANES), jnp.float32),
        ],
        scratch_shapes=[
            pltpu.VMEM((shards * owned * PAD, LANES), jnp.float32),
            pltpu.VMEM((UNROLL * SUBLANES * 2 * PAD, LANES), jnp.float32),
            pltpu.VMEM((group_rows, LANES), jnp.float32),
        ],
        cost_estimate=pl.CostEstimate(
            flops=blocks * total * LANES * 64,
            bytes_accessed=blocks * (shards * comps * owned * LANES * 2 + total * 5 * LANES * 4) * 4,
            transcendentals=0,
        ),
        compiler_params=pltpu.CompilerParams(vmem_limit_bytes=VMEM_LIMIT),
        name="sens_chunk",
    )(rows, fields, coef)


def scale_kernel(counts, inverse, meansq_ref, *refs):
    sens_refs, (out_ref, cover_ref, spread, cover) = refs[: len(counts)], refs[len(counts) :]
    rows = sens_refs[0].shape[1]
    step = pl.program_id(0)

    @pl.when(step == 0)
    def _():
        cover[...] = jnp.zeros_like(cover)

    for k in range(rows // (4 * LANES)):
        scale = lax.rsqrt(meansq_ref[0, pl.ds(k, 1), :] * inverse + 1e-06)
        column = jnp.broadcast_to(scale, (LANES, LANES)).T
        for p in range(4):
            spread[pl.ds(k * 4 * LANES + p, LANES, stride=4), :] = column
    place = 0
    for ref, blocks in zip(sens_refs, counts):
        for b in range(blocks):
            normed = ref[b] * spread[...]
            out_ref[:, :, place * LANES : (place + 1) * LANES] = normed.astype(out_ref.dtype).reshape(rows // 4, 4, LANES)
            squares = (normed * normed).reshape(rows // SUBLANES, SUBLANES, LANES)
            cover[pl.ds(place * SUBLANES, SUBLANES), :] += jnp.sum(squares, axis=0)
            place += 1

    @pl.when(step == pl.num_programs(0) - 1)
    def _():
        for k in range(place):
            cover_ref[pl.ds(k, 1), :] = jnp.sum(cover[pl.ds(k * SUBLANES, SUBLANES), :], axis=0, keepdims=True)


def scaled(sumsq, inverse, sens, step_rows):
    counts = tuple(s.shape[0] for s in sens)
    columns = sum(counts)
    total = sens[0].shape[1] // 4
    rows = step_rows * 4
    out, cover = pl.pallas_call(
        functools.partial(scale_kernel, counts, inverse),
        grid=(total // step_rows,),
        in_specs=[pl.BlockSpec((1, step_rows // LANES, LANES), lambda i: (i, 0, 0))]
        + [pl.BlockSpec((c, rows, LANES), lambda i: (0, i, 0)) for c in counts],
        out_specs=[
            pl.BlockSpec((step_rows, 4, columns * LANES), lambda i: (i, 0, 0)),
            pl.BlockSpec((columns, LANES), lambda i: (0, 0)),
        ],
        out_shape=[
            jax.ShapeDtypeStruct((total, 4, columns * LANES), jnp.bfloat16),
            jax.ShapeDtypeStruct((columns, LANES), jnp.float32),
        ],
        scratch_shapes=[pltpu.VMEM((rows, LANES), jnp.float32), pltpu.VMEM((columns * SUBLANES, LANES), jnp.float32)],
        compiler_params=pltpu.CompilerParams(vmem_limit_bytes=VMEM_LIMIT),
        name="scaled",
    )(sumsq.reshape(total // step_rows, step_rows // LANES, LANES), *sens)
    return out, cover.reshape(columns * LANES)


def sum_over_cells(x, shards):
    if shards & (shards - 1):
        return lax.psum(x, "cell")
    bit = 1
    while bit < shards:
        x = x + lax.ppermute(x, "cell", [(i, i ^ bit) for i in range(shards)])
        bit *= 2
    return x


def coefficients(horiz, vertical, tilt_angle, azimuth):
    sin_t, cos_t = jnp.sin(tilt_angle), jnp.cos(tilt_angle)
    sin_p, cos_p = jnp.sin(azimuth), jnp.cos(azimuth)
    zero = jnp.zeros_like(horiz)
    return jnp.stack(
        [
            sin_t * cos_p,
            sin_t * sin_p,
            cos_t,
            cos_t * cos_p,
            cos_t * sin_p,
            -sin_t,
            -sin_t * sin_p,
            sin_t * cos_p,
            -horiz,
            -vertical,
            horiz - vertical,
        ]
        + [zero] * 5
    )


def local(fields, horiz, vertical, tilt_angle, azimuth, electrode_quads):
    shards = lax.axis_size("cell")
    cell_dev = horiz.shape[0]
    total = electrode_quads.shape[0]
    small = fields.size * fields.dtype.itemsize <= 16 * MIB
    widths = (cell_dev - LANES, LANES) if small else (LANES,) * (cell_dev // LANES)
    fields = fields.transpose(1, 0, 2)
    rows = (electrode_quads.T * PAD).reshape(-1)
    coef = coefficients(horiz, vertical, tilt_angle, azimuth)

    sens, squares = [], []
    first, received = 0, None
    for width in widths:
        ready = send_order(fields, shards, first, width)
        if received is not None:
            ready, received = lax.optimization_barrier((ready, received))
        arriving = lax.all_to_all(ready, "cell", split_axis=0, concat_axis=0, tiled=True)
        if received is not None:
            done = sens_chunk(rows, received, coef[:, first - received.shape[-1] : first], GROUP_ROWS, FILL_STEPS)
            sens.append(done[0])
            squares.append(done[1])
        received = arriving
        first += width
    done = sens_chunk(rows, received, coef[:, first - received.shape[-1] : first], GROUP_ROWS, FILL_STEPS)
    sens.append(done[0])
    squares.append(done[1])
    partial_sq = sum(jnp.sum(s, axis=0) for s in squares)
    total_sq = sum_over_cells(partial_sq, shards)
    return scaled(total_sq, 1.0 / (4.0 * cell_dev * shards), sens, GROUP_ROWS)


def solution(mesh):
    placed = (
        P(("grp", "cell"), None, None),
        P(("grp", "cell")),
        P(("grp", "cell")),
        P(("grp", "cell")),
        P(("grp", "cell")),
        P("grp", None),
    )
    return jax.shard_map(
        local,
        mesh=mesh,
        in_specs=placed,
        out_specs=(P("grp", None, "cell"), P(("grp", "cell"))),
        check_vma=False,
    )
```

```python
import functools

import jax
import jax.numpy as jnp
from jax import lax
from jax.experimental import pallas as pl
from jax.experimental.pallas import tpu as pltpu
from jax.sharding import PartitionSpec as P

LANES = 128
SUBLANES = 8
UNROLL = 16
FILL_STEPS = 4
GROUP_ROWS = 512
SCALE_ROWS = 256
PAD = 4
MIB = 1 << 20
VMEM_LIMIT = 60 * MIB
SENS_LIMIT = 32 * MIB
SCALE_LIMIT = 48 * MIB
NEAR_BYTES = 4 * MIB


def send_order_kernel(first, fields_ref, out_ref, held, in_sems, out_sems):
    shards, _, _, width = held.shape
    cell_dev = fields_ref.shape[2] // shards
    arrive = [
        pltpu.make_async_copy(fields_ref.at[:, :, pl.ds(d * cell_dev + first, width)], held.at[d], in_sems.at[d])
        for d in range(shards)
    ]
    leave = [pltpu.make_async_copy(held.at[d], out_ref.at[d], out_sems.at[d]) for d in range(shards)]
    for copy in arrive:
        copy.start()
    for d in range(shards):
        arrive[d].wait()
        leave[d].start()
    for copy in leave:
        copy.wait()


def send_order(fields, shards, first, width):
    comps, owned, cells = fields.shape
    shape = (shards, comps, owned, width)
    return pl.pallas_call(
        functools.partial(send_order_kernel, first),
        in_specs=[pl.BlockSpec(memory_space=pl.ANY)],
        out_specs=pl.BlockSpec(memory_space=pl.ANY),
        out_shape=jax.ShapeDtypeStruct(shape, fields.dtype),
        scratch_shapes=[
            pltpu.VMEM(shape, fields.dtype),
            pltpu.SemaphoreType.DMA((shards,)),
            pltpu.SemaphoreType.DMA((shards,)),
        ],
        cost_estimate=pl.CostEstimate(flops=0, bytes_accessed=4 * comps * owned * width * shards, transcendentals=0),
        compiler_params=pltpu.CompilerParams(vmem_limit_bytes=VMEM_LIMIT),
        name="send_order",
    )(fields)


def sens_kernel(fill_steps, group_rows, near, rows_ref, fields_ref, coef_ref, before_ref, *refs):
    sens_ref, sumsq_ref, table, picked, squares = refs[-5:]
    step = pl.program_id(0)
    owned = fields_ref.shape[2]
    sources = table.shape[0] // (PAD * owned * fill_steps)
    batch_rows = SUBLANES * UNROLL
    total_rows = rows_ref.shape[0] // 4

    @pl.when(step < fill_steps)
    def _():
        for source in range(sources):
            place = step * sources + source
            for comp in range(fields_ref.shape[1]):
                values = fields_ref[place if near else source, comp].astype(jnp.float32)
                table[pl.ds(place * (owned * PAD) + comp, owned, stride=PAD), :] = values

    @pl.when(step >= fill_steps)
    def _():
        first = (step - fill_steps) * group_rows
        coef = [coef_ref[pl.ds(k, 1), :] for k in range(11)]
        ax, ay, az, tx, ty, tz, ux, uy, nh, nv, nc = coef

        def fetch(index):
            return table[pl.ds(pl.multiple_of(rows_ref[index], PAD), PAD), :]

        def close(batch):
            turned = squares[pl.ds(pl.multiple_of(batch * batch_rows, batch_rows), batch_rows), :].T
            total = jnp.sum(turned, axis=0, keepdims=True)
            sumsq_ref[0, pl.ds(batch, 1), :] = total + before_ref[0, pl.ds(batch, 1), :]

        squares[pl.ds(0, batch_rows), :] = jnp.zeros((batch_rows, LANES), jnp.float32)

        @pl.loop(0, group_rows // batch_rows)
        def _(batch):
            close(jnp.maximum(batch - 1, 0))
            base = first + batch * batch_rows
            for j in range(batch_rows):
                i = base + j
                picked[pl.ds(j * PAD, PAD), :] = fetch(i) - fetch(total_rows + i)
                picked[pl.ds((batch_rows + j) * PAD, PAD), :] = fetch(2 * total_rows + i) - fetch(3 * total_rows + i)
            for g in range(UNROLL):
                start = g * SUBLANES
                sx, sy, sz = (picked[pl.ds(start * PAD + k, SUBLANES, stride=PAD), :] for k in range(3))
                rx, ry, rz = (picked[pl.ds((batch_rows + start) * PAD + k, SUBLANES, stride=PAD), :] for k in range(3))
                sn = sx * ax + sy * ay + sz * az
                rn = rx * ax + ry * ay + rz * az
                st = sx * tx + sy * ty + sz * tz
                rt = rx * tx + ry * ty + rz * tz
                sp = sx * ux + sy * uy
                rp = rx * ux + ry * uy
                dot = sx * rx + sy * ry + sz * rz
                both = sn * rn
                values = (nh * (dot - both), nv * both, nc * (st * rn + sn * rt), nc * (sp * rn + sn * rp))
                place = ((base if near else batch * batch_rows) + start) * 4
                for k in range(4):
                    sens_ref[pl.ds(place + k, SUBLANES, stride=4), :] = values[k]
                squares[pl.ds(batch * batch_rows + start, SUBLANES), :] = (
                    values[0] * values[0] + values[1] * values[1] + values[2] * values[2] + values[3] * values[3]
                )

        close(group_rows // batch_rows - 1)


def sens_block(rows, fields, lane_block, coef, before, near, fill_steps, group_rows):
    shards, comps, owned, _ = fields.shape
    total = rows.size // 4
    groups = total // group_rows
    if near:
        fields_spec = sens_spec = pl.BlockSpec(memory_space=pltpu.VMEM)
        sens_shape = pltpu.VMEM((total * 4, LANES), jnp.float32)
    else:
        sens_spec = pl.BlockSpec((group_rows * 4, LANES), lambda i: (jnp.maximum(i - fill_steps, 0), 0))
        sens_shape = pltpu.HBM((total * 4, LANES), jnp.float32)
        fields_spec = pl.BlockSpec(
            (shards // fill_steps, comps, owned, LANES), lambda i: (jnp.minimum(i, fill_steps - 1), 0, 0, lane_block)
        )
    sums = pl.BlockSpec((1, group_rows // LANES, LANES), lambda i: (jnp.maximum(i - fill_steps, 0), 0, 0))
    return pl.pallas_call(
        functools.partial(sens_kernel, fill_steps, group_rows, near),
        grid=(fill_steps + groups,),
        in_specs=[
            pl.BlockSpec(memory_space=pltpu.SMEM),
            fields_spec,
            pl.BlockSpec((16, LANES), lambda i: (0, 0)),
            sums,
        ],
        out_specs=[sens_spec, sums],
        out_shape=[
            sens_shape,
            jax.ShapeDtypeStruct((groups, group_rows // LANES, LANES), jnp.float32),
        ],
        scratch_shapes=[
            pltpu.VMEM((shards * owned * PAD, LANES), jnp.float32),
            pltpu.VMEM((2 * UNROLL * SUBLANES * PAD, LANES), jnp.float32),
            pltpu.VMEM((group_rows, LANES), jnp.float32),
        ],
        cost_estimate=pl.CostEstimate(
            flops=total * LANES * 64,
            bytes_accessed=(shards * comps * owned * LANES * 2 + total * 5 * LANES * 4) * 4,
            transcendentals=0,
        ),
        compiler_params=pltpu.CompilerParams(vmem_limit_bytes=SENS_LIMIT),
        name="sens_block",
    )(rows, fields, coef, before)


def scale_kernel(inverse, far, mine_ref, theirs_ref, *refs):
    sens_refs, (out_ref, cover_ref, held, ready, spread, cover, in_sems, out_sems) = refs[:-8], refs[-8:]
    far_refs, near_refs = sens_refs[:far], sens_refs[far:]
    rows = spread.shape[0]
    step_rows = rows // 4
    steps = ready.shape[0] // step_rows

    def arrive(step, b):
        part = pl.ds(pl.multiple_of(step * rows, rows), rows)
        return pltpu.make_async_copy(far_refs[b].at[part], held.at[b, part], in_sems.at[step, b])

    def leave(step):
        part = pl.ds(pl.multiple_of(step * step_rows, step_rows), step_rows)
        return pltpu.make_async_copy(ready.at[part], out_ref.at[part], out_sems.at[step])

    for step in range(steps):
        for b in range(far):
            arrive(step, b).start()
    cover[...] = jnp.zeros_like(cover)

    @pl.loop(0, steps)
    def _(step):
        for k in range(step_rows // LANES):
            line = pl.ds(step * (step_rows // LANES) + k, 1)
            meansq = (mine_ref[line, :] + theirs_ref[line, :]) * inverse
            column = jnp.broadcast_to(lax.rsqrt(meansq + 1e-06), (LANES, LANES)).T
            for p in range(4):
                spread[pl.ds(k * 4 * LANES + p, LANES, stride=4), :] = column
        part = pl.ds(pl.multiple_of(step * rows, rows), rows)

        def write(b, values):
            normed = values * spread[...]
            place = pl.ds(pl.multiple_of(step * step_rows, step_rows), step_rows)
            lanes = slice(b * LANES, (b + 1) * LANES)
            ready[place, :, lanes] = normed.astype(ready.dtype).reshape(step_rows, 4, LANES)
            squares = (normed * normed).reshape(rows // SUBLANES, SUBLANES, LANES)
            cover[pl.ds(b * SUBLANES, SUBLANES), :] += jnp.sum(squares, axis=0)

        for b, ref in enumerate(near_refs):
            write(far + b, ref[part, :])
        for b in range(far):
            arrive(step, b).wait()
            write(b, held[b, part, :])
        leave(step).start()

    for b in range(len(sens_refs)):
        cover_ref[pl.ds(b, 1), :] = jnp.sum(cover[pl.ds(b * SUBLANES, SUBLANES), :], axis=0, keepdims=True)
    for step in range(steps):
        leave(step).wait()


def scaled(mine, theirs, inverse, far, near, step_rows):
    columns, total = len(far) + len(near), (far + near)[0].shape[0] // 4
    steps = total // step_rows
    near = [pltpu.with_memory_space_constraint(s, pltpu.VMEM) for s in near]
    whole = pl.BlockSpec(memory_space=pltpu.VMEM)
    out, cover = pl.pallas_call(
        functools.partial(scale_kernel, inverse, len(far)),
        in_specs=[whole, whole] + [pl.BlockSpec(memory_space=pltpu.HBM)] * len(far) + [whole] * len(near),
        out_specs=[pl.BlockSpec(memory_space=pltpu.HBM), whole],
        out_shape=[
            jax.ShapeDtypeStruct((total, 4, columns * LANES), jnp.bfloat16),
            jax.ShapeDtypeStruct((columns, LANES), jnp.float32),
        ],
        scratch_shapes=[
            pltpu.VMEM((len(far), total * 4, LANES), jnp.float32),
            pltpu.VMEM((total, 4, columns * LANES), jnp.bfloat16),
            pltpu.VMEM((step_rows * 4, LANES), jnp.float32),
            pltpu.VMEM((columns * SUBLANES, LANES), jnp.float32),
            pltpu.SemaphoreType.DMA((steps, len(far))),
            pltpu.SemaphoreType.DMA((steps,)),
        ],
        compiler_params=pltpu.CompilerParams(vmem_limit_bytes=SCALE_LIMIT),
        name="scaled",
    )(mine.reshape(-1, LANES), theirs.reshape(-1, LANES), *far, *near)
    return out, cover.reshape(columns * LANES)


def sum_over_cells(x, shards):
    if shards & (shards - 1):
        return lax.psum(x, "cell"), jnp.zeros_like(x)
    other, bit = jnp.zeros_like(x), 1
    while bit < shards:
        x = x + other
        other = lax.ppermute(x, "cell", [(i, i ^ bit) for i in range(shards)])
        bit *= 2
    return x, other


def coefficients(horiz, vertical, tilt_angle, azimuth):
    sin_t, cos_t = jnp.sin(tilt_angle), jnp.cos(tilt_angle)
    sin_p, cos_p = jnp.sin(azimuth), jnp.cos(azimuth)
    zero = jnp.zeros_like(horiz)
    return jnp.stack(
        [
            sin_t * cos_p,
            sin_t * sin_p,
            cos_t,
            cos_t * cos_p,
            cos_t * sin_p,
            -sin_t,
            -sin_t * sin_p,
            sin_t * cos_p,
            -horiz,
            -vertical,
            horiz - vertical,
        ]
        + [zero] * 5
    )


def local(fields, horiz, vertical, tilt_angle, azimuth, electrode_quads):
    shards = lax.axis_size("cell")
    cell_dev = horiz.shape[0]
    small = fields.size * fields.dtype.itemsize <= 16 * MIB
    widths = (cell_dev - LANES, LANES) if small else (LANES,) * (cell_dev // LANES)
    fields = fields.transpose(1, 0, 2)
    rows = (electrode_quads.T * PAD).reshape(-1)
    coef = coefficients(horiz, vertical, tilt_angle, azimuth)

    total = electrode_quads.shape[0]
    far, near, before = [], [], jnp.zeros((total // GROUP_ROWS, GROUP_ROWS // LANES, LANES), jnp.float32)

    def finish(received, first, before, last):
        width = received.shape[-1]
        here = last and width == LANES and total * 4 * LANES * 4 <= NEAR_BYTES
        for k in range(width // LANES):
            own = coef[:, first + k * LANES : first + (k + 1) * LANES]
            values, before = sens_block(rows, received, k, own, before, here, FILL_STEPS, GROUP_ROWS)
            (near if here else far).append(values)
        return before

    first, received = 0, None
    for width in widths:
        ready = send_order(fields, shards, first, width)
        if received is not None:
            ready, received = lax.optimization_barrier((ready, received))
        arriving = lax.all_to_all(ready, "cell", split_axis=0, concat_axis=0, tiled=True)
        if received is not None:
            before = finish(received, first - received.shape[-1], before, False)
        received = arriving
        first += width
    before = finish(received, first - received.shape[-1], before, True)
    mine, theirs = sum_over_cells(before, shards)
    return scaled(mine, theirs, 1.0 / (4.0 * cell_dev * shards), far, near, SCALE_ROWS)


def solution(mesh):
    placed = (
        P(("grp", "cell"), None, None),
        P(("grp", "cell")),
        P(("grp", "cell")),
        P(("grp", "cell")),
        P(("grp", "cell")),
        P("grp", None),
    )
    return jax.shard_map(
        local,
        mesh=mesh,
        in_specs=placed,
        out_specs=(P("grp", None, "cell"), P(("grp", "cell"))),
        check_vma=False,
    )
```

```python
import functools

import jax
import jax.numpy as jnp
from jax import lax
from jax.experimental import pallas as pl
from jax.experimental.pallas import tpu as pltpu
from jax.sharding import PartitionSpec as P

LANES = 128
SUBLANES = 8
UNROLL = 16
FILL_STEPS = 4
GROUP_ROWS = 512
SCALE_ROWS = 256
ROW_TILE = 16
PAD = 4
MIB = 1 << 20
VMEM_LIMIT = 60 * MIB
SENS_LIMIT = 32 * MIB
SCALE_LIMIT = 48 * MIB
NEAR_BYTES = 4 * MIB


def one_hots(quads_ref, column, high):
    index = quads_ref[pl.ds(column, 1), :]
    total = index.shape[1]
    upper = lax.broadcasted_iota(jnp.int32, (high, total), 0) == index // LANES
    lower = lax.broadcasted_iota(jnp.int32, (LANES, total), 0) == index % LANES
    return upper.astype(jnp.bfloat16), lower.astype(jnp.bfloat16)


def rank_kernel(per, quads_ref, rank_ref, most_ref):
    high = rank_ref.shape[0]
    count = jnp.zeros((high, LANES), jnp.float32)
    for column in range(4):
        upper, lower = one_hots(quads_ref, column, high)
        count += lax.dot_general(upper, lower, (((1,), (1,)), ((), ())), preferred_element_type=jnp.float32)
    named = (count > 0).astype(jnp.bfloat16)
    i, j = (lax.broadcasted_iota(jnp.int32, (LANES, LANES), d) for d in range(2))
    within = jnp.dot(named, (i < j).astype(jnp.bfloat16), preferred_element_type=jnp.float32)
    lines = jnp.dot(named, jnp.ones((LANES, LANES), jnp.bfloat16), preferred_element_type=jnp.float32)
    i, j = (lax.broadcasted_iota(jnp.int32, (high, high), d) for d in range(2))
    ahead = ((j < i) & (j // per == i // per)).astype(jnp.bfloat16)
    before = jnp.dot(ahead, lines.astype(jnp.bfloat16), preferred_element_type=jnp.float32)
    rank = jnp.where(count > 0, within + before, -1.0)
    rank_ref[...] = rank
    most_ref[...] = jnp.broadcast_to(jnp.max(rank, axis=(0, 1), keepdims=True) + 1.0, most_ref.shape)


def named_ranks(quads, electrodes, owned):
    whole = pl.BlockSpec(memory_space=pltpu.VMEM)
    rank, most = pl.pallas_call(
        functools.partial(rank_kernel, owned // LANES),
        in_specs=[whole],
        out_specs=[whole, whole],
        out_shape=[
            jax.ShapeDtypeStruct((electrodes // LANES, LANES), jnp.float32),
            jax.ShapeDtypeStruct((SUBLANES, LANES), jnp.float32),
        ],
        name="named_ranks",
    )(quads)
    return rank, most[0, 0]


def table_rows_kernel(owned, kept, quads_ref, rank_ref, rows_ref):
    rank = rank_ref[...].astype(jnp.bfloat16)
    for column in range(4):
        upper, lower = one_hots(quads_ref, column, rank.shape[0])
        ranks = lax.dot_general(rank, upper, (((0,), (0,)), ((), ())), preferred_element_type=jnp.float32)
        own = jnp.sum(ranks * lower.astype(jnp.float32), axis=0, keepdims=True).astype(jnp.int32)
        rows_ref[pl.ds(column, 1), :] = (quads_ref[pl.ds(column, 1), :] // owned * kept + own) * PAD


def table_rows(quads, rank, owned, kept):
    whole = pl.BlockSpec(memory_space=pltpu.VMEM)
    return pl.pallas_call(
        functools.partial(table_rows_kernel, owned, kept),
        in_specs=[whole, whole],
        out_specs=whole,
        out_shape=jax.ShapeDtypeStruct(quads.shape, jnp.int32),
        name="table_rows",
    )(quads, rank)


def send_order_kernel(first, fields_ref, out_ref, held, in_sems, out_sems):
    shards, _, _, width = held.shape
    cell_dev = fields_ref.shape[2] // shards
    arrive = [
        pltpu.make_async_copy(fields_ref.at[:, :, pl.ds(d * cell_dev + first, width)], held.at[d], in_sems.at[d])
        for d in range(shards)
    ]
    leave = [pltpu.make_async_copy(held.at[d], out_ref.at[d], out_sems.at[d]) for d in range(shards)]
    for copy in arrive:
        copy.start()
    for d in range(shards):
        arrive[d].wait()
        leave[d].start()
    for copy in leave:
        copy.wait()


def send_named_kernel(first, fields_ref, rank_ref, out_ref, held, packed, choose, in_sems, out_sems):
    shards, comps, owned, width = held.shape
    kept = packed.shape[2]
    cell_dev = fields_ref.shape[2] // shards

    def arrive(d):
        lanes = pl.ds(pl.multiple_of(d * cell_dev + first, LANES), width)
        return pltpu.make_async_copy(fields_ref.at[:, :, lanes], held.at[d], in_sems.at[d])

    def leave(d):
        return pltpu.make_async_copy(packed.at[d], out_ref.at[d], out_sems.at[d])

    for d in range(shards):
        arrive(d).start()
    me = lax.axis_index("cell")
    place = lax.broadcasted_iota(jnp.int32, (kept, LANES), 0).astype(jnp.float32)
    for k in range(owned // LANES):
        line = rank_ref[pl.ds(me * (owned // LANES) + k, 1), :]
        choose[:, k * LANES : (k + 1) * LANES] = (place == line).astype(choose.dtype)

    @pl.loop(0, shards)
    def _(d):
        arrive(d).wait()
        for comp in range(comps):
            rows = jnp.dot(choose[...], held[d, comp], preferred_element_type=jnp.float32)
            packed[d, comp] = rows.astype(packed.dtype)
        leave(d).start()

    for d in range(shards):
        leave(d).wait()


def send_order(fields, rank, kept, shards, first, width):
    comps, owned, cells = fields.shape
    held = (shards, comps, owned, width)
    sent = (shards, comps, kept, width)
    scratch = [pltpu.VMEM(held, fields.dtype)]
    in_specs, args = [pl.BlockSpec(memory_space=pl.ANY)], [fields]
    if rank is not None:
        scratch += [pltpu.VMEM(sent, fields.dtype), pltpu.VMEM((kept, owned), fields.dtype)]
        in_specs.append(pl.BlockSpec(memory_space=pltpu.VMEM))
        args.append(rank)
    return pl.pallas_call(
        functools.partial(send_order_kernel if rank is None else send_named_kernel, first),
        in_specs=in_specs,
        out_specs=pl.BlockSpec(memory_space=pl.ANY),
        out_shape=jax.ShapeDtypeStruct(sent, fields.dtype),
        scratch_shapes=scratch + [pltpu.SemaphoreType.DMA((shards,)), pltpu.SemaphoreType.DMA((shards,))],
        cost_estimate=pl.CostEstimate(flops=0, bytes_accessed=4 * comps * owned * width * shards, transcendentals=0),
        compiler_params=pltpu.CompilerParams(vmem_limit_bytes=VMEM_LIMIT),
        name="send_order",
    )(*args)


def sens_kernel(fill_steps, group_rows, near, rows_ref, fields_ref, coef_ref, before_ref, *refs):
    sens_ref, sumsq_ref, table, picked, squares = refs[-5:]
    step = pl.program_id(0)
    owned = fields_ref.shape[2]
    sources = table.shape[0] // (PAD * owned * fill_steps)
    batch_rows = SUBLANES * UNROLL
    total_rows = rows_ref.shape[0] // 4

    @pl.when(step < fill_steps)
    def _():
        for source in range(sources):
            place = step * sources + source
            for comp in range(fields_ref.shape[1]):
                values = fields_ref[place if near else source, comp].astype(jnp.float32)
                table[pl.ds(place * (owned * PAD) + comp, owned, stride=PAD), :] = values

    @pl.when(step >= fill_steps)
    def _():
        first = (step - fill_steps) * group_rows
        coef = [coef_ref[pl.ds(k, 1), :] for k in range(11)]
        ax, ay, az, tx, ty, tz, ux, uy, nh, nv, nc = coef

        def fetch(index):
            return table[pl.ds(pl.multiple_of(rows_ref[index], PAD), PAD), :]

        def close(batch):
            turned = squares[pl.ds(pl.multiple_of(batch * batch_rows, batch_rows), batch_rows), :].T
            total = jnp.sum(turned, axis=0, keepdims=True)
            sumsq_ref[0, pl.ds(batch, 1), :] = total + before_ref[0, pl.ds(batch, 1), :]

        squares[pl.ds(0, batch_rows), :] = jnp.zeros((batch_rows, LANES), jnp.float32)

        @pl.loop(0, group_rows // batch_rows)
        def _(batch):
            close(jnp.maximum(batch - 1, 0))
            base = first + batch * batch_rows
            for j in range(batch_rows):
                i = base + j
                picked[pl.ds(j * PAD, PAD), :] = fetch(i) - fetch(total_rows + i)
                picked[pl.ds((batch_rows + j) * PAD, PAD), :] = fetch(2 * total_rows + i) - fetch(3 * total_rows + i)
            for g in range(UNROLL):
                start = g * SUBLANES
                sx, sy, sz = (picked[pl.ds(start * PAD + k, SUBLANES, stride=PAD), :] for k in range(3))
                rx, ry, rz = (picked[pl.ds((batch_rows + start) * PAD + k, SUBLANES, stride=PAD), :] for k in range(3))
                sn = sx * ax + sy * ay + sz * az
                rn = rx * ax + ry * ay + rz * az
                st = sx * tx + sy * ty + sz * tz
                rt = rx * tx + ry * ty + rz * tz
                sp = sx * ux + sy * uy
                rp = rx * ux + ry * uy
                dot = sx * rx + sy * ry + sz * rz
                both = sn * rn
                values = (nh * (dot - both), nv * both, nc * (st * rn + sn * rt), nc * (sp * rn + sn * rp))
                place = ((base if near else batch * batch_rows) + start) * 4
                for k in range(4):
                    sens_ref[pl.ds(place + k, SUBLANES, stride=4), :] = values[k]
                squares[pl.ds(batch * batch_rows + start, SUBLANES), :] = (
                    values[0] * values[0] + values[1] * values[1] + values[2] * values[2] + values[3] * values[3]
                )

        close(group_rows // batch_rows - 1)


def sens_block(rows, fields, lane_block, coef, before, near, fill_steps, group_rows):
    shards, comps, owned, _ = fields.shape
    total = rows.size // 4
    groups = total // group_rows
    if near:
        fields_spec = sens_spec = pl.BlockSpec(memory_space=pltpu.VMEM)
        sens_shape = pltpu.VMEM((total * 4, LANES), jnp.float32)
    else:
        sens_spec = pl.BlockSpec((group_rows * 4, LANES), lambda i: (jnp.maximum(i - fill_steps, 0), 0))
        sens_shape = pltpu.HBM((total * 4, LANES), jnp.float32)
        fields_spec = pl.BlockSpec(
            (shards // fill_steps, comps, owned, LANES), lambda i: (jnp.minimum(i, fill_steps - 1), 0, 0, lane_block)
        )
    sums = pl.BlockSpec((1, group_rows // LANES, LANES), lambda i: (jnp.maximum(i - fill_steps, 0), 0, 0))
    return pl.pallas_call(
        functools.partial(sens_kernel, fill_steps, group_rows, near),
        grid=(fill_steps + groups,),
        in_specs=[
            pl.BlockSpec(memory_space=pltpu.SMEM),
            fields_spec,
            pl.BlockSpec((16, LANES), lambda i: (0, 0)),
            sums,
        ],
        out_specs=[sens_spec, sums],
        out_shape=[
            sens_shape,
            jax.ShapeDtypeStruct((groups, group_rows // LANES, LANES), jnp.float32),
        ],
        scratch_shapes=[
            pltpu.VMEM((shards * owned * PAD, LANES), jnp.float32),
            pltpu.VMEM((2 * UNROLL * SUBLANES * PAD, LANES), jnp.float32),
            pltpu.VMEM((group_rows, LANES), jnp.float32),
        ],
        cost_estimate=pl.CostEstimate(
            flops=total * LANES * 64,
            bytes_accessed=(shards * comps * owned * LANES * 2 + total * 5 * LANES * 4) * 4,
            transcendentals=0,
        ),
        compiler_params=pltpu.CompilerParams(vmem_limit_bytes=SENS_LIMIT),
        name="sens_block",
    )(rows, fields, coef, before)


def scale_kernel(inverse, far, mine_ref, theirs_ref, *refs):
    sens_refs, (out_ref, cover_ref, held, ready, spread, cover, in_sems, out_sems) = refs[:-8], refs[-8:]
    far_refs, near_refs = sens_refs[:far], sens_refs[far:]
    rows = spread.shape[0]
    step_rows = rows // 4
    steps = ready.shape[0] // step_rows

    def arrive(step, b):
        part = pl.ds(pl.multiple_of(step * rows, rows), rows)
        return pltpu.make_async_copy(far_refs[b].at[part], held.at[b, part], in_sems.at[step, b])

    def leave(step):
        part = pl.ds(pl.multiple_of(step * step_rows, step_rows), step_rows)
        return pltpu.make_async_copy(ready.at[part], out_ref.at[part], out_sems.at[step])

    for step in range(steps):
        for b in range(far):
            arrive(step, b).start()
    cover[...] = jnp.zeros_like(cover)

    @pl.loop(0, steps)
    def _(step):
        for k in range(step_rows // LANES):
            line = pl.ds(step * (step_rows // LANES) + k, 1)
            meansq = (mine_ref[line, :] + theirs_ref[line, :]) * inverse
            column = jnp.broadcast_to(lax.rsqrt(meansq + 1e-06), (LANES, LANES)).T
            for p in range(4):
                spread[pl.ds(k * 4 * LANES + p, LANES, stride=4), :] = column
        part = pl.ds(pl.multiple_of(step * rows, rows), rows)

        def write(b, values):
            normed = values * spread[...]
            place = pl.ds(pl.multiple_of(step * step_rows, step_rows), step_rows)
            lanes = slice(b * LANES, (b + 1) * LANES)
            ready[place, :, lanes] = normed.astype(ready.dtype).reshape(step_rows, 4, LANES)
            squares = (normed * normed).reshape(rows // SUBLANES, SUBLANES, LANES)
            cover[pl.ds(b * SUBLANES, SUBLANES), :] += jnp.sum(squares, axis=0)

        for b, ref in enumerate(near_refs):
            write(far + b, ref[part, :])
        for b in range(far):
            arrive(step, b).wait()
            write(b, held[b, part, :])
        leave(step).start()

    for b in range(len(sens_refs)):
        cover_ref[pl.ds(b, 1), :] = jnp.sum(cover[pl.ds(b * SUBLANES, SUBLANES), :], axis=0, keepdims=True)
    for step in range(steps):
        leave(step).wait()


def scaled(mine, theirs, inverse, far, near, step_rows):
    columns, total = len(far) + len(near), (far + near)[0].shape[0] // 4
    steps = total // step_rows
    near = [pltpu.with_memory_space_constraint(s, pltpu.VMEM) for s in near]
    whole = pl.BlockSpec(memory_space=pltpu.VMEM)
    out, cover = pl.pallas_call(
        functools.partial(scale_kernel, inverse, len(far)),
        in_specs=[whole, whole] + [pl.BlockSpec(memory_space=pltpu.HBM)] * len(far) + [whole] * len(near),
        out_specs=[pl.BlockSpec(memory_space=pltpu.HBM), whole],
        out_shape=[
            jax.ShapeDtypeStruct((total, 4, columns * LANES), jnp.bfloat16),
            jax.ShapeDtypeStruct((columns, LANES), jnp.float32),
        ],
        scratch_shapes=[
            pltpu.VMEM((len(far), total * 4, LANES), jnp.float32),
            pltpu.VMEM((total, 4, columns * LANES), jnp.bfloat16),
            pltpu.VMEM((step_rows * 4, LANES), jnp.float32),
            pltpu.VMEM((columns * SUBLANES, LANES), jnp.float32),
            pltpu.SemaphoreType.DMA((steps, len(far))),
            pltpu.SemaphoreType.DMA((steps,)),
        ],
        compiler_params=pltpu.CompilerParams(vmem_limit_bytes=SCALE_LIMIT),
        name="scaled",
    )(mine.reshape(-1, LANES), theirs.reshape(-1, LANES), *far, *near)
    return out, cover.reshape(columns * LANES)


def sum_over_cells(x, shards):
    if shards & (shards - 1):
        return lax.psum(x, "cell"), jnp.zeros_like(x)
    other, bit = jnp.zeros_like(x), 1
    while bit < shards:
        x = x + other
        other = lax.ppermute(x, "cell", [(i, i ^ bit) for i in range(shards)])
        bit *= 2
    return x, other


def coefficients(horiz, vertical, tilt_angle, azimuth):
    sin_t, cos_t = jnp.sin(tilt_angle), jnp.cos(tilt_angle)
    sin_p, cos_p = jnp.sin(azimuth), jnp.cos(azimuth)
    zero = jnp.zeros_like(horiz)
    return jnp.stack(
        [
            sin_t * cos_p,
            sin_t * sin_p,
            cos_t,
            cos_t * cos_p,
            cos_t * sin_p,
            -sin_t,
            -sin_t * sin_p,
            sin_t * cos_p,
            -horiz,
            -vertical,
            horiz - vertical,
        ]
        + [zero] * 5
    )


def transfer_and_solve(fields, quads, rank, coef, kept, shards):
    comps, owned, cells = fields.shape
    cell_dev = cells // shards
    total = quads.shape[1]
    small = fields.size * fields.dtype.itemsize <= 16 * MIB
    widths = (cell_dev - LANES, LANES) if small else (LANES,) * (cell_dev // LANES)
    if rank is None:
        rows = quads * PAD
    else:
        rows = table_rows(quads, rank, owned, kept)
    rows = rows.reshape(-1)
    far, near, before = [], [], jnp.zeros((total // GROUP_ROWS, GROUP_ROWS // LANES, LANES), jnp.float32)

    def finish(received, first, before, last):
        width = received.shape[-1]
        here = last and width == LANES and total * 4 * LANES * 4 <= NEAR_BYTES
        for k in range(width // LANES):
            own = coef[:, first + k * LANES : first + (k + 1) * LANES]
            values, before = sens_block(rows, received, k, own, before, here, FILL_STEPS, GROUP_ROWS)
            (near if here else far).append(values)
        return before

    first, received = 0, None
    for width in widths:
        ready = send_order(fields, rank, kept, shards, first, width)
        if received is not None:
            ready, received = lax.optimization_barrier((ready, received))
        arriving = lax.all_to_all(ready, "cell", split_axis=0, concat_axis=0, tiled=True)
        if received is not None:
            before = finish(received, first - received.shape[-1], before, False)
        received = arriving
        first += width
    before = finish(received, first - received.shape[-1], before, True)
    mine, theirs = sum_over_cells(before, shards)
    return scaled(mine, theirs, 1.0 / (4.0 * cell_dev * shards), far, near, SCALE_ROWS)


def local(fields, horiz, vertical, tilt_angle, azimuth, electrode_quads):
    shards = lax.axis_size("cell")
    owned = fields.shape[0]
    fields = fields.transpose(1, 0, 2)
    quads = electrode_quads.T
    coef = coefficients(horiz, vertical, tilt_angle, azimuth)
    kept = owned * 15 // 16 // ROW_TILE * ROW_TILE
    if owned % LANES or owned > 2 * LANES or kept == 0:
        return transfer_and_solve(fields, quads, None, coef, owned, shards)
    rank, most = named_ranks(quads, shards * owned, owned)
    return lax.cond(
        most <= kept,
        lambda f, q, r, c: transfer_and_solve(f, q, r, c, kept, shards),
        lambda f, q, r, c: transfer_and_solve(f, q, None, c, owned, shards),
        fields,
        quads,
        rank,
        coef,
    )


def solution(mesh):
    placed = (
        P(("grp", "cell"), None, None),
        P(("grp", "cell")),
        P(("grp", "cell")),
        P(("grp", "cell")),
        P(("grp", "cell")),
        P("grp", None),
    )
    return jax.shard_map(
        local,
        mesh=mesh,
        in_specs=placed,
        out_specs=(P("grp", None, "cell"), P(("grp", "cell"))),
        check_vma=False,
    )
```

```python
import functools

import jax
import jax.numpy as jnp
from jax import lax
from jax.experimental import pallas as pl
from jax.experimental.pallas import tpu as pltpu
from jax.sharding import PartitionSpec as P

LANES = 128
SUBLANES = 8
UNROLL = 16
FILL_STEPS = 4
GROUP_ROWS = 512
SCALE_ROWS = 256
ROW_TILE = 8
KEEPS = (29, 30)
PAD = 4
MIB = 1 << 20
VMEM_LIMIT = 60 * MIB
SENS_LIMIT = 32 * MIB
SCALE_LIMIT = 48 * MIB
NEAR_BYTES = 4 * MIB


def one_hots(quads_ref, column, high):
    index = quads_ref[pl.ds(column, 1), :]
    total = index.shape[1]
    upper = lax.broadcasted_iota(jnp.int32, (high, total), 0) == index // LANES
    lower = lax.broadcasted_iota(jnp.int32, (LANES, total), 0) == index % LANES
    return upper.astype(jnp.bfloat16), lower.astype(jnp.bfloat16)


def named_ranks(quads_ref, high, per):
    count = jnp.zeros((high, LANES), jnp.float32)
    for column in range(4):
        upper, lower = one_hots(quads_ref, column, high)
        count += lax.dot_general(upper, lower, (((1,), (1,)), ((), ())), preferred_element_type=jnp.float32)
    named = (count > 0).astype(jnp.bfloat16)
    i, j = (lax.broadcasted_iota(jnp.int32, (LANES, LANES), d) for d in range(2))
    within = jnp.dot(named, (i < j).astype(jnp.bfloat16), preferred_element_type=jnp.float32)
    lines = jnp.dot(named, jnp.ones((LANES, LANES), jnp.bfloat16), preferred_element_type=jnp.float32)
    i, j = (lax.broadcasted_iota(jnp.int32, (high, high), d) for d in range(2))
    ahead = ((j < i) & (j // per == i // per)).astype(jnp.bfloat16)
    before = jnp.dot(ahead, lines.astype(jnp.bfloat16), preferred_element_type=jnp.float32)
    return jnp.where(count > 0, within + before, -1.0)


def table_rows_kernel(owned, kept, quads_ref, rank_ref, rows_ref):
    rank = rank_ref[...].astype(jnp.bfloat16)
    for column in range(4):
        upper, lower = one_hots(quads_ref, column, rank.shape[0])
        ranks = lax.dot_general(rank, upper, (((0,), (0,)), ((), ())), preferred_element_type=jnp.float32)
        own = jnp.sum(ranks * lower.astype(jnp.float32), axis=0, keepdims=True).astype(jnp.int32)
        rows_ref[pl.ds(column, 1), :] = (quads_ref[pl.ds(column, 1), :] // owned * kept + own) * PAD


def table_rows(quads, rank, owned, kept):
    whole = pl.BlockSpec(memory_space=pltpu.VMEM)
    return pl.pallas_call(
        functools.partial(table_rows_kernel, owned, kept),
        in_specs=[whole, whole],
        out_specs=whole,
        out_shape=jax.ShapeDtypeStruct(quads.shape, jnp.int32),
        name="table_rows",
    )(quads, rank)


def send_order_kernel(first, fields_ref, out_ref, held, in_sems, out_sems):
    shards, _, _, width = held.shape
    cell_dev = fields_ref.shape[2] // shards
    arrive = [
        pltpu.make_async_copy(fields_ref.at[:, :, pl.ds(d * cell_dev + first, width)], held.at[d], in_sems.at[d])
        for d in range(shards)
    ]
    leave = [pltpu.make_async_copy(held.at[d], out_ref.at[d], out_sems.at[d]) for d in range(shards)]
    for copy in arrive:
        copy.start()
    for d in range(shards):
        arrive[d].wait()
        leave[d].start()
    for copy in leave:
        copy.wait()


def choose_rows(choose, rank_ref):
    kept, owned = choose.shape
    me = lax.axis_index("cell")
    place = lax.broadcasted_iota(jnp.int32, (kept, LANES), 0).astype(jnp.float32)
    for k in range(owned // LANES):
        line = rank_ref[pl.ds(me * (owned // LANES) + k, 1), :]
        choose[:, k * LANES : (k + 1) * LANES] = (place == line).astype(choose.dtype)


def send_chosen(arrive, choose, held, packed, out_ref, out_sems):
    shards, comps = held.shape[:2]
    kept = packed.shape[2]

    def leave(d):
        return pltpu.make_async_copy(packed.at[d], out_ref.at[d], out_sems.at[d])

    @pl.loop(0, shards)
    def _(d):
        arrive(d).wait()
        for comp in range(comps):
            rows = jnp.dot(choose[pl.ds(0, kept), :], held[d, comp], preferred_element_type=jnp.float32)
            packed[d, comp] = rows.astype(packed.dtype)
        leave(d).start()

    @pl.loop(0, shards)
    def _(d):
        leave(d).wait()


def arrival(first, fields_ref, held, in_sems):
    shards, _, _, width = held.shape
    cell_dev = fields_ref.shape[2] // shards

    def arrive(d):
        lanes = pl.ds(pl.multiple_of(d * cell_dev + first, LANES), width)
        return pltpu.make_async_copy(fields_ref.at[:, :, lanes], held.at[d], in_sems.at[d])

    return arrive


def send_named_kernel(first, fields_ref, rank_ref, out_ref, held, packed, choose, in_sems, out_sems):
    arrive = arrival(first, fields_ref, held, in_sems)
    for d in range(held.shape[0]):
        arrive(d).start()
    choose_rows(choose, rank_ref)
    send_chosen(arrive, choose, held, packed, out_ref, out_sems)


def send_first_kernel(keeps, fields_ref, quads_ref, *refs):
    out_refs, (rank_ref, chosen_ref, held) = refs[: len(keeps)], refs[len(keeps) : len(keeps) + 3]
    packed, (choose, in_sems, out_sems) = refs[len(keeps) + 3 : -3], refs[-3:]
    arrive = arrival(0, fields_ref, held, in_sems)
    for d in range(held.shape[0]):
        arrive(d).start()
    rank = named_ranks(quads_ref, rank_ref.shape[0], held.shape[2] // LANES)
    rank_ref[...] = rank
    most = (jnp.max(rank) + 1.0).astype(jnp.int32)
    chosen = sum((most > kept).astype(jnp.int32) for kept in keeps)
    chosen_ref[0] = chosen
    choose_rows(choose, rank_ref)
    for k, kept in enumerate(keeps):

        @pl.when(chosen == k)
        def _():
            send_chosen(arrive, choose, held, packed[k], out_refs[k], out_sems)

    @pl.when(chosen == len(keeps))
    def _():
        for d in range(held.shape[0]):
            arrive(d).wait()


def send_first(fields, quads, keeps, shards, width):
    comps, owned, cells = fields.shape
    sent = [(shards, comps, kept, width) for kept in keeps]
    anywhere, whole = pl.BlockSpec(memory_space=pl.ANY), pl.BlockSpec(memory_space=pltpu.VMEM)
    *ready, rank, chosen = pl.pallas_call(
        functools.partial(send_first_kernel, keeps),
        in_specs=[anywhere, whole],
        out_specs=[anywhere] * len(keeps) + [whole, pl.BlockSpec(memory_space=pltpu.SMEM)],
        out_shape=[jax.ShapeDtypeStruct(shape, fields.dtype) for shape in sent]
        + [
            jax.ShapeDtypeStruct((shards * owned // LANES, LANES), jnp.float32),
            jax.ShapeDtypeStruct((1,), jnp.int32),
        ],
        scratch_shapes=[pltpu.VMEM((shards, comps, owned, width), fields.dtype)]
        + [pltpu.VMEM(shape, fields.dtype) for shape in sent]
        + [
            pltpu.VMEM((max(keeps), owned), fields.dtype),
            pltpu.SemaphoreType.DMA((shards,)),
            pltpu.SemaphoreType.DMA((shards,)),
        ],
        compiler_params=pltpu.CompilerParams(vmem_limit_bytes=VMEM_LIMIT),
        name="send_first",
    )(fields, quads)
    return ready, rank, chosen[0]


def send_order(fields, rank, kept, shards, first, width):
    comps, owned, cells = fields.shape
    held = (shards, comps, owned, width)
    sent = (shards, comps, kept, width)
    scratch = [pltpu.VMEM(held, fields.dtype)]
    in_specs, args = [pl.BlockSpec(memory_space=pl.ANY)], [fields]
    if rank is not None:
        scratch += [pltpu.VMEM(sent, fields.dtype), pltpu.VMEM((kept, owned), fields.dtype)]
        in_specs.append(pl.BlockSpec(memory_space=pltpu.VMEM))
        args.append(rank)
    return pl.pallas_call(
        functools.partial(send_order_kernel if rank is None else send_named_kernel, first),
        in_specs=in_specs,
        out_specs=pl.BlockSpec(memory_space=pl.ANY),
        out_shape=jax.ShapeDtypeStruct(sent, fields.dtype),
        scratch_shapes=scratch + [pltpu.SemaphoreType.DMA((shards,)), pltpu.SemaphoreType.DMA((shards,))],
        cost_estimate=pl.CostEstimate(flops=0, bytes_accessed=4 * comps * owned * width * shards, transcendentals=0),
        compiler_params=pltpu.CompilerParams(vmem_limit_bytes=VMEM_LIMIT),
        name="send_order",
    )(*args)


def sens_kernel(fill_steps, group_rows, near, rows_ref, fields_ref, coef_ref, before_ref, *refs):
    sens_ref, sumsq_ref, table, picked, squares = refs[-5:]
    step = pl.program_id(0)
    owned = fields_ref.shape[2]
    sources = table.shape[0] // (PAD * owned * fill_steps)
    batch_rows = SUBLANES * UNROLL
    total_rows = rows_ref.shape[0] // 4

    @pl.when(step < fill_steps)
    def _():
        for source in range(sources):
            place = step * sources + source
            for comp in range(fields_ref.shape[1]):
                values = fields_ref[place if near else source, comp].astype(jnp.float32)
                table[pl.ds(place * (owned * PAD) + comp, owned, stride=PAD), :] = values

    @pl.when(step >= fill_steps)
    def _():
        first = (step - fill_steps) * group_rows
        coef = [coef_ref[pl.ds(k, 1), :] for k in range(11)]
        ax, ay, az, tx, ty, tz, ux, uy, nh, nv, nc = coef

        def fetch(index):
            return table[pl.ds(pl.multiple_of(rows_ref[index], PAD), PAD), :]

        def close(batch):
            turned = squares[pl.ds(pl.multiple_of(batch * batch_rows, batch_rows), batch_rows), :].T
            total = jnp.sum(turned, axis=0, keepdims=True)
            sumsq_ref[0, pl.ds(batch, 1), :] = total + before_ref[0, pl.ds(batch, 1), :]

        squares[pl.ds(0, batch_rows), :] = jnp.zeros((batch_rows, LANES), jnp.float32)

        @pl.loop(0, group_rows // batch_rows)
        def _(batch):
            close(jnp.maximum(batch - 1, 0))
            base = first + batch * batch_rows
            for j in range(batch_rows):
                i = base + j
                picked[pl.ds(j * PAD, PAD), :] = fetch(i) - fetch(total_rows + i)
                picked[pl.ds((batch_rows + j) * PAD, PAD), :] = fetch(2 * total_rows + i) - fetch(3 * total_rows + i)
            for g in range(UNROLL):
                start = g * SUBLANES
                sx, sy, sz = (picked[pl.ds(start * PAD + k, SUBLANES, stride=PAD), :] for k in range(3))
                rx, ry, rz = (picked[pl.ds((batch_rows + start) * PAD + k, SUBLANES, stride=PAD), :] for k in range(3))
                sn = sx * ax + sy * ay + sz * az
                rn = rx * ax + ry * ay + rz * az
                st = sx * tx + sy * ty + sz * tz
                rt = rx * tx + ry * ty + rz * tz
                sp = sx * ux + sy * uy
                rp = rx * ux + ry * uy
                dot = sx * rx + sy * ry + sz * rz
                both = sn * rn
                values = (nh * (dot - both), nv * both, nc * (st * rn + sn * rt), nc * (sp * rn + sn * rp))
                place = ((base if near else batch * batch_rows) + start) * 4
                for k in range(4):
                    sens_ref[pl.ds(place + k, SUBLANES, stride=4), :] = values[k]
                squares[pl.ds(batch * batch_rows + start, SUBLANES), :] = (
                    values[0] * values[0] + values[1] * values[1] + values[2] * values[2] + values[3] * values[3]
                )

        close(group_rows // batch_rows - 1)


def sens_block(rows, fields, lane_block, coef, before, near, fill_steps, group_rows):
    shards, comps, owned, _ = fields.shape
    total = rows.size // 4
    groups = total // group_rows
    if near:
        fields_spec = sens_spec = pl.BlockSpec(memory_space=pltpu.VMEM)
        sens_shape = pltpu.VMEM((total * 4, LANES), jnp.float32)
    else:
        sens_spec = pl.BlockSpec((group_rows * 4, LANES), lambda i: (jnp.maximum(i - fill_steps, 0), 0))
        sens_shape = pltpu.HBM((total * 4, LANES), jnp.float32)
        fields_spec = pl.BlockSpec(
            (shards // fill_steps, comps, owned, LANES), lambda i: (jnp.minimum(i, fill_steps - 1), 0, 0, lane_block)
        )
    sums = pl.BlockSpec((1, group_rows // LANES, LANES), lambda i: (jnp.maximum(i - fill_steps, 0), 0, 0))
    return pl.pallas_call(
        functools.partial(sens_kernel, fill_steps, group_rows, near),
        grid=(fill_steps + groups,),
        in_specs=[
            pl.BlockSpec(memory_space=pltpu.SMEM),
            fields_spec,
            pl.BlockSpec((16, LANES), lambda i: (0, 0)),
            sums,
        ],
        out_specs=[sens_spec, sums],
        out_shape=[
            sens_shape,
            jax.ShapeDtypeStruct((groups, group_rows // LANES, LANES), jnp.float32),
        ],
        scratch_shapes=[
            pltpu.VMEM((shards * owned * PAD, LANES), jnp.float32),
            pltpu.VMEM((2 * UNROLL * SUBLANES * PAD, LANES), jnp.float32),
            pltpu.VMEM((group_rows, LANES), jnp.float32),
        ],
        cost_estimate=pl.CostEstimate(
            flops=total * LANES * 64,
            bytes_accessed=(shards * comps * owned * LANES * 2 + total * 5 * LANES * 4) * 4,
            transcendentals=0,
        ),
        compiler_params=pltpu.CompilerParams(vmem_limit_bytes=SENS_LIMIT),
        name="sens_block",
    )(rows, fields, coef, before)


def scale_kernel(inverse, far, mine_ref, theirs_ref, *refs):
    sens_refs, (out_ref, cover_ref, held, ready, spread, cover, in_sems, out_sems) = refs[:-8], refs[-8:]
    far_refs, near_refs = sens_refs[:far], sens_refs[far:]
    rows = spread.shape[0]
    step_rows = rows // 4
    steps = ready.shape[0] // step_rows

    def arrive(step, b):
        part = pl.ds(pl.multiple_of(step * rows, rows), rows)
        return pltpu.make_async_copy(far_refs[b].at[part], held.at[b, part], in_sems.at[step, b])

    def leave(step):
        part = pl.ds(pl.multiple_of(step * step_rows, step_rows), step_rows)
        return pltpu.make_async_copy(ready.at[part], out_ref.at[part], out_sems.at[step])

    for step in range(steps):
        for b in range(far):
            arrive(step, b).start()
    cover[...] = jnp.zeros_like(cover)

    @pl.loop(0, steps)
    def _(step):
        for k in range(step_rows // LANES):
            line = pl.ds(step * (step_rows // LANES) + k, 1)
            meansq = (mine_ref[line, :] + theirs_ref[line, :]) * inverse
            column = jnp.broadcast_to(lax.rsqrt(meansq + 1e-06), (LANES, LANES)).T
            for p in range(4):
                spread[pl.ds(k * 4 * LANES + p, LANES, stride=4), :] = column
        part = pl.ds(pl.multiple_of(step * rows, rows), rows)

        def write(b, values):
            normed = values * spread[...]
            place = pl.ds(pl.multiple_of(step * step_rows, step_rows), step_rows)
            lanes = slice(b * LANES, (b + 1) * LANES)
            ready[place, :, lanes] = normed.astype(ready.dtype).reshape(step_rows, 4, LANES)
            squares = (normed * normed).reshape(rows // SUBLANES, SUBLANES, LANES)
            cover[pl.ds(b * SUBLANES, SUBLANES), :] += jnp.sum(squares, axis=0)

        for b, ref in enumerate(near_refs):
            write(far + b, ref[part, :])
        for b in range(far):
            arrive(step, b).wait()
            write(b, held[b, part, :])
        leave(step).start()

    for b in range(len(sens_refs)):
        cover_ref[pl.ds(b, 1), :] = jnp.sum(cover[pl.ds(b * SUBLANES, SUBLANES), :], axis=0, keepdims=True)
    for step in range(steps):
        leave(step).wait()


def scaled(mine, theirs, inverse, far, near, step_rows):
    columns, total = len(far) + len(near), (far + near)[0].shape[0] // 4
    steps = total // step_rows
    near = [pltpu.with_memory_space_constraint(s, pltpu.VMEM) for s in near]
    whole = pl.BlockSpec(memory_space=pltpu.VMEM)
    out, cover = pl.pallas_call(
        functools.partial(scale_kernel, inverse, len(far)),
        in_specs=[whole, whole] + [pl.BlockSpec(memory_space=pltpu.HBM)] * len(far) + [whole] * len(near),
        out_specs=[pl.BlockSpec(memory_space=pltpu.HBM), whole],
        out_shape=[
            jax.ShapeDtypeStruct((total, 4, columns * LANES), jnp.bfloat16),
            jax.ShapeDtypeStruct((columns, LANES), jnp.float32),
        ],
        scratch_shapes=[
            pltpu.VMEM((len(far), total * 4, LANES), jnp.float32),
            pltpu.VMEM((total, 4, columns * LANES), jnp.bfloat16),
            pltpu.VMEM((step_rows * 4, LANES), jnp.float32),
            pltpu.VMEM((columns * SUBLANES, LANES), jnp.float32),
            pltpu.SemaphoreType.DMA((steps, len(far))),
            pltpu.SemaphoreType.DMA((steps,)),
        ],
        compiler_params=pltpu.CompilerParams(vmem_limit_bytes=SCALE_LIMIT),
        name="scaled",
    )(mine.reshape(-1, LANES), theirs.reshape(-1, LANES), *far, *near)
    return out, cover.reshape(columns * LANES)


def sum_over_cells(x, shards):
    if shards & (shards - 1):
        return lax.psum(x, "cell"), jnp.zeros_like(x)
    other, bit = jnp.zeros_like(x), 1
    while bit < shards:
        x = x + other
        other = lax.ppermute(x, "cell", [(i, i ^ bit) for i in range(shards)])
        bit *= 2
    return x, other


def coefficients(horiz, vertical, tilt_angle, azimuth):
    sin_t, cos_t = jnp.sin(tilt_angle), jnp.cos(tilt_angle)
    sin_p, cos_p = jnp.sin(azimuth), jnp.cos(azimuth)
    zero = jnp.zeros_like(horiz)
    return jnp.stack(
        [
            sin_t * cos_p,
            sin_t * sin_p,
            cos_t,
            cos_t * cos_p,
            cos_t * sin_p,
            -sin_t,
            -sin_t * sin_p,
            sin_t * cos_p,
            -horiz,
            -vertical,
            horiz - vertical,
        ]
        + [zero] * 5
    )


def cell_parts(fields, shards):
    cell_dev = fields.shape[2] // shards
    if fields.size * fields.dtype.itemsize <= 16 * MIB:
        return (cell_dev - LANES, LANES)
    return (LANES,) * (cell_dev // LANES)


def transfer_and_solve(ready, fields, quads, rank, properties, kept, shards):
    comps, owned, cells = fields.shape
    cell_dev = cells // shards
    total = quads.shape[1]
    coef = coefficients(*properties)
    rows = quads * PAD if rank is None else table_rows(quads, rank, owned, kept)
    rows = rows.reshape(-1)
    far, near, before = [], [], jnp.zeros((total // GROUP_ROWS, GROUP_ROWS // LANES, LANES), jnp.float32)

    def finish(received, first, before, last):
        width = received.shape[-1]
        here = last and width == LANES and total * 4 * LANES * 4 <= NEAR_BYTES
        for k in range(width // LANES):
            own = coef[:, first + k * LANES : first + (k + 1) * LANES]
            values, before = sens_block(rows, received, k, own, before, here, FILL_STEPS, GROUP_ROWS)
            (near if here else far).append(values)
        return before

    first, received = 0, None
    for width in cell_parts(fields, shards):
        if ready is None:
            ready = send_order(fields, rank, kept, shards, first, width)
        if received is not None:
            ready, received = lax.optimization_barrier((ready, received))
        arriving = lax.all_to_all(ready, "cell", split_axis=0, concat_axis=0, tiled=True)
        if received is not None:
            before = finish(received, first - received.shape[-1], before, False)
        received, ready = arriving, None
        first += width
    before = finish(received, first - received.shape[-1], before, True)
    mine, theirs = sum_over_cells(before, shards)
    return scaled(mine, theirs, 1.0 / (4.0 * cell_dev * shards), far, near, SCALE_ROWS)


def local(fields, horiz, vertical, tilt_angle, azimuth, electrode_quads):
    shards = lax.axis_size("cell")
    owned = fields.shape[0]
    fields = fields.transpose(1, 0, 2)
    quads = electrode_quads.T
    properties = (horiz, vertical, tilt_angle, azimuth)
    if owned % LANES or owned > 2 * LANES:
        return transfer_and_solve(None, fields, quads, None, properties, owned, shards)
    keeps = tuple(sorted({owned * part // 32 // ROW_TILE * ROW_TILE for part in KEEPS}))
    ready, rank, chosen = send_first(fields, quads, keeps, shards, cell_parts(fields, shards)[0])

    def branch(k):
        if k == len(keeps):
            return lambda ready, rank, *rest: transfer_and_solve(None, *rest[:2], None, rest[2:], owned, shards)
        return lambda ready, rank, *rest: transfer_and_solve(
            ready[k], *rest[:2], rank, rest[2:], keeps[k], shards
        )

    branches = [branch(k) for k in range(len(keeps) + 1)]
    return lax.switch(chosen, branches, ready, rank, fields, quads, *properties)


def solution(mesh):
    placed = (
        P(("grp", "cell"), None, None),
        P(("grp", "cell")),
        P(("grp", "cell")),
        P(("grp", "cell")),
        P(("grp", "cell")),
        P("grp", None),
    )
    return jax.shard_map(
        local,
        mesh=mesh,
        in_specs=placed,
        out_specs=(P("grp", None, "cell"), P(("grp", "cell"))),
        check_vma=False,
    )
```

```python
import functools

import jax
import jax.numpy as jnp
from jax import lax
from jax.experimental import pallas as pl
from jax.experimental.pallas import tpu as pltpu
from jax.sharding import PartitionSpec as P

LANES = 128
SUBLANES = 8
UNROLL = 16
FILL_STEPS = 4
GROUP_ROWS = 512
SCALE_ROWS = 256
ROW_TILE = 8
KEEPS = (29, 30)
PAD = 4
MIB = 1 << 20
VMEM_LIMIT = 60 * MIB
SENS_LIMIT = 32 * MIB
SCALE_LIMIT = 48 * MIB
NEAR_BYTES = 4 * MIB


def one_hots(quads_ref, column, high):
    index = quads_ref[pl.ds(column, 1), :]
    total = index.shape[1]
    upper = lax.broadcasted_iota(jnp.int32, (high, total), 0) == index // LANES
    lower = lax.broadcasted_iota(jnp.int32, (LANES, total), 0) == index % LANES
    return upper.astype(jnp.bfloat16), lower.astype(jnp.bfloat16)


def named_ranks(quads_ref, high, per):
    count = jnp.zeros((high, LANES), jnp.float32)
    for column in range(4):
        upper, lower = one_hots(quads_ref, column, high)
        count += lax.dot_general(upper, lower, (((1,), (1,)), ((), ())), preferred_element_type=jnp.float32)
    named = (count > 0).astype(jnp.bfloat16)
    i, j = (lax.broadcasted_iota(jnp.int32, (LANES, LANES), d) for d in range(2))
    within = jnp.dot(named, (i < j).astype(jnp.bfloat16), preferred_element_type=jnp.float32)
    lines = jnp.dot(named, jnp.ones((LANES, LANES), jnp.bfloat16), preferred_element_type=jnp.float32)
    i, j = (lax.broadcasted_iota(jnp.int32, (high, high), d) for d in range(2))
    ahead = ((j < i) & (j // per == i // per)).astype(jnp.bfloat16)
    before = jnp.dot(ahead, lines.astype(jnp.bfloat16), preferred_element_type=jnp.float32)
    return jnp.where(count > 0, within + before, -1.0)


def table_rows_kernel(owned, kept, quads_ref, rank_ref, rows_ref):
    rank = rank_ref[...].astype(jnp.bfloat16)
    for column in range(4):
        upper, lower = one_hots(quads_ref, column, rank.shape[0])
        ranks = lax.dot_general(rank, upper, (((0,), (0,)), ((), ())), preferred_element_type=jnp.float32)
        own = jnp.sum(ranks * lower.astype(jnp.float32), axis=0, keepdims=True).astype(jnp.int32)
        rows_ref[pl.ds(column, 1), :] = (quads_ref[pl.ds(column, 1), :] // owned * kept + own) * PAD


def table_rows(quads, rank, owned, kept):
    whole = pl.BlockSpec(memory_space=pltpu.VMEM)
    return pl.pallas_call(
        functools.partial(table_rows_kernel, owned, kept),
        in_specs=[whole, whole],
        out_specs=whole,
        out_shape=jax.ShapeDtypeStruct(quads.shape, jnp.int32),
        name="table_rows",
    )(quads, rank)


def send_order_kernel(first, fields_ref, out_ref, held, in_sems, out_sems):
    shards, _, _, width = held.shape
    cell_dev = fields_ref.shape[2] // shards
    arrive = [
        pltpu.make_async_copy(fields_ref.at[:, :, pl.ds(d * cell_dev + first, width)], held.at[d], in_sems.at[d])
        for d in range(shards)
    ]
    leave = [pltpu.make_async_copy(held.at[d], out_ref.at[d], out_sems.at[d]) for d in range(shards)]
    for copy in arrive:
        copy.start()
    for d in range(shards):
        arrive[d].wait()
        leave[d].start()
    for copy in leave:
        copy.wait()


def choose_rows(choose, rank_ref):
    kept, owned = choose.shape
    me = lax.axis_index("cell")
    place = lax.broadcasted_iota(jnp.int32, (kept, LANES), 0).astype(jnp.float32)
    for k in range(owned // LANES):
        line = rank_ref[pl.ds(me * (owned // LANES) + k, 1), :]
        choose[:, k * LANES : (k + 1) * LANES] = (place == line).astype(choose.dtype)


def send_chosen(arrive, choose, held, packed, out_ref, out_sems):
    shards, comps = held.shape[:2]
    kept = packed.shape[2]

    def leave(d):
        return pltpu.make_async_copy(packed.at[d], out_ref.at[d], out_sems.at[d])

    @pl.loop(0, shards)
    def _(d):
        arrive(d).wait()
        for comp in range(comps):
            rows = jnp.dot(choose[pl.ds(0, kept), :], held[d, comp], preferred_element_type=jnp.float32)
            packed[d, comp] = rows.astype(packed.dtype)
        leave(d).start()

    @pl.loop(0, shards)
    def _(d):
        leave(d).wait()


def arrival(first, fields_ref, held, in_sems):
    shards, _, _, width = held.shape
    cell_dev = fields_ref.shape[2] // shards

    def arrive(d):
        lanes = pl.ds(pl.multiple_of(d * cell_dev + first, LANES), width)
        return pltpu.make_async_copy(fields_ref.at[:, :, lanes], held.at[d], in_sems.at[d])

    return arrive


def send_named_kernel(first, fields_ref, rank_ref, out_ref, held, packed, choose, in_sems, out_sems):
    arrive = arrival(first, fields_ref, held, in_sems)
    for d in range(held.shape[0]):
        arrive(d).start()
    choose_rows(choose, rank_ref)
    send_chosen(arrive, choose, held, packed, out_ref, out_sems)


def send_first_kernel(keeps, fields_ref, quads_ref, *refs):
    out_refs, (rank_ref, chosen_ref, held) = refs[: len(keeps)], refs[len(keeps) : len(keeps) + 3]
    packed, (choose, in_sems, out_sems) = refs[len(keeps) + 3 : -3], refs[-3:]
    arrive = arrival(0, fields_ref, held, in_sems)
    for d in range(held.shape[0]):
        arrive(d).start()
    rank = named_ranks(quads_ref, rank_ref.shape[0], held.shape[2] // LANES)
    rank_ref[...] = rank
    most = (jnp.max(rank) + 1.0).astype(jnp.int32)
    chosen = sum((most > kept).astype(jnp.int32) for kept in keeps)
    chosen_ref[0] = chosen
    choose_rows(choose, rank_ref)
    for k, kept in enumerate(keeps):

        @pl.when(chosen == k)
        def _():
            send_chosen(arrive, choose, held, packed[k], out_refs[k], out_sems)

    @pl.when(chosen == len(keeps))
    def _():
        for d in range(held.shape[0]):
            arrive(d).wait()


def send_first(fields, quads, keeps, shards, width):
    comps, owned, cells = fields.shape
    sent = [(shards, comps, kept, width) for kept in keeps]
    anywhere, whole = pl.BlockSpec(memory_space=pl.ANY), pl.BlockSpec(memory_space=pltpu.VMEM)
    *ready, rank, chosen = pl.pallas_call(
        functools.partial(send_first_kernel, keeps),
        in_specs=[anywhere, whole],
        out_specs=[anywhere] * len(keeps) + [whole, pl.BlockSpec(memory_space=pltpu.SMEM)],
        out_shape=[jax.ShapeDtypeStruct(shape, fields.dtype) for shape in sent]
        + [
            jax.ShapeDtypeStruct((shards * owned // LANES, LANES), jnp.float32),
            jax.ShapeDtypeStruct((1,), jnp.int32),
        ],
        scratch_shapes=[pltpu.VMEM((shards, comps, owned, width), fields.dtype)]
        + [pltpu.VMEM(shape, fields.dtype) for shape in sent]
        + [
            pltpu.VMEM((max(keeps), owned), fields.dtype),
            pltpu.SemaphoreType.DMA((shards,)),
            pltpu.SemaphoreType.DMA((shards,)),
        ],
        compiler_params=pltpu.CompilerParams(vmem_limit_bytes=VMEM_LIMIT),
        name="send_first",
    )(fields, quads)
    return ready, rank, chosen[0]


def send_order(fields, rank, kept, shards, first, width):
    comps, owned, cells = fields.shape
    held = (shards, comps, owned, width)
    sent = (shards, comps, kept, width)
    scratch = [pltpu.VMEM(held, fields.dtype)]
    in_specs, args = [pl.BlockSpec(memory_space=pl.ANY)], [fields]
    if rank is not None:
        scratch += [pltpu.VMEM(sent, fields.dtype), pltpu.VMEM((kept, owned), fields.dtype)]
        in_specs.append(pl.BlockSpec(memory_space=pltpu.VMEM))
        args.append(rank)
    return pl.pallas_call(
        functools.partial(send_order_kernel if rank is None else send_named_kernel, first),
        in_specs=in_specs,
        out_specs=pl.BlockSpec(memory_space=pl.ANY),
        out_shape=jax.ShapeDtypeStruct(sent, fields.dtype),
        scratch_shapes=scratch + [pltpu.SemaphoreType.DMA((shards,)), pltpu.SemaphoreType.DMA((shards,))],
        cost_estimate=pl.CostEstimate(flops=0, bytes_accessed=4 * comps * owned * width * shards, transcendentals=0),
        compiler_params=pltpu.CompilerParams(vmem_limit_bytes=VMEM_LIMIT),
        name="send_order",
    )(*args)


def sens_kernel(fill_steps, group_rows, near, all_rows_ref, fields_ref, coef_ref, before_ref, *refs):
    sens_ref, sumsq_ref, table, picked, squares, rows_ref, rows_sem = refs
    step = pl.program_id(0)
    rows_copy = pltpu.make_async_copy(all_rows_ref, rows_ref, rows_sem)

    @pl.when(step == 0)
    def _():
        rows_copy.start()

    @pl.when(step == fill_steps)
    def _():
        rows_copy.wait()

    owned = fields_ref.shape[2]
    sources = table.shape[0] // (PAD * owned * fill_steps)
    batch_rows = SUBLANES * UNROLL
    total_rows = rows_ref.shape[0] // 4

    @pl.when(step < fill_steps)
    def _():
        for source in range(sources):
            place = step * sources + source
            for comp in range(fields_ref.shape[1]):
                values = fields_ref[place if near else source, comp].astype(jnp.float32)
                table[pl.ds(place * (owned * PAD) + comp, owned, stride=PAD), :] = values

    @pl.when(step >= fill_steps)
    def _():
        first = (step - fill_steps) * group_rows
        coef = [coef_ref[pl.ds(k, 1), :] for k in range(11)]
        ax, ay, az, tx, ty, tz, ux, uy, nh, nv, nc = coef

        def fetch(index):
            return table[pl.ds(pl.multiple_of(rows_ref[index], PAD), PAD), :]

        def close(batch):
            turned = squares[pl.ds(pl.multiple_of(batch * batch_rows, batch_rows), batch_rows), :].T
            total = jnp.sum(turned, axis=0, keepdims=True)
            sumsq_ref[0, pl.ds(batch, 1), :] = total + before_ref[0, pl.ds(batch, 1), :]

        squares[pl.ds(0, batch_rows), :] = jnp.zeros((batch_rows, LANES), jnp.float32)

        @pl.loop(0, group_rows // batch_rows)
        def _(batch):
            close(jnp.maximum(batch - 1, 0))
            base = first + batch * batch_rows
            for j in range(batch_rows):
                i = base + j
                picked[pl.ds(j * PAD, PAD), :] = fetch(i) - fetch(total_rows + i)
                picked[pl.ds((batch_rows + j) * PAD, PAD), :] = fetch(2 * total_rows + i) - fetch(3 * total_rows + i)
            for g in range(UNROLL):
                start = g * SUBLANES
                sx, sy, sz = (picked[pl.ds(start * PAD + k, SUBLANES, stride=PAD), :] for k in range(3))
                rx, ry, rz = (picked[pl.ds((batch_rows + start) * PAD + k, SUBLANES, stride=PAD), :] for k in range(3))
                sn = sx * ax + sy * ay + sz * az
                rn = rx * ax + ry * ay + rz * az
                st = sx * tx + sy * ty + sz * tz
                rt = rx * tx + ry * ty + rz * tz
                sp = sx * ux + sy * uy
                rp = rx * ux + ry * uy
                dot = sx * rx + sy * ry + sz * rz
                both = sn * rn
                values = (nh * (dot - both), nv * both, nc * (st * rn + sn * rt), nc * (sp * rn + sn * rp))
                place = ((base if near else batch * batch_rows) + start) * 4
                for k in range(4):
                    sens_ref[pl.ds(place + k, SUBLANES, stride=4), :] = values[k]
                squares[pl.ds(batch * batch_rows + start, SUBLANES), :] = (
                    values[0] * values[0] + values[1] * values[1] + values[2] * values[2] + values[3] * values[3]
                )

        close(group_rows // batch_rows - 1)


def sens_block(rows, fields, lane_block, coef, before, near, fill_steps, group_rows):
    shards, comps, owned, _ = fields.shape
    total = rows.size // 4
    groups = total // group_rows
    if near:
        fields_spec = sens_spec = pl.BlockSpec(memory_space=pltpu.VMEM)
        sens_shape = pltpu.VMEM((total * 4, LANES), jnp.float32)
    else:
        sens_spec = pl.BlockSpec((group_rows * 4, LANES), lambda i: (jnp.maximum(i - fill_steps, 0), 0))
        sens_shape = pltpu.HBM((total * 4, LANES), jnp.float32)
        fields_spec = pl.BlockSpec(
            (shards // fill_steps, comps, owned, LANES), lambda i: (jnp.minimum(i, fill_steps - 1), 0, 0, lane_block)
        )
    sums = pl.BlockSpec((1, group_rows // LANES, LANES), lambda i: (jnp.maximum(i - fill_steps, 0), 0, 0))
    return pl.pallas_call(
        functools.partial(sens_kernel, fill_steps, group_rows, near),
        grid=(fill_steps + groups,),
        in_specs=[
            pl.BlockSpec(memory_space=pl.ANY),
            fields_spec,
            pl.BlockSpec((16, LANES), lambda i: (0, 0)),
            sums,
        ],
        out_specs=[sens_spec, sums],
        out_shape=[
            sens_shape,
            jax.ShapeDtypeStruct((groups, group_rows // LANES, LANES), jnp.float32),
        ],
        scratch_shapes=[
            pltpu.VMEM((shards * owned * PAD, LANES), jnp.float32),
            pltpu.VMEM((2 * UNROLL * SUBLANES * PAD, LANES), jnp.float32),
            pltpu.VMEM((group_rows, LANES), jnp.float32),
            pltpu.SMEM(rows.shape, jnp.int32),
            pltpu.SemaphoreType.DMA,
        ],
        cost_estimate=pl.CostEstimate(
            flops=total * LANES * 64,
            bytes_accessed=(shards * comps * owned * LANES * 2 + total * 5 * LANES * 4) * 4,
            transcendentals=0,
        ),
        compiler_params=pltpu.CompilerParams(vmem_limit_bytes=SENS_LIMIT),
        name="sens_block",
    )(rows, fields, coef, before)


def scale_kernel(inverse, far, mine_ref, theirs_ref, *refs):
    sens_refs, (out_ref, cover_ref, held, ready, spread, cover, in_sems, out_sems) = refs[:-8], refs[-8:]
    far_refs, near_refs = sens_refs[:far], sens_refs[far:]
    rows = spread.shape[0]
    step_rows = rows // 4
    steps = ready.shape[0] // step_rows

    def arrive(step, b):
        part = pl.ds(pl.multiple_of(step * rows, rows), rows)
        return pltpu.make_async_copy(far_refs[b].at[part], held.at[b, part], in_sems.at[step, b])

    def leave(step):
        part = pl.ds(pl.multiple_of(step * step_rows, step_rows), step_rows)
        return pltpu.make_async_copy(ready.at[part], out_ref.at[part], out_sems.at[step])

    for step in range(steps):
        for b in range(far):
            arrive(step, b).start()
    cover[...] = jnp.zeros_like(cover)

    @pl.loop(0, steps)
    def _(step):
        for k in range(step_rows // LANES):
            line = pl.ds(step * (step_rows // LANES) + k, 1)
            meansq = (mine_ref[line, :] + theirs_ref[line, :]) * inverse
            column = jnp.broadcast_to(lax.rsqrt(meansq + 1e-06), (LANES, LANES)).T
            for p in range(4):
                spread[pl.ds(k * 4 * LANES + p, LANES, stride=4), :] = column
        part = pl.ds(pl.multiple_of(step * rows, rows), rows)

        def write(b, values):
            normed = values * spread[...]
            place = pl.ds(pl.multiple_of(step * step_rows, step_rows), step_rows)
            lanes = slice(b * LANES, (b + 1) * LANES)
            ready[place, :, lanes] = normed.astype(ready.dtype).reshape(step_rows, 4, LANES)
            squares = (normed * normed).reshape(rows // SUBLANES, SUBLANES, LANES)
            cover[pl.ds(b * SUBLANES, SUBLANES), :] += jnp.sum(squares, axis=0)

        for b, ref in enumerate(near_refs):
            write(far + b, ref[part, :])
        for b in range(far):
            arrive(step, b).wait()
            write(b, held[b, part, :])
        leave(step).start()

    for b in range(len(sens_refs)):
        cover_ref[pl.ds(b, 1), :] = jnp.sum(cover[pl.ds(b * SUBLANES, SUBLANES), :], axis=0, keepdims=True)
    for step in range(steps):
        leave(step).wait()


def scaled(mine, theirs, inverse, far, near, step_rows):
    columns, total = len(far) + len(near), (far + near)[0].shape[0] // 4
    steps = total // step_rows
    near = [pltpu.with_memory_space_constraint(s, pltpu.VMEM) for s in near]
    whole = pl.BlockSpec(memory_space=pltpu.VMEM)
    out, cover = pl.pallas_call(
        functools.partial(scale_kernel, inverse, len(far)),
        in_specs=[whole, whole] + [pl.BlockSpec(memory_space=pltpu.HBM)] * len(far) + [whole] * len(near),
        out_specs=[pl.BlockSpec(memory_space=pltpu.HBM), whole],
        out_shape=[
            jax.ShapeDtypeStruct((total, 4, columns * LANES), jnp.bfloat16),
            jax.ShapeDtypeStruct((columns, LANES), jnp.float32),
        ],
        scratch_shapes=[
            pltpu.VMEM((len(far), total * 4, LANES), jnp.float32),
            pltpu.VMEM((total, 4, columns * LANES), jnp.bfloat16),
            pltpu.VMEM((step_rows * 4, LANES), jnp.float32),
            pltpu.VMEM((columns * SUBLANES, LANES), jnp.float32),
            pltpu.SemaphoreType.DMA((steps, len(far))),
            pltpu.SemaphoreType.DMA((steps,)),
        ],
        compiler_params=pltpu.CompilerParams(vmem_limit_bytes=SCALE_LIMIT),
        name="scaled",
    )(mine.reshape(-1, LANES), theirs.reshape(-1, LANES), *far, *near)
    return out, cover.reshape(columns * LANES)


def sum_over_cells(x, shards):
    if shards & (shards - 1):
        return lax.psum(x, "cell"), jnp.zeros_like(x)
    other, bit = jnp.zeros_like(x), 1
    while bit < shards:
        x = x + other
        other = lax.ppermute(x, "cell", [(i, i ^ bit) for i in range(shards)])
        bit *= 2
    return x, other


def coefficients(horiz, vertical, tilt_angle, azimuth):
    sin_t, cos_t = jnp.sin(tilt_angle), jnp.cos(tilt_angle)
    sin_p, cos_p = jnp.sin(azimuth), jnp.cos(azimuth)
    zero = jnp.zeros_like(horiz)
    return jnp.stack(
        [
            sin_t * cos_p,
            sin_t * sin_p,
            cos_t,
            cos_t * cos_p,
            cos_t * sin_p,
            -sin_t,
            -sin_t * sin_p,
            sin_t * cos_p,
            -horiz,
            -vertical,
            horiz - vertical,
        ]
        + [zero] * 5
    )


def cell_parts(fields, shards):
    cell_dev = fields.shape[2] // shards
    if fields.size * fields.dtype.itemsize <= 16 * MIB:
        return (cell_dev - LANES, LANES)
    return (LANES,) * (cell_dev // LANES)


def transfer_and_solve(ready, fields, quads, rank, properties, kept, shards):
    comps, owned, cells = fields.shape
    cell_dev = cells // shards
    total = quads.shape[1]
    coef = coefficients(*properties)
    rows = quads * PAD if rank is None else table_rows(quads, rank, owned, kept)
    rows = rows.reshape(-1)
    far, near, before = [], [], jnp.zeros((total // GROUP_ROWS, GROUP_ROWS // LANES, LANES), jnp.float32)

    def finish(received, first, before, last):
        width = received.shape[-1]
        here = last and width == LANES and total * 4 * LANES * 4 <= NEAR_BYTES
        for k in range(width // LANES):
            own = coef[:, first + k * LANES : first + (k + 1) * LANES]
            fill_steps, group_rows = (1, total) if here else (FILL_STEPS, GROUP_ROWS)
            before = before.reshape(total // group_rows, group_rows // LANES, LANES)
            values, before = sens_block(rows, received, k, own, before, here, fill_steps, group_rows)
            (near if here else far).append(values)
        return before

    first, received = 0, None
    for width in cell_parts(fields, shards):
        if ready is None:
            ready = send_order(fields, rank, kept, shards, first, width)
        if received is not None:
            ready, received = lax.optimization_barrier((ready, received))
        arriving = lax.all_to_all(ready, "cell", split_axis=0, concat_axis=0, tiled=True)
        if received is not None:
            before = finish(received, first - received.shape[-1], before, False)
        received, ready = arriving, None
        first += width
    before = finish(received, first - received.shape[-1], before, True)
    mine, theirs = sum_over_cells(before, shards)
    return scaled(mine, theirs, 1.0 / (4.0 * cell_dev * shards), far, near, SCALE_ROWS)


def local(fields, horiz, vertical, tilt_angle, azimuth, electrode_quads):
    shards = lax.axis_size("cell")
    owned = fields.shape[0]
    fields = fields.transpose(1, 0, 2)
    quads = electrode_quads.T
    properties = (horiz, vertical, tilt_angle, azimuth)
    if owned % LANES or owned > 2 * LANES:
        return transfer_and_solve(None, fields, quads, None, properties, owned, shards)
    keeps = tuple(sorted({owned * part // 32 // ROW_TILE * ROW_TILE for part in KEEPS}))
    ready, rank, chosen = send_first(fields, quads, keeps, shards, cell_parts(fields, shards)[0])

    def branch(k):
        if k == len(keeps):
            return lambda ready, rank, *rest: transfer_and_solve(None, *rest[:2], None, rest[2:], owned, shards)
        return lambda ready, rank, *rest: transfer_and_solve(
            ready[k], *rest[:2], rank, rest[2:], keeps[k], shards
        )

    branches = [branch(k) for k in range(len(keeps) + 1)]
    return lax.switch(chosen, branches, ready, rank, fields, quads, *properties)


def solution(mesh):
    placed = (
        P(("grp", "cell"), None, None),
        P(("grp", "cell")),
        P(("grp", "cell")),
        P(("grp", "cell")),
        P(("grp", "cell")),
        P("grp", None),
    )
    return jax.shard_map(
        local,
        mesh=mesh,
        in_specs=placed,
        out_specs=(P("grp", None, "cell"), P(("grp", "cell"))),
        check_vma=False,
    )
```

```python
import functools

import jax
import jax.numpy as jnp
from jax import lax
from jax.experimental import pallas as pl
from jax.experimental.pallas import tpu as pltpu
from jax.sharding import PartitionSpec as P

LANES = 128
SUBLANES = 8
UNROLL = 16
FILL_STEPS = 4
GROUP_ROWS = 512
SCALE_ROWS = 256
ROW_TILE = 8
KEEPS = (28, 30)
POOL = 5
PAD = 4
MIB = 1 << 20
VMEM_LIMIT = 60 * MIB
SENS_LIMIT = 32 * MIB
SCALE_LIMIT = 48 * MIB
NEAR_BYTES = 4 * MIB


def one_hots(quads_ref, column, high):
    index = quads_ref[pl.ds(column, 1), :]
    total = index.shape[1]
    upper = lax.broadcasted_iota(jnp.int32, (high, total), 0) == index // LANES
    lower = lax.broadcasted_iota(jnp.int32, (LANES, total), 0) == index % LANES
    return upper.astype(jnp.bfloat16), lower.astype(jnp.bfloat16)


def named_ranks(quads_ref, high, per, base):
    count = jnp.zeros((high, LANES), jnp.float32)
    for column in range(4):
        upper, lower = one_hots(quads_ref, column, high)
        count += lax.dot_general(upper, lower, (((1,), (1,)), ((), ())), preferred_element_type=jnp.float32)
    named = (count > 0).astype(jnp.bfloat16)

    def dot(a, b):
        return jnp.dot(a.astype(jnp.bfloat16), b.astype(jnp.bfloat16), preferred_element_type=jnp.float32)

    i, j = (lax.broadcasted_iota(jnp.int32, (LANES, LANES), d) for d in range(2))
    within = dot(named, i < j)
    lines = dot(named, jnp.ones((LANES, LANES), jnp.bfloat16))
    i, j = (lax.broadcasted_iota(jnp.int32, (high, high), d) for d in range(2))
    rank = jnp.where(count > 0, within + dot((j < i) & (j // per == i // per), lines), -1.0)
    over = jnp.maximum(dot(j // per == i // per, lines) - base, 0.0)
    ahead = dot((j // per < i // per) & (j % per == 0), over)
    slot = jnp.where(rank >= base, rank - base + ahead, -1.0)
    return rank, slot, ahead + over


def table_rows_kernel(quads_ref, place_ref, rows_ref):
    place = place_ref[...]
    coarse = jnp.floor(place * (1.0 / 16.0))
    fine = place - 16.0 * coarse
    for column in range(4):
        upper, lower = one_hots(quads_ref, column, place.shape[0])

        def pick(part):
            spread = lax.dot_general(
                part.astype(jnp.bfloat16), upper, (((0,), (0,)), ((), ())), preferred_element_type=jnp.float32
            )
            return jnp.sum(spread * lower.astype(jnp.float32), axis=0, keepdims=True)

        rows_ref[pl.ds(column, 1), :] = (pick(coarse) * 16.0 + pick(fine)).astype(jnp.int32) * PAD


def table_rows(quads, place):
    whole = pl.BlockSpec(memory_space=pltpu.VMEM)
    return pl.pallas_call(
        table_rows_kernel,
        in_specs=[whole, whole],
        out_specs=whole,
        out_shape=jax.ShapeDtypeStruct(quads.shape, jnp.int32),
        name="table_rows",
    )(quads, place)


def send_order_kernel(first, fields_ref, out_ref, held, in_sems, out_sems):
    shards, _, _, width = held.shape
    cell_dev = fields_ref.shape[2] // shards
    arrive = [
        pltpu.make_async_copy(fields_ref.at[:, :, pl.ds(d * cell_dev + first, width)], held.at[d], in_sems.at[d])
        for d in range(shards)
    ]
    leave = [pltpu.make_async_copy(held.at[d], out_ref.at[d], out_sems.at[d]) for d in range(shards)]
    for copy in arrive:
        copy.start()
    for d in range(shards):
        arrive[d].wait()
        leave[d].start()
    for copy in leave:
        copy.wait()


def choose_rows(choose, rank_ref):
    kept, owned = choose.shape
    me = lax.axis_index("cell")
    place = lax.broadcasted_iota(jnp.int32, (kept, LANES), 0).astype(jnp.float32)
    for k in range(owned // LANES):
        line = rank_ref[pl.ds(me * (owned // LANES) + k, 1), :]
        choose[:, k * LANES : (k + 1) * LANES] = (place == line).astype(choose.dtype)


def send_chosen(arrive, choose, held, packed, out_ref, out_sems):
    shards, comps = held.shape[:2]
    kept = packed.shape[2]

    def leave(d):
        return pltpu.make_async_copy(packed.at[d], out_ref.at[d], out_sems.at[d])

    @pl.loop(0, shards)
    def _(d):
        arrive(d).wait()
        for comp in range(comps):
            rows = jnp.dot(choose[pl.ds(0, kept), :], held[d, comp], preferred_element_type=jnp.float32)
            packed[d, comp] = rows.astype(packed.dtype)
        leave(d).start()

    @pl.loop(0, shards)
    def _(d):
        leave(d).wait()


def arrival(first, fields_ref, held, in_sems):
    shards, _, _, width = held.shape
    cell_dev = fields_ref.shape[2] // shards

    def arrive(d):
        lanes = pl.ds(pl.multiple_of(d * cell_dev + first, LANES), width)
        return pltpu.make_async_copy(fields_ref.at[:, :, lanes], held.at[d], in_sems.at[d])

    return arrive


def send_named_kernel(first, fields_ref, rank_ref, out_ref, held, packed, choose, in_sems, out_sems):
    arrive = arrival(first, fields_ref, held, in_sems)
    for d in range(held.shape[0]):
        arrive(d).start()
    choose_rows(choose, rank_ref)
    send_chosen(arrive, choose, held, packed, out_ref, out_sems)


def send_first_kernel(keeps, pool, fields_ref, quads_ref, *refs):
    out_refs, (rank_ref, slot_ref, place_ref, chosen_ref, held) = refs[: len(keeps)], refs[len(keeps) : len(keeps) + 5]
    packed, (choose, in_sems, out_sems) = refs[len(keeps) + 5 : -3], refs[-3:]
    arrive = arrival(0, fields_ref, held, in_sems)
    for d in range(held.shape[0]):
        arrive(d).start()
    shards, _, owned, _ = held.shape
    high, per = rank_ref.shape[0], owned // LANES
    rank, slot, taken = named_ranks(quads_ref, high, per, float(keeps[0]))
    rank_ref[...] = rank
    slot_ref[...] = slot
    most = (jnp.max(rank) + 1.0).astype(jnp.int32)
    pooled = (jnp.max(taken) <= pool).astype(jnp.int32)
    chosen = sum((most > kept).astype(jnp.int32) for kept in keeps[1:])
    chosen = (1 - pooled) * (1 + chosen)
    chosen_ref[0] = chosen
    owner = (lax.broadcasted_iota(jnp.int32, (high, LANES), 0) // per).astype(jnp.float32)
    place = jnp.where(slot < 0.0, owner * keeps[0] + rank, slot + shards * keeps[0])
    for k, kept in enumerate(keeps[1:]):
        place = jnp.where(chosen == k + 1, owner * kept + rank, place)
    place_ref[...] = place
    choose_rows(choose, rank_ref)
    for k, kept in enumerate(keeps):

        @pl.when(chosen == k)
        def _():
            send_chosen(arrive, choose, held, packed[k], out_refs[k], out_sems)

    @pl.when(chosen == len(keeps))
    def _():
        for d in range(held.shape[0]):
            arrive(d).wait()


def send_first(fields, quads, keeps, pool, shards, width):
    comps, owned, cells = fields.shape
    sent = [(shards, comps, kept, width) for kept in keeps]
    anywhere, whole = pl.BlockSpec(memory_space=pl.ANY), pl.BlockSpec(memory_space=pltpu.VMEM)
    table = jax.ShapeDtypeStruct((shards * owned // LANES, LANES), jnp.float32)
    *ready, rank, slot, place, chosen = pl.pallas_call(
        functools.partial(send_first_kernel, keeps, pool),
        in_specs=[anywhere, whole],
        out_specs=[anywhere] * len(keeps) + [whole] * 3 + [pl.BlockSpec(memory_space=pltpu.SMEM)],
        out_shape=[jax.ShapeDtypeStruct(shape, fields.dtype) for shape in sent]
        + [table] * 3
        + [jax.ShapeDtypeStruct((1,), jnp.int32)],
        scratch_shapes=[pltpu.VMEM((shards, comps, owned, width), fields.dtype)]
        + [pltpu.VMEM(shape, fields.dtype) for shape in sent]
        + [
            pltpu.VMEM((max(keeps), owned), fields.dtype),
            pltpu.SemaphoreType.DMA((shards,)),
            pltpu.SemaphoreType.DMA((shards,)),
        ],
        compiler_params=pltpu.CompilerParams(vmem_limit_bytes=VMEM_LIMIT),
        name="send_first",
    )(fields, quads)
    return ready, (rank, slot, place), chosen[0]


def send_order(fields, rank, kept, shards, first, width):
    comps, owned, cells = fields.shape
    held = (shards, comps, owned, width)
    sent = (shards, comps, kept, width)
    scratch = [pltpu.VMEM(held, fields.dtype)]
    in_specs, args = [pl.BlockSpec(memory_space=pl.ANY)], [fields]
    if rank is not None:
        scratch += [pltpu.VMEM(sent, fields.dtype), pltpu.VMEM((kept, owned), fields.dtype)]
        in_specs.append(pl.BlockSpec(memory_space=pltpu.VMEM))
        args.append(rank)
    return pl.pallas_call(
        functools.partial(send_order_kernel if rank is None else send_named_kernel, first),
        in_specs=in_specs,
        out_specs=pl.BlockSpec(memory_space=pl.ANY),
        out_shape=jax.ShapeDtypeStruct(sent, fields.dtype),
        scratch_shapes=scratch + [pltpu.SemaphoreType.DMA((shards,)), pltpu.SemaphoreType.DMA((shards,))],
        cost_estimate=pl.CostEstimate(flops=0, bytes_accessed=4 * comps * owned * width * shards, transcendentals=0),
        compiler_params=pltpu.CompilerParams(vmem_limit_bytes=VMEM_LIMIT),
        name="send_order",
    )(*args)


def sens_kernel(sources, fill_steps, group_rows, near, all_rows_ref, fields_ref, coef_ref, before_ref, *refs):
    sens_ref, sumsq_ref, table, picked, squares, rows_ref, rows_sem = refs[-7:]
    step = pl.program_id(0)
    rows_copy = pltpu.make_async_copy(all_rows_ref, rows_ref, rows_sem)

    @pl.when(step == 0)
    def _():
        rows_copy.start()

    @pl.when(step == fill_steps)
    def _():
        rows_copy.wait()
        if len(refs) > 7:
            pool_ref = refs[0]
            pool = pool_ref.shape[1]
            for comp in range(pool_ref.shape[0]):
                values = pool_ref[comp].astype(jnp.float32)
                table[pl.ds(table.shape[0] - pool * PAD + comp, pool, stride=PAD), :] = values

    owned = fields_ref.shape[2]
    batch_rows = SUBLANES * UNROLL
    total_rows = rows_ref.shape[0] // 4

    @pl.when(step < fill_steps)
    def _():
        for source in range(sources):
            place = step * sources + source
            for comp in range(fields_ref.shape[1]):
                values = fields_ref[place if near else source, comp].astype(jnp.float32)
                table[pl.ds(place * (owned * PAD) + comp, owned, stride=PAD), :] = values

    @pl.when(step >= fill_steps)
    def _():
        first = (step - fill_steps) * group_rows
        coef = [coef_ref[pl.ds(k, 1), :] for k in range(11)]
        ax, ay, az, tx, ty, tz, ux, uy, nh, nv, nc = coef

        def fetch(index):
            return table[pl.ds(pl.multiple_of(rows_ref[index], PAD), PAD), :]

        def close(batch):
            turned = squares[pl.ds(pl.multiple_of(batch * batch_rows, batch_rows), batch_rows), :].T
            total = jnp.sum(turned, axis=0, keepdims=True)
            sumsq_ref[0, pl.ds(batch, 1), :] = total + before_ref[0, pl.ds(batch, 1), :]

        squares[pl.ds(0, batch_rows), :] = jnp.zeros((batch_rows, LANES), jnp.float32)

        @pl.loop(0, group_rows // batch_rows)
        def _(batch):
            close(jnp.maximum(batch - 1, 0))
            base = first + batch * batch_rows
            for j in range(batch_rows):
                i = base + j
                picked[pl.ds(j * PAD, PAD), :] = fetch(i) - fetch(total_rows + i)
                picked[pl.ds((batch_rows + j) * PAD, PAD), :] = fetch(2 * total_rows + i) - fetch(3 * total_rows + i)
            for g in range(UNROLL):
                start = g * SUBLANES
                sx, sy, sz = (picked[pl.ds(start * PAD + k, SUBLANES, stride=PAD), :] for k in range(3))
                rx, ry, rz = (picked[pl.ds((batch_rows + start) * PAD + k, SUBLANES, stride=PAD), :] for k in range(3))
                sn = sx * ax + sy * ay + sz * az
                rn = rx * ax + ry * ay + rz * az
                st = sx * tx + sy * ty + sz * tz
                rt = rx * tx + ry * ty + rz * tz
                sp = sx * ux + sy * uy
                rp = rx * ux + ry * uy
                dot = sx * rx + sy * ry + sz * rz
                both = sn * rn
                values = (nh * (dot - both), nv * both, nc * (st * rn + sn * rt), nc * (sp * rn + sn * rp))
                place = ((base if near else batch * batch_rows) + start) * 4
                for k in range(4):
                    sens_ref[pl.ds(place + k, SUBLANES, stride=4), :] = values[k]
                squares[pl.ds(batch * batch_rows + start, SUBLANES), :] = (
                    values[0] * values[0] + values[1] * values[1] + values[2] * values[2] + values[3] * values[3]
                )

        close(group_rows // batch_rows - 1)


def sens_block(rows, fields, pool, lane_block, cell_block, coef, before, near, fill_steps, group_rows):
    shards, comps, owned, _ = fields.shape
    total = rows.size // 4
    groups = total // group_rows
    if near:
        fields_spec = sens_spec = pl.BlockSpec(memory_space=pltpu.VMEM)
        sens_shape = pltpu.VMEM((total * 4, LANES), jnp.float32)
    else:
        sens_spec = pl.BlockSpec((group_rows * 4, LANES), lambda i: (jnp.maximum(i - fill_steps, 0), 0))
        sens_shape = pltpu.HBM((total * 4, LANES), jnp.float32)
        fields_spec = pl.BlockSpec(
            (shards // fill_steps, comps, owned, LANES), lambda i: (jnp.minimum(i, fill_steps - 1), 0, 0, lane_block)
        )
    sums = pl.BlockSpec((1, group_rows // LANES, LANES), lambda i: (jnp.maximum(i - fill_steps, 0), 0, 0))
    pools = [] if pool is None else [pool]
    pool_rows = sum(p.shape[1] for p in pools)
    return pl.pallas_call(
        functools.partial(sens_kernel, shards // fill_steps, fill_steps, group_rows, near),
        grid=(fill_steps + groups,),
        in_specs=[
            pl.BlockSpec(memory_space=pl.ANY),
            fields_spec,
            pl.BlockSpec((16, LANES), lambda i: (0, 0)),
            sums,
        ]
        + [pl.BlockSpec((comps, pool_rows, LANES), lambda i: (0, 0, cell_block)) for _ in pools],
        out_specs=[sens_spec, sums],
        out_shape=[
            sens_shape,
            jax.ShapeDtypeStruct((groups, group_rows // LANES, LANES), jnp.float32),
        ],
        scratch_shapes=[
            pltpu.VMEM(((shards * owned + pool_rows) * PAD, LANES), jnp.float32),
            pltpu.VMEM((2 * UNROLL * SUBLANES * PAD, LANES), jnp.float32),
            pltpu.VMEM((group_rows, LANES), jnp.float32),
            pltpu.SMEM(rows.shape, jnp.int32),
            pltpu.SemaphoreType.DMA,
        ],
        cost_estimate=pl.CostEstimate(
            flops=total * LANES * 64,
            bytes_accessed=(shards * comps * owned * LANES * 2 + total * 5 * LANES * 4) * 4,
            transcendentals=0,
        ),
        compiler_params=pltpu.CompilerParams(vmem_limit_bytes=SENS_LIMIT),
        name="sens_block",
    )(rows, fields, coef, before, *pools)


def scale_kernel(inverse, far, mine_ref, theirs_ref, *refs):
    sens_refs, (out_ref, cover_ref, held, ready, spread, cover, in_sems, out_sems) = refs[:-8], refs[-8:]
    far_refs, near_refs = sens_refs[:far], sens_refs[far:]
    rows = spread.shape[0]
    step_rows = rows // 4
    steps = ready.shape[0] // step_rows

    def arrive(step, b):
        part = pl.ds(pl.multiple_of(step * rows, rows), rows)
        return pltpu.make_async_copy(far_refs[b].at[part], held.at[b, part], in_sems.at[step, b])

    def leave(step):
        part = pl.ds(pl.multiple_of(step * step_rows, step_rows), step_rows)
        return pltpu.make_async_copy(ready.at[part], out_ref.at[part], out_sems.at[step])

    for step in range(steps):
        for b in range(far):
            arrive(step, b).start()
    cover[...] = jnp.zeros_like(cover)

    @pl.loop(0, steps)
    def _(step):
        for k in range(step_rows // LANES):
            line = pl.ds(step * (step_rows // LANES) + k, 1)
            meansq = (mine_ref[line, :] + theirs_ref[line, :]) * inverse
            column = jnp.broadcast_to(lax.rsqrt(meansq + 1e-06), (LANES, LANES)).T
            for p in range(4):
                spread[pl.ds(k * 4 * LANES + p, LANES, stride=4), :] = column
        part = pl.ds(pl.multiple_of(step * rows, rows), rows)

        def write(b, values):
            normed = values * spread[...]
            place = pl.ds(pl.multiple_of(step * step_rows, step_rows), step_rows)
            lanes = slice(b * LANES, (b + 1) * LANES)
            ready[place, :, lanes] = normed.astype(ready.dtype).reshape(step_rows, 4, LANES)
            squares = (normed * normed).reshape(rows // SUBLANES, SUBLANES, LANES)
            cover[pl.ds(b * SUBLANES, SUBLANES), :] += jnp.sum(squares, axis=0)

        for b, ref in enumerate(near_refs):
            write(far + b, ref[part, :])
        for b in range(far):
            arrive(step, b).wait()
            write(b, held[b, part, :])
        leave(step).start()

    for b in range(len(sens_refs)):
        cover_ref[pl.ds(b, 1), :] = jnp.sum(cover[pl.ds(b * SUBLANES, SUBLANES), :], axis=0, keepdims=True)
    for step in range(steps):
        leave(step).wait()


def scaled(mine, theirs, inverse, far, near, step_rows):
    columns, total = len(far) + len(near), (far + near)[0].shape[0] // 4
    steps = total // step_rows
    near = [pltpu.with_memory_space_constraint(s, pltpu.VMEM) for s in near]
    whole = pl.BlockSpec(memory_space=pltpu.VMEM)
    out, cover = pl.pallas_call(
        functools.partial(scale_kernel, inverse, len(far)),
        in_specs=[whole, whole] + [pl.BlockSpec(memory_space=pltpu.HBM)] * len(far) + [whole] * len(near),
        out_specs=[pl.BlockSpec(memory_space=pltpu.HBM), whole],
        out_shape=[
            jax.ShapeDtypeStruct((total, 4, columns * LANES), jnp.bfloat16),
            jax.ShapeDtypeStruct((columns, LANES), jnp.float32),
        ],
        scratch_shapes=[
            pltpu.VMEM((len(far), total * 4, LANES), jnp.float32),
            pltpu.VMEM((total, 4, columns * LANES), jnp.bfloat16),
            pltpu.VMEM((step_rows * 4, LANES), jnp.float32),
            pltpu.VMEM((columns * SUBLANES, LANES), jnp.float32),
            pltpu.SemaphoreType.DMA((steps, len(far))),
            pltpu.SemaphoreType.DMA((steps,)),
        ],
        compiler_params=pltpu.CompilerParams(vmem_limit_bytes=SCALE_LIMIT),
        name="scaled",
    )(mine.reshape(-1, LANES), theirs.reshape(-1, LANES), *far, *near)
    return out, cover.reshape(columns * LANES)


def sum_over_cells(x, shards):
    if shards & (shards - 1):
        return lax.psum(x, "cell"), jnp.zeros_like(x)
    other, bit = jnp.zeros_like(x), 1
    while bit < shards:
        x = x + other
        other = lax.ppermute(x, "cell", [(i, i ^ bit) for i in range(shards)])
        bit *= 2
    return x, other


def coefficients(horiz, vertical, tilt_angle, azimuth):
    sin_t, cos_t = jnp.sin(tilt_angle), jnp.cos(tilt_angle)
    sin_p, cos_p = jnp.sin(azimuth), jnp.cos(azimuth)
    zero = jnp.zeros_like(horiz)
    return jnp.stack(
        [
            sin_t * cos_p,
            sin_t * sin_p,
            cos_t,
            cos_t * cos_p,
            cos_t * sin_p,
            -sin_t,
            -sin_t * sin_p,
            sin_t * cos_p,
            -horiz,
            -vertical,
            horiz - vertical,
        ]
        + [zero] * 5
    )


def scatter_over_cells(x, shards):
    if shards & (shards - 1):
        return lax.psum_scatter(x, "cell", scatter_dimension=0, tiled=False)
    me, bit = lax.axis_index("cell"), 1
    while bit < shards:
        x = x.reshape((x.shape[0] // 2, 2) + x.shape[1:])
        own = (me // bit) % 2
        kept, sent = (lax.dynamic_index_in_dim(x, k, axis=1, keepdims=False) for k in (own, 1 - own))
        x = kept + lax.ppermute(sent, "cell", [(i, i ^ bit) for i in range(shards)])
        bit *= 2
    return x[0]


def cell_parts(fields, shards):
    cell_dev = fields.shape[2] // shards
    if fields.size * fields.dtype.itemsize <= 16 * MIB:
        return (cell_dev - LANES, LANES)
    return (LANES,) * (cell_dev // LANES)


def transfer_and_solve(ready, fields, quads, tables, properties, kept, pool_rows, shards):
    comps, owned, cells = fields.shape
    cell_dev = cells // shards
    total = quads.shape[1]
    coef = coefficients(*properties)
    rank, slot, place = tables or (None, None, None)
    rows = quads * PAD if rank is None else table_rows(quads, place)
    pool = None
    if pool_rows:
        pool = scatter_over_cells(send_order(fields, slot, pool_rows, shards, 0, cell_dev), shards)
    rows = rows.reshape(-1)
    far, near, before = [], [], jnp.zeros((total // GROUP_ROWS, GROUP_ROWS // LANES, LANES), jnp.float32)

    def finish(received, first, before, last):
        width = received.shape[-1]
        here = last and width == LANES and total * 4 * LANES * 4 <= NEAR_BYTES
        for k in range(width // LANES):
            own = coef[:, first + k * LANES : first + (k + 1) * LANES]
            fill_steps, group_rows = (1, total) if here else (FILL_STEPS, GROUP_ROWS)
            before = before.reshape(total // group_rows, group_rows // LANES, LANES)
            block = first // LANES + k
            values, before = sens_block(
                rows, received, pool, k, block, own, before, here, fill_steps, group_rows
            )
            (near if here else far).append(values)
        return before

    first, received = 0, None
    for width in cell_parts(fields, shards):
        if ready is None:
            ready = send_order(fields, rank, kept, shards, first, width)
        if received is not None:
            ready, received, pool, rows, coef = lax.optimization_barrier((ready, received, pool, rows, coef))
        arriving = lax.all_to_all(ready, "cell", split_axis=0, concat_axis=0, tiled=True)
        if received is not None:
            before = finish(received, first - received.shape[-1], before, False)
        received, ready = arriving, None
        first += width
    before = finish(received, first - received.shape[-1], before, True)
    mine, theirs = sum_over_cells(before, shards)
    return scaled(mine, theirs, 1.0 / (4.0 * cell_dev * shards), far, near, SCALE_ROWS)


def local(fields, horiz, vertical, tilt_angle, azimuth, electrode_quads):
    shards = lax.axis_size("cell")
    owned = fields.shape[0]
    fields = fields.transpose(1, 0, 2)
    quads = electrode_quads.T
    properties = (horiz, vertical, tilt_angle, azimuth)
    if owned % LANES or owned > 2 * LANES:
        return transfer_and_solve(None, fields, quads, None, properties, owned, 0, shards)
    keeps = tuple(owned * part // 32 // ROW_TILE * ROW_TILE for part in KEEPS)
    pool = owned * POOL // 32 // ROW_TILE * ROW_TILE
    ready, tables, chosen = send_first(fields, quads, keeps, pool, shards, cell_parts(fields, shards)[0])

    def branch(k):
        if k == len(keeps):
            return lambda ready, tables, fields, quads, *properties: transfer_and_solve(
                None, fields, quads, None, properties, owned, 0, shards
            )
        return lambda ready, tables, fields, quads, *properties: transfer_and_solve(
            ready[k], fields, quads, tables, properties, keeps[k], 0 if k else pool, shards
        )

    branches = [branch(k) for k in range(len(keeps) + 1)]
    return lax.switch(chosen, branches, ready, tables, fields, quads, *properties)


def solution(mesh):
    placed = (
        P(("grp", "cell"), None, None),
        P(("grp", "cell")),
        P(("grp", "cell")),
        P(("grp", "cell")),
        P(("grp", "cell")),
        P("grp", None),
    )
    return jax.shard_map(
        local,
        mesh=mesh,
        in_specs=placed,
        out_specs=(P("grp", None, "cell"), P(("grp", "cell"))),
        check_vma=False,
    )
```

```python
import functools

import jax
import jax.numpy as jnp
from jax import lax
from jax.experimental import pallas as pl
from jax.experimental.pallas import tpu as pltpu
from jax.sharding import PartitionSpec as P

LANES = 128
SUBLANES = 8
UNROLL = 16
FILL_STEPS = 4
GROUP_ROWS = 512
SCALE_ROWS = 256
ROW_TILE = 8
KEEPS = (28, 30)
POOL = 5
PAD = 4
MIB = 1 << 20
VMEM_LIMIT = 60 * MIB
SENS_LIMIT = 32 * MIB
SCALE_LIMIT = 48 * MIB
NEAR_BYTES = 4 * MIB


def one_hots(quads_ref, column, high):
    index = quads_ref[pl.ds(column, 1), :]
    total = index.shape[1]
    upper = lax.broadcasted_iota(jnp.int32, (high, total), 0) == index // LANES
    lower = lax.broadcasted_iota(jnp.int32, (LANES, total), 0) == index % LANES
    return upper.astype(jnp.bfloat16), lower.astype(jnp.bfloat16)


def named_ranks(quads_ref, high, per, base):
    count = jnp.zeros((high, LANES), jnp.float32)
    for column in range(4):
        upper, lower = one_hots(quads_ref, column, high)
        count += lax.dot_general(upper, lower, (((1,), (1,)), ((), ())), preferred_element_type=jnp.float32)
    named = (count > 0).astype(jnp.bfloat16)

    def dot(a, b):
        return jnp.dot(a.astype(jnp.bfloat16), b.astype(jnp.bfloat16), preferred_element_type=jnp.float32)

    i, j = (lax.broadcasted_iota(jnp.int32, (LANES, LANES), d) for d in range(2))
    within = dot(named, i < j)
    lines = dot(named, jnp.ones((LANES, LANES), jnp.bfloat16))
    i, j = (lax.broadcasted_iota(jnp.int32, (high, high), d) for d in range(2))
    rank = jnp.where(count > 0, within + dot((j < i) & (j // per == i // per), lines), -1.0)
    over = jnp.maximum(dot(j // per == i // per, lines) - base, 0.0)
    ahead = dot((j // per < i // per) & (j % per == 0), over)
    slot = jnp.where(rank >= base, rank - base + ahead, -1.0)
    return rank, slot, ahead + over


def table_rows_kernel(quads_ref, place_ref, rows_ref):
    place = place_ref[...]
    coarse = jnp.floor(place * (1.0 / 16.0))
    fine = place - 16.0 * coarse
    for column in range(4):
        upper, lower = one_hots(quads_ref, column, place.shape[0])

        def pick(part):
            spread = lax.dot_general(
                part.astype(jnp.bfloat16), upper, (((0,), (0,)), ((), ())), preferred_element_type=jnp.float32
            )
            return jnp.sum(spread * lower.astype(jnp.float32), axis=0, keepdims=True)

        rows_ref[pl.ds(column, 1), :] = (pick(coarse) * 16.0 + pick(fine)).astype(jnp.int32) * PAD


def table_rows(quads, place):
    whole = pl.BlockSpec(memory_space=pltpu.VMEM)
    return pl.pallas_call(
        table_rows_kernel,
        in_specs=[whole, whole],
        out_specs=whole,
        out_shape=jax.ShapeDtypeStruct(quads.shape, jnp.int32),
        name="table_rows",
    )(quads, place)


def send_order_kernel(first, fields_ref, out_ref, held, in_sems, out_sems):
    shards, _, _, width = held.shape
    cell_dev = fields_ref.shape[2] // shards
    arrive = [
        pltpu.make_async_copy(fields_ref.at[:, :, pl.ds(d * cell_dev + first, width)], held.at[d], in_sems.at[d])
        for d in range(shards)
    ]
    leave = [pltpu.make_async_copy(held.at[d], out_ref.at[d], out_sems.at[d]) for d in range(shards)]
    for copy in arrive:
        copy.start()
    for d in range(shards):
        arrive[d].wait()
        leave[d].start()
    for copy in leave:
        copy.wait()


def choose_rows(choose, rank_ref):
    kept, owned = choose.shape
    me = lax.axis_index("cell")
    place = lax.broadcasted_iota(jnp.int32, (kept, LANES), 0).astype(jnp.float32)
    for k in range(owned // LANES):
        line = rank_ref[pl.ds(me * (owned // LANES) + k, 1), :]
        choose[:, k * LANES : (k + 1) * LANES] = (place == line).astype(choose.dtype)


def send_chosen(arrive, choose, held, packed, out_ref, out_sems):
    shards, comps = held.shape[:2]
    kept = packed.shape[2]

    def leave(d):
        return pltpu.make_async_copy(packed.at[d], out_ref.at[d], out_sems.at[d])

    @pl.loop(0, shards)
    def _(d):
        arrive(d).wait()
        for comp in range(comps):
            rows = jnp.dot(choose[pl.ds(0, kept), :], held[d, comp], preferred_element_type=jnp.float32)
            packed[d, comp] = rows.astype(packed.dtype)
        leave(d).start()

    @pl.loop(0, shards)
    def _(d):
        leave(d).wait()


def arrival(first, fields_ref, held, in_sems):
    shards, _, _, width = held.shape
    cell_dev = fields_ref.shape[2] // shards

    def arrive(d):
        lanes = pl.ds(pl.multiple_of(d * cell_dev + first, LANES), width)
        return pltpu.make_async_copy(fields_ref.at[:, :, lanes], held.at[d], in_sems.at[d])

    return arrive


def send_named_kernel(first, fields_ref, rank_ref, out_ref, held, packed, choose, in_sems, out_sems):
    arrive = arrival(first, fields_ref, held, in_sems)
    for d in range(held.shape[0]):
        arrive(d).start()
    choose_rows(choose, rank_ref)
    send_chosen(arrive, choose, held, packed, out_ref, out_sems)


def send_first_kernel(keeps, pool, fields_ref, quads_ref, *refs):
    out_refs, (rank_ref, slot_ref, place_ref, chosen_ref, held) = refs[: len(keeps)], refs[len(keeps) : len(keeps) + 5]
    packed, (choose, in_sems, out_sems) = refs[len(keeps) + 5 : -3], refs[-3:]
    arrive = arrival(0, fields_ref, held, in_sems)
    for d in range(held.shape[0]):
        arrive(d).start()
    shards, _, owned, _ = held.shape
    high, per = rank_ref.shape[0], owned // LANES
    rank, slot, taken = named_ranks(quads_ref, high, per, float(keeps[0]))
    rank_ref[...] = rank
    slot_ref[...] = slot
    most = (jnp.max(rank) + 1.0).astype(jnp.int32)
    pooled = (jnp.max(taken) <= pool).astype(jnp.int32)
    chosen = sum((most > kept).astype(jnp.int32) for kept in keeps[1:])
    chosen = (1 - pooled) * (1 + chosen)
    chosen_ref[0] = chosen
    owner = (lax.broadcasted_iota(jnp.int32, (high, LANES), 0) // per).astype(jnp.float32)
    place = jnp.where(slot < 0.0, owner * keeps[0] + rank, slot + shards * keeps[0])
    for k, kept in enumerate(keeps[1:]):
        place = jnp.where(chosen == k + 1, owner * kept + rank, place)
    place_ref[...] = place
    choose_rows(choose, rank_ref)
    for k, kept in enumerate(keeps):

        @pl.when(chosen == k)
        def _():
            send_chosen(arrive, choose, held, packed[k], out_refs[k], out_sems)

    @pl.when(chosen == len(keeps))
    def _():
        for d in range(held.shape[0]):
            arrive(d).wait()


def send_first(fields, quads, keeps, pool, shards, width):
    comps, owned, cells = fields.shape
    sent = [(shards, comps, kept, width) for kept in keeps]
    anywhere, whole = pl.BlockSpec(memory_space=pl.ANY), pl.BlockSpec(memory_space=pltpu.VMEM)
    table = jax.ShapeDtypeStruct((shards * owned // LANES, LANES), jnp.float32)
    *ready, rank, slot, place, chosen = pl.pallas_call(
        functools.partial(send_first_kernel, keeps, pool),
        in_specs=[anywhere, whole],
        out_specs=[anywhere] * len(keeps) + [whole] * 3 + [pl.BlockSpec(memory_space=pltpu.SMEM)],
        out_shape=[jax.ShapeDtypeStruct(shape, fields.dtype) for shape in sent]
        + [table] * 3
        + [jax.ShapeDtypeStruct((1,), jnp.int32)],
        scratch_shapes=[pltpu.VMEM((shards, comps, owned, width), fields.dtype)]
        + [pltpu.VMEM(shape, fields.dtype) for shape in sent]
        + [
            pltpu.VMEM((max(keeps), owned), fields.dtype),
            pltpu.SemaphoreType.DMA((shards,)),
            pltpu.SemaphoreType.DMA((shards,)),
        ],
        compiler_params=pltpu.CompilerParams(vmem_limit_bytes=VMEM_LIMIT),
        name="send_first",
    )(fields, quads)
    return ready, (rank, slot, place), chosen[0]


def send_order(fields, rank, kept, shards, first, width):
    comps, owned, cells = fields.shape
    held = (shards, comps, owned, width)
    sent = (shards, comps, kept, width)
    scratch = [pltpu.VMEM(held, fields.dtype)]
    in_specs, args = [pl.BlockSpec(memory_space=pl.ANY)], [fields]
    if rank is not None:
        scratch += [pltpu.VMEM(sent, fields.dtype), pltpu.VMEM((kept, owned), fields.dtype)]
        in_specs.append(pl.BlockSpec(memory_space=pltpu.VMEM))
        args.append(rank)
    return pl.pallas_call(
        functools.partial(send_order_kernel if rank is None else send_named_kernel, first),
        in_specs=in_specs,
        out_specs=pl.BlockSpec(memory_space=pl.ANY),
        out_shape=jax.ShapeDtypeStruct(sent, fields.dtype),
        scratch_shapes=scratch + [pltpu.SemaphoreType.DMA((shards,)), pltpu.SemaphoreType.DMA((shards,))],
        cost_estimate=pl.CostEstimate(flops=0, bytes_accessed=4 * comps * owned * width * shards, transcendentals=0),
        compiler_params=pltpu.CompilerParams(vmem_limit_bytes=VMEM_LIMIT),
        name="send_order",
    )(*args)


def sens_kernel(sources, fill_steps, group_rows, near, all_rows_ref, fields_ref, coef_ref, before_ref, *refs):
    sens_ref, sumsq_ref, table, picked, squares, rows_ref, rows_sem = refs[-7:]
    step = pl.program_id(0)
    rows_copy = pltpu.make_async_copy(all_rows_ref, rows_ref, rows_sem)

    @pl.when(step == 0)
    def _():
        rows_copy.start()

    @pl.when(step == fill_steps)
    def _():
        rows_copy.wait()
        if len(refs) > 7:
            pool_ref = refs[0]
            pool = pool_ref.shape[1]
            for comp in range(pool_ref.shape[0]):
                values = pool_ref[comp].astype(jnp.float32)
                table[pl.ds(table.shape[0] - pool * PAD + comp, pool, stride=PAD), :] = values

    owned = fields_ref.shape[2]
    batch_rows = SUBLANES * UNROLL
    total_rows = rows_ref.shape[0] // 4

    @pl.when(step < fill_steps)
    def _():
        for source in range(sources):
            place = step * sources + source
            for comp in range(fields_ref.shape[1]):
                values = fields_ref[place if near else source, comp].astype(jnp.float32)
                table[pl.ds(place * (owned * PAD) + comp, owned, stride=PAD), :] = values

    @pl.when(step >= fill_steps)
    def _():
        first = (step - fill_steps) * group_rows
        coef = [coef_ref[pl.ds(k, 1), :] for k in range(11)]
        ax, ay, az, tx, ty, tz, ux, uy, nh, nv, nc = coef

        def fetch(index):
            return table[pl.ds(pl.multiple_of(rows_ref[index], PAD), PAD), :]

        def close(batch):
            turned = squares[pl.ds(pl.multiple_of(batch * batch_rows, batch_rows), batch_rows), :].T
            total = jnp.sum(turned, axis=0, keepdims=True)
            sumsq_ref[0, pl.ds(batch, 1), :] = total + before_ref[0, pl.ds(batch, 1), :]

        squares[pl.ds(0, batch_rows), :] = jnp.zeros((batch_rows, LANES), jnp.float32)

        @pl.loop(0, group_rows // batch_rows)
        def _(batch):
            close(jnp.maximum(batch - 1, 0))
            base = first + batch * batch_rows
            for j in range(batch_rows):
                i = base + j
                picked[pl.ds(j * PAD, PAD), :] = fetch(i) - fetch(total_rows + i)
                picked[pl.ds((batch_rows + j) * PAD, PAD), :] = fetch(2 * total_rows + i) - fetch(3 * total_rows + i)
            for g in range(UNROLL):
                start = g * SUBLANES
                sx, sy, sz = (picked[pl.ds(start * PAD + k, SUBLANES, stride=PAD), :] for k in range(3))
                rx, ry, rz = (picked[pl.ds((batch_rows + start) * PAD + k, SUBLANES, stride=PAD), :] for k in range(3))
                sn = sx * ax + sy * ay + sz * az
                rn = rx * ax + ry * ay + rz * az
                st = sx * tx + sy * ty + sz * tz
                rt = rx * tx + ry * ty + rz * tz
                sp = sx * ux + sy * uy
                rp = rx * ux + ry * uy
                dot = sx * rx + sy * ry + sz * rz
                both = sn * rn
                values = (nh * (dot - both), nv * both, nc * (st * rn + sn * rt), nc * (sp * rn + sn * rp))
                place = ((base if near else batch * batch_rows) + start) * 4
                for k in range(4):
                    sens_ref[pl.ds(place + k, SUBLANES, stride=4), :] = values[k]
                squares[pl.ds(batch * batch_rows + start, SUBLANES), :] = (
                    values[0] * values[0] + values[1] * values[1] + values[2] * values[2] + values[3] * values[3]
                )

        close(group_rows // batch_rows - 1)


def sens_block(rows, fields, pool, lane_block, cell_block, coef, before, near, fill_steps, group_rows):
    shards, comps, owned, _ = fields.shape
    total = rows.size // 4
    groups = total // group_rows
    if near:
        fields_spec = sens_spec = pl.BlockSpec(memory_space=pltpu.VMEM)
        sens_shape = pltpu.VMEM((total * 4, LANES), jnp.float32)
    else:
        sens_spec = pl.BlockSpec((group_rows * 4, LANES), lambda i: (jnp.maximum(i - fill_steps, 0), 0))
        sens_shape = pltpu.HBM((total * 4, LANES), jnp.float32)
        fields_spec = pl.BlockSpec(
            (shards // fill_steps, comps, owned, LANES), lambda i: (jnp.minimum(i, fill_steps - 1), 0, 0, lane_block)
        )
    sums = pl.BlockSpec((1, group_rows // LANES, LANES), lambda i: (jnp.maximum(i - fill_steps, 0), 0, 0))
    pools = [] if pool is None else [pool]
    pool_rows = sum(p.shape[1] for p in pools)
    return pl.pallas_call(
        functools.partial(sens_kernel, shards // fill_steps, fill_steps, group_rows, near),
        grid=(fill_steps + groups,),
        in_specs=[
            pl.BlockSpec(memory_space=pl.ANY),
            fields_spec,
            pl.BlockSpec((16, LANES), lambda i: (0, 0)),
            sums,
        ]
        + [pl.BlockSpec((comps, pool_rows, LANES), lambda i: (0, 0, cell_block)) for _ in pools],
        out_specs=[sens_spec, sums],
        out_shape=[
            sens_shape,
            jax.ShapeDtypeStruct((groups, group_rows // LANES, LANES), jnp.float32),
        ],
        scratch_shapes=[
            pltpu.VMEM(((shards * owned + pool_rows) * PAD, LANES), jnp.float32),
            pltpu.VMEM((2 * UNROLL * SUBLANES * PAD, LANES), jnp.float32),
            pltpu.VMEM((group_rows, LANES), jnp.float32),
            pltpu.SMEM(rows.shape, jnp.int32),
            pltpu.SemaphoreType.DMA,
        ],
        cost_estimate=pl.CostEstimate(
            flops=total * LANES * 64,
            bytes_accessed=(shards * comps * owned * LANES * 2 + total * 5 * LANES * 4) * 4,
            transcendentals=0,
        ),
        compiler_params=pltpu.CompilerParams(vmem_limit_bytes=SENS_LIMIT),
        name="sens_block",
    )(rows, fields, coef, before, *pools)


def scale_kernel(inverse, far, mine_ref, theirs_ref, *refs):
    sens_refs, (out_ref, cover_ref, held, ready, spread, cover, in_sems, out_sems) = refs[:-8], refs[-8:]
    far_refs, near_refs = sens_refs[:far], sens_refs[far:]
    rows = spread.shape[0]
    step_rows = rows // 4
    steps = ready.shape[0] // step_rows

    def arrive(step, b):
        part = pl.ds(pl.multiple_of(step * rows, rows), rows)
        return pltpu.make_async_copy(far_refs[b].at[part], held.at[b, part], in_sems.at[step, b])

    def leave(step):
        part = pl.ds(pl.multiple_of(step * step_rows, step_rows), step_rows)
        return pltpu.make_async_copy(ready.at[part], out_ref.at[part], out_sems.at[step])

    for step in range(steps):
        for b in range(far):
            arrive(step, b).start()
    cover[...] = jnp.zeros_like(cover)

    @pl.loop(0, steps)
    def _(step):
        for k in range(step_rows // LANES):
            line = pl.ds(step * (step_rows // LANES) + k, 1)
            meansq = (mine_ref[line, :] + theirs_ref[line, :]) * inverse
            column = jnp.broadcast_to(lax.rsqrt(meansq + 1e-06), (LANES, LANES)).T
            for p in range(4):
                spread[pl.ds(k * 4 * LANES + p, LANES, stride=4), :] = column
        part = pl.ds(pl.multiple_of(step * rows, rows), rows)

        def write(b, values):
            normed = values * spread[...]
            place = pl.ds(pl.multiple_of(step * step_rows, step_rows), step_rows)
            lanes = slice(b * LANES, (b + 1) * LANES)
            ready[place, :, lanes] = normed.astype(ready.dtype).reshape(step_rows, 4, LANES)
            squares = (normed * normed).reshape(rows // SUBLANES, SUBLANES, LANES)
            cover[pl.ds(b * SUBLANES, SUBLANES), :] += jnp.sum(squares, axis=0)

        for b, ref in enumerate(near_refs):
            write(far + b, ref[part, :])
        for b in range(far):
            arrive(step, b).wait()
            write(b, held[b, part, :])
        leave(step).start()

    for b in range(len(sens_refs)):
        cover_ref[pl.ds(b, 1), :] = jnp.sum(cover[pl.ds(b * SUBLANES, SUBLANES), :], axis=0, keepdims=True)
    for step in range(steps):
        leave(step).wait()


def scaled(mine, theirs, inverse, far, near, step_rows):
    columns, total = len(far) + len(near), (far + near)[0].shape[0] // 4
    steps = total // step_rows
    near = [pltpu.with_memory_space_constraint(s, pltpu.VMEM) for s in near]
    whole = pl.BlockSpec(memory_space=pltpu.VMEM)
    out, cover = pl.pallas_call(
        functools.partial(scale_kernel, inverse, len(far)),
        in_specs=[whole, whole] + [pl.BlockSpec(memory_space=pltpu.HBM)] * len(far) + [whole] * len(near),
        out_specs=[pl.BlockSpec(memory_space=pltpu.HBM), whole],
        out_shape=[
            jax.ShapeDtypeStruct((total, 4, columns * LANES), jnp.bfloat16),
            jax.ShapeDtypeStruct((columns, LANES), jnp.float32),
        ],
        scratch_shapes=[
            pltpu.VMEM((len(far), total * 4, LANES), jnp.float32),
            pltpu.VMEM((total, 4, columns * LANES), jnp.bfloat16),
            pltpu.VMEM((step_rows * 4, LANES), jnp.float32),
            pltpu.VMEM((columns * SUBLANES, LANES), jnp.float32),
            pltpu.SemaphoreType.DMA((steps, len(far))),
            pltpu.SemaphoreType.DMA((steps,)),
        ],
        compiler_params=pltpu.CompilerParams(vmem_limit_bytes=SCALE_LIMIT),
        name="scaled",
    )(mine.reshape(-1, LANES), theirs.reshape(-1, LANES), *far, *near)
    return out, cover.reshape(columns * LANES)


def sum_over_cells(x, shards):
    if shards & (shards - 1):
        return lax.psum(x, "cell"), jnp.zeros_like(x)
    other, unit = jnp.zeros_like(x), 1
    while unit < shards:
        x = x + other
        size = 4 if unit in (4,) and unit * 4 <= shards else 2
        other = sum(lax.ppermute(x, "cell", [(i, i ^ (k * unit)) for i in range(shards)]) for k in range(1, size))
        unit *= size
    return x, other


def coefficients(horiz, vertical, tilt_angle, azimuth):
    sin_t, cos_t = jnp.sin(tilt_angle), jnp.cos(tilt_angle)
    sin_p, cos_p = jnp.sin(azimuth), jnp.cos(azimuth)
    zero = jnp.zeros_like(horiz)
    return jnp.stack(
        [
            sin_t * cos_p,
            sin_t * sin_p,
            cos_t,
            cos_t * cos_p,
            cos_t * sin_p,
            -sin_t,
            -sin_t * sin_p,
            sin_t * cos_p,
            -horiz,
            -vertical,
            horiz - vertical,
        ]
        + [zero] * 5
    )


def scatter_over_cells(x, shards):
    if shards & (shards - 1):
        return lax.psum_scatter(x, "cell", scatter_dimension=0, tiled=False)
    me, bit = lax.axis_index("cell"), 1
    while bit < shards:
        x = x.reshape((x.shape[0] // 2, 2) + x.shape[1:])
        own = (me // bit) % 2
        kept, sent = (lax.dynamic_index_in_dim(x, k, axis=1, keepdims=False) for k in (own, 1 - own))
        x = kept + lax.ppermute(sent, "cell", [(i, i ^ bit) for i in range(shards)])
        bit *= 2
    return x[0]


def cell_parts(fields, shards):
    cell_dev = fields.shape[2] // shards
    if fields.size * fields.dtype.itemsize <= 16 * MIB:
        return (cell_dev - LANES, LANES)
    return (LANES,) * (cell_dev // LANES)


def transfer_and_solve(ready, fields, quads, tables, properties, kept, pool_rows, shards):
    comps, owned, cells = fields.shape
    cell_dev = cells // shards
    total = quads.shape[1]
    coef = coefficients(*properties)
    rank, slot, place = tables or (None, None, None)
    rows = quads * PAD if rank is None else table_rows(quads, place)
    pool = None
    if pool_rows:
        pool = scatter_over_cells(send_order(fields, slot, pool_rows, shards, 0, cell_dev), shards)
    rows = rows.reshape(-1)
    far, near, before = [], [], jnp.zeros((total // GROUP_ROWS, GROUP_ROWS // LANES, LANES), jnp.float32)

    def finish(received, first, before, last):
        width = received.shape[-1]
        here = last and width == LANES and total * 4 * LANES * 4 <= NEAR_BYTES
        for k in range(width // LANES):
            own = coef[:, first + k * LANES : first + (k + 1) * LANES]
            fill_steps, group_rows = (1, total) if here else (FILL_STEPS, GROUP_ROWS)
            before = before.reshape(total // group_rows, group_rows // LANES, LANES)
            block = first // LANES + k
            values, before = sens_block(
                rows, received, pool, k, block, own, before, here, fill_steps, group_rows
            )
            (near if here else far).append(values)
        return before

    first, received = 0, None
    for width in cell_parts(fields, shards):
        if ready is None:
            ready = send_order(fields, rank, kept, shards, first, width)
        if received is not None:
            ready, received, pool, rows, coef = lax.optimization_barrier((ready, received, pool, rows, coef))
        arriving = lax.all_to_all(ready, "cell", split_axis=0, concat_axis=0, tiled=True)
        if received is not None:
            before = finish(received, first - received.shape[-1], before, False)
        received, ready = arriving, None
        first += width
    before = finish(received, first - received.shape[-1], before, True)
    mine, theirs = sum_over_cells(before, shards)
    return scaled(mine, theirs, 1.0 / (4.0 * cell_dev * shards), far, near, SCALE_ROWS)


def local(fields, horiz, vertical, tilt_angle, azimuth, electrode_quads):
    shards = lax.axis_size("cell")
    owned = fields.shape[0]
    fields = fields.transpose(1, 0, 2)
    quads = electrode_quads.T
    properties = (horiz, vertical, tilt_angle, azimuth)
    if owned % LANES or owned > 2 * LANES:
        return transfer_and_solve(None, fields, quads, None, properties, owned, 0, shards)
    keeps = tuple(owned * part // 32 // ROW_TILE * ROW_TILE for part in KEEPS)
    pool = owned * POOL // 32 // ROW_TILE * ROW_TILE
    ready, tables, chosen = send_first(fields, quads, keeps, pool, shards, cell_parts(fields, shards)[0])

    def branch(k):
        if k == len(keeps):
            return lambda ready, tables, fields, quads, *properties: transfer_and_solve(
                None, fields, quads, None, properties, owned, 0, shards
            )
        return lambda ready, tables, fields, quads, *properties: transfer_and_solve(
            ready[k], fields, quads, tables, properties, keeps[k], 0 if k else pool, shards
        )

    branches = [branch(k) for k in range(len(keeps) + 1)]
    return lax.switch(chosen, branches, ready, tables, fields, quads, *properties)


def solution(mesh):
    placed = (
        P(("grp", "cell"), None, None),
        P(("grp", "cell")),
        P(("grp", "cell")),
        P(("grp", "cell")),
        P(("grp", "cell")),
        P("grp", None),
    )
    return jax.shard_map(
        local,
        mesh=mesh,
        in_specs=placed,
        out_specs=(P("grp", None, "cell"), P(("grp", "cell"))),
        check_vma=False,
    )
```

```python
import functools

import jax
import jax.numpy as jnp
from jax import lax
from jax.experimental import pallas as pl
from jax.experimental.pallas import tpu as pltpu
from jax.sharding import PartitionSpec as P

LANES = 128
SUBLANES = 8
UNROLL = 16
FILL_STEPS = 4
GROUP_ROWS = 512
SCALE_ROWS = 256
ROW_TILE = 16
KEEPS = (28, 30)
POOL = 6
PAD = 4
MIB = 1 << 20
VMEM_LIMIT = 60 * MIB
SENS_LIMIT = 32 * MIB
SCALE_LIMIT = 48 * MIB
NEAR_BYTES = 4 * MIB


def one_hots(quads_ref, column, high):
    index = quads_ref[pl.ds(column, 1), :]
    total = index.shape[1]
    upper = lax.broadcasted_iota(jnp.int32, (high, total), 0) == index // LANES
    lower = lax.broadcasted_iota(jnp.int32, (LANES, total), 0) == index % LANES
    return upper.astype(jnp.bfloat16), lower.astype(jnp.bfloat16)


def named_ranks(quads_ref, high, per, base):
    count = jnp.zeros((high, LANES), jnp.float32)
    for column in range(4):
        upper, lower = one_hots(quads_ref, column, high)
        count += lax.dot_general(upper, lower, (((1,), (1,)), ((), ())), preferred_element_type=jnp.float32)
    named = (count > 0).astype(jnp.bfloat16)

    def dot(a, b):
        return jnp.dot(a.astype(jnp.bfloat16), b.astype(jnp.bfloat16), preferred_element_type=jnp.float32)

    i, j = (lax.broadcasted_iota(jnp.int32, (LANES, LANES), d) for d in range(2))
    within = dot(named, i < j)
    lines = dot(named, jnp.ones((LANES, LANES), jnp.bfloat16))
    i, j = (lax.broadcasted_iota(jnp.int32, (high, high), d) for d in range(2))
    rank = jnp.where(count > 0, within + dot((j < i) & (j // per == i // per), lines), -1.0)
    over = jnp.maximum(dot(j // per == i // per, lines) - base, 0.0)
    ahead = dot((j // per < i // per) & (j % per == 0), over)
    slot = jnp.where(rank >= base, rank - base + ahead, -1.0)
    return rank, slot, ahead + over


def table_rows_kernel(quads_ref, place_ref, rows_ref):
    place = place_ref[...]
    coarse = jnp.floor(place * (1.0 / 16.0))
    fine = place - 16.0 * coarse
    for column in range(4):
        upper, lower = one_hots(quads_ref, column, place.shape[0])

        def pick(part):
            spread = lax.dot_general(
                part.astype(jnp.bfloat16), upper, (((0,), (0,)), ((), ())), preferred_element_type=jnp.float32
            )
            return jnp.sum(spread * lower.astype(jnp.float32), axis=0, keepdims=True)

        rows_ref[pl.ds(column, 1), :] = (pick(coarse) * 16.0 + pick(fine)).astype(jnp.int32) * PAD


def table_rows(quads, place):
    whole = pl.BlockSpec(memory_space=pltpu.VMEM)
    return pl.pallas_call(
        table_rows_kernel,
        in_specs=[whole, whole],
        out_specs=whole,
        out_shape=jax.ShapeDtypeStruct(quads.shape, jnp.int32),
        name="table_rows",
    )(quads, place)


def send_order_kernel(first, fields_ref, out_ref, held, in_sems, out_sems):
    shards, _, _, width = held.shape
    cell_dev = fields_ref.shape[2] // shards
    arrive = [
        pltpu.make_async_copy(fields_ref.at[:, :, pl.ds(d * cell_dev + first, width)], held.at[d], in_sems.at[d])
        for d in range(shards)
    ]
    leave = [pltpu.make_async_copy(held.at[d], out_ref.at[d], out_sems.at[d]) for d in range(shards)]
    for copy in arrive:
        copy.start()
    for d in range(shards):
        arrive[d].wait()
        leave[d].start()
    for copy in leave:
        copy.wait()


def choose_rows(choose, rank_ref):
    kept, owned = choose.shape
    me = lax.axis_index("cell")
    place = lax.broadcasted_iota(jnp.int32, (kept, LANES), 0).astype(jnp.float32)
    for k in range(owned // LANES):
        line = rank_ref[pl.ds(me * (owned // LANES) + k, 1), :]
        choose[:, k * LANES : (k + 1) * LANES] = (place == line).astype(choose.dtype)


def send_chosen(arrive, choose, held, packed, out_ref, out_sems):
    shards, comps = held.shape[:2]
    kept = packed.shape[2]

    def leave(d):
        return pltpu.make_async_copy(packed.at[d], out_ref.at[d], out_sems.at[d])

    @pl.loop(0, shards)
    def _(d):
        arrive(d).wait()
        for comp in range(comps):
            rows = jnp.dot(choose[pl.ds(0, kept), :], held[d, comp], preferred_element_type=jnp.float32)
            packed[d, comp] = rows.astype(packed.dtype)
        leave(d).start()

    @pl.loop(0, shards)
    def _(d):
        leave(d).wait()


def arrival(first, fields_ref, held, in_sems):
    shards, _, _, width = held.shape
    cell_dev = fields_ref.shape[2] // shards

    def arrive(d):
        lanes = pl.ds(pl.multiple_of(d * cell_dev + first, LANES), width)
        return pltpu.make_async_copy(fields_ref.at[:, :, lanes], held.at[d], in_sems.at[d])

    return arrive


def send_named_kernel(first, fields_ref, rank_ref, out_ref, held, packed, choose, in_sems, out_sems):
    arrive = arrival(first, fields_ref, held, in_sems)
    for d in range(held.shape[0]):
        arrive(d).start()
    choose_rows(choose, rank_ref)
    send_chosen(arrive, choose, held, packed, out_ref, out_sems)


def send_first_kernel(keeps, pool, fields_ref, quads_ref, *refs):
    out_refs, (rank_ref, slot_ref, place_ref, chosen_ref, held) = refs[: len(keeps)], refs[len(keeps) : len(keeps) + 5]
    packed, (choose, in_sems, out_sems) = refs[len(keeps) + 5 : -3], refs[-3:]
    arrive = arrival(0, fields_ref, held, in_sems)
    for d in range(held.shape[0]):
        arrive(d).start()
    shards, _, owned, _ = held.shape
    high, per = rank_ref.shape[0], owned // LANES
    rank, slot, taken = named_ranks(quads_ref, high, per, float(keeps[0]))
    rank_ref[...] = rank
    slot_ref[...] = slot
    most = (jnp.max(rank) + 1.0).astype(jnp.int32)
    pooled = (jnp.max(taken) <= pool).astype(jnp.int32)
    chosen = sum((most > kept).astype(jnp.int32) for kept in keeps[1:])
    chosen = (1 - pooled) * (1 + chosen)
    chosen_ref[0] = chosen
    owner = (lax.broadcasted_iota(jnp.int32, (high, LANES), 0) // per).astype(jnp.float32)
    place = jnp.where(slot < 0.0, owner * keeps[0] + rank, slot + shards * keeps[0])
    for k, kept in enumerate(keeps[1:]):
        place = jnp.where(chosen == k + 1, owner * kept + rank, place)
    place_ref[...] = place
    choose_rows(choose, rank_ref)
    for k, kept in enumerate(keeps):

        @pl.when(chosen == k)
        def _():
            send_chosen(arrive, choose, held, packed[k], out_refs[k], out_sems)

    @pl.when(chosen == len(keeps))
    def _():
        for d in range(held.shape[0]):
            arrive(d).wait()


def send_first(fields, quads, keeps, pool, shards, width):
    comps, owned, cells = fields.shape
    sent = [(shards, comps, kept, width) for kept in keeps]
    anywhere, whole = pl.BlockSpec(memory_space=pl.ANY), pl.BlockSpec(memory_space=pltpu.VMEM)
    table = jax.ShapeDtypeStruct((shards * owned // LANES, LANES), jnp.float32)
    *ready, rank, slot, place, chosen = pl.pallas_call(
        functools.partial(send_first_kernel, keeps, pool),
        in_specs=[anywhere, whole],
        out_specs=[anywhere] * len(keeps) + [whole] * 3 + [pl.BlockSpec(memory_space=pltpu.SMEM)],
        out_shape=[jax.ShapeDtypeStruct(shape, fields.dtype) for shape in sent]
        + [table] * 3
        + [jax.ShapeDtypeStruct((1,), jnp.int32)],
        scratch_shapes=[pltpu.VMEM((shards, comps, owned, width), fields.dtype)]
        + [pltpu.VMEM(shape, fields.dtype) for shape in sent]
        + [
            pltpu.VMEM((max(keeps), owned), fields.dtype),
            pltpu.SemaphoreType.DMA((shards,)),
            pltpu.SemaphoreType.DMA((shards,)),
        ],
        compiler_params=pltpu.CompilerParams(vmem_limit_bytes=VMEM_LIMIT),
        name="send_first",
    )(fields, quads)
    return ready, (rank, slot, place), chosen[0]


def send_order(fields, rank, kept, shards, first, width):
    comps, owned, cells = fields.shape
    held = (shards, comps, owned, width)
    sent = (shards, comps, kept, width)
    scratch = [pltpu.VMEM(held, fields.dtype)]
    in_specs, args = [pl.BlockSpec(memory_space=pl.ANY)], [fields]
    if rank is not None:
        scratch += [pltpu.VMEM(sent, fields.dtype), pltpu.VMEM((kept, owned), fields.dtype)]
        in_specs.append(pl.BlockSpec(memory_space=pltpu.VMEM))
        args.append(rank)
    return pl.pallas_call(
        functools.partial(send_order_kernel if rank is None else send_named_kernel, first),
        in_specs=in_specs,
        out_specs=pl.BlockSpec(memory_space=pl.ANY),
        out_shape=jax.ShapeDtypeStruct(sent, fields.dtype),
        scratch_shapes=scratch + [pltpu.SemaphoreType.DMA((shards,)), pltpu.SemaphoreType.DMA((shards,))],
        cost_estimate=pl.CostEstimate(flops=0, bytes_accessed=4 * comps * owned * width * shards, transcendentals=0),
        compiler_params=pltpu.CompilerParams(vmem_limit_bytes=VMEM_LIMIT),
        name="send_order",
    )(*args)


def sens_kernel(sources, fill_steps, group_rows, near, all_rows_ref, fields_ref, coef_ref, before_ref, *refs):
    sens_ref, sumsq_ref, table, picked, squares, rows_ref, rows_sem = refs[-7:]
    step = pl.program_id(0)
    rows_copy = pltpu.make_async_copy(all_rows_ref, rows_ref, rows_sem)

    @pl.when(step == 0)
    def _():
        rows_copy.start()

    @pl.when(step == fill_steps)
    def _():
        rows_copy.wait()
        if len(refs) > 7:
            pool_ref = refs[0]
            pool = pool_ref.shape[1]
            for comp in range(pool_ref.shape[0]):
                values = pool_ref[comp].astype(jnp.float32)
                table[pl.ds(table.shape[0] - pool * PAD + comp, pool, stride=PAD), :] = values

    owned = fields_ref.shape[2]
    batch_rows = SUBLANES * UNROLL
    total_rows = rows_ref.shape[0] // 4

    @pl.when(step < fill_steps)
    def _():
        for source in range(sources):
            place = step * sources + source
            for comp in range(fields_ref.shape[1]):
                values = fields_ref[place if near else source, comp].astype(jnp.float32)
                table[pl.ds(place * (owned * PAD) + comp, owned, stride=PAD), :] = values

    @pl.when(step >= fill_steps)
    def _():
        first = (step - fill_steps) * group_rows
        coef = [coef_ref[pl.ds(k, 1), :] for k in range(11)]
        ax, ay, az, tx, ty, tz, ux, uy, nh, nv, nc = coef

        def fetch(index):
            return table[pl.ds(pl.multiple_of(rows_ref[index], PAD), PAD), :]

        def close(batch):
            turned = squares[pl.ds(pl.multiple_of(batch * batch_rows, batch_rows), batch_rows), :].T
            total = jnp.sum(turned, axis=0, keepdims=True)
            sumsq_ref[0, pl.ds(batch, 1), :] = total + before_ref[0, pl.ds(batch, 1), :]

        squares[pl.ds(0, batch_rows), :] = jnp.zeros((batch_rows, LANES), jnp.float32)

        @pl.loop(0, group_rows // batch_rows)
        def _(batch):
            close(jnp.maximum(batch - 1, 0))
            base = first + batch * batch_rows
            for j in range(batch_rows):
                i = base + j
                picked[pl.ds(j * PAD, PAD), :] = fetch(i) - fetch(total_rows + i)
                picked[pl.ds((batch_rows + j) * PAD, PAD), :] = fetch(2 * total_rows + i) - fetch(3 * total_rows + i)
            for g in range(UNROLL):
                start = g * SUBLANES
                sx, sy, sz = (picked[pl.ds(start * PAD + k, SUBLANES, stride=PAD), :] for k in range(3))
                rx, ry, rz = (picked[pl.ds((batch_rows + start) * PAD + k, SUBLANES, stride=PAD), :] for k in range(3))
                sn = sx * ax + sy * ay + sz * az
                rn = rx * ax + ry * ay + rz * az
                st = sx * tx + sy * ty + sz * tz
                rt = rx * tx + ry * ty + rz * tz
                sp = sx * ux + sy * uy
                rp = rx * ux + ry * uy
                dot = sx * rx + sy * ry + sz * rz
                both = sn * rn
                values = (nh * (dot - both), nv * both, nc * (st * rn + sn * rt), nc * (sp * rn + sn * rp))
                place = ((base if near else batch * batch_rows) + start) * 4
                for k in range(4):
                    sens_ref[pl.ds(place + k, SUBLANES, stride=4), :] = values[k]
                squares[pl.ds(batch * batch_rows + start, SUBLANES), :] = (
                    values[0] * values[0] + values[1] * values[1] + values[2] * values[2] + values[3] * values[3]
                )

        close(group_rows // batch_rows - 1)


def sens_block(rows, fields, pool, lane_block, cell_block, coef, before, near, fill_steps, group_rows):
    shards, comps, owned, _ = fields.shape
    total = rows.size // 4
    groups = total // group_rows
    if near:
        fields_spec = sens_spec = pl.BlockSpec(memory_space=pltpu.VMEM)
        sens_shape = pltpu.VMEM((total * 4, LANES), jnp.float32)
    else:
        sens_spec = pl.BlockSpec((group_rows * 4, LANES), lambda i: (jnp.maximum(i - fill_steps, 0), 0))
        sens_shape = pltpu.HBM((total * 4, LANES), jnp.float32)
        fields_spec = pl.BlockSpec(
            (shards // fill_steps, comps, owned, LANES), lambda i: (jnp.minimum(i, fill_steps - 1), 0, 0, lane_block)
        )
    sums = pl.BlockSpec((1, group_rows // LANES, LANES), lambda i: (jnp.maximum(i - fill_steps, 0), 0, 0))
    pools = [] if pool is None else [pool]
    pool_rows = sum(p.shape[1] for p in pools)
    return pl.pallas_call(
        functools.partial(sens_kernel, shards // fill_steps, fill_steps, group_rows, near),
        grid=(fill_steps + groups,),
        in_specs=[
            pl.BlockSpec(memory_space=pl.ANY),
            fields_spec,
            pl.BlockSpec((16, LANES), lambda i: (0, 0)),
            sums,
        ]
        + [pl.BlockSpec((comps, pool_rows, LANES), lambda i: (0, 0, cell_block)) for _ in pools],
        out_specs=[sens_spec, sums],
        out_shape=[
            sens_shape,
            jax.ShapeDtypeStruct((groups, group_rows // LANES, LANES), jnp.float32),
        ],
        scratch_shapes=[
            pltpu.VMEM(((shards * owned + pool_rows) * PAD, LANES), jnp.float32),
            pltpu.VMEM((2 * UNROLL * SUBLANES * PAD, LANES), jnp.float32),
            pltpu.VMEM((group_rows, LANES), jnp.float32),
            pltpu.SMEM(rows.shape, jnp.int32),
            pltpu.SemaphoreType.DMA,
        ],
        cost_estimate=pl.CostEstimate(
            flops=total * LANES * 64,
            bytes_accessed=(shards * comps * owned * LANES * 2 + total * 5 * LANES * 4) * 4,
            transcendentals=0,
        ),
        compiler_params=pltpu.CompilerParams(vmem_limit_bytes=SENS_LIMIT),
        name="sens_block",
    )(rows, fields, coef, before, *pools)


def scale_kernel(inverse, far, mine_ref, theirs_ref, *refs):
    sens_refs, (out_ref, cover_ref, held, ready, spread, cover, in_sems, out_sems) = refs[:-8], refs[-8:]
    far_refs, near_refs = sens_refs[:far], sens_refs[far:]
    rows = spread.shape[0]
    step_rows = rows // 4
    steps = ready.shape[0] // step_rows

    def arrive(step, b):
        part = pl.ds(pl.multiple_of(step * rows, rows), rows)
        return pltpu.make_async_copy(far_refs[b].at[part], held.at[b, part], in_sems.at[step, b])

    def leave(step):
        part = pl.ds(pl.multiple_of(step * step_rows, step_rows), step_rows)
        return pltpu.make_async_copy(ready.at[part], out_ref.at[part], out_sems.at[step])

    for step in range(steps):
        for b in range(far):
            arrive(step, b).start()
    cover[...] = jnp.zeros_like(cover)

    @pl.loop(0, steps)
    def _(step):
        for k in range(step_rows // LANES):
            line = pl.ds(step * (step_rows // LANES) + k, 1)
            meansq = (mine_ref[line, :] + theirs_ref[line, :]) * inverse
            column = jnp.broadcast_to(lax.rsqrt(meansq + 1e-06), (LANES, LANES)).T
            for p in range(4):
                spread[pl.ds(k * 4 * LANES + p, LANES, stride=4), :] = column
        part = pl.ds(pl.multiple_of(step * rows, rows), rows)

        def write(b, values):
            normed = values * spread[...]
            place = pl.ds(pl.multiple_of(step * step_rows, step_rows), step_rows)
            lanes = slice(b * LANES, (b + 1) * LANES)
            ready[place, :, lanes] = normed.astype(ready.dtype).reshape(step_rows, 4, LANES)
            squares = (normed * normed).reshape(rows // SUBLANES, SUBLANES, LANES)
            cover[pl.ds(b * SUBLANES, SUBLANES), :] += jnp.sum(squares, axis=0)

        for b, ref in enumerate(near_refs):
            write(far + b, ref[part, :])
        for b in range(far):
            arrive(step, b).wait()
            write(b, held[b, part, :])
        leave(step).start()

    for b in range(len(sens_refs)):
        cover_ref[pl.ds(b, 1), :] = jnp.sum(cover[pl.ds(b * SUBLANES, SUBLANES), :], axis=0, keepdims=True)
    for step in range(steps):
        leave(step).wait()


def scaled(mine, theirs, inverse, far, near, step_rows):
    columns, total = len(far) + len(near), (far + near)[0].shape[0] // 4
    steps = total // step_rows
    near = [pltpu.with_memory_space_constraint(s, pltpu.VMEM) for s in near]
    whole = pl.BlockSpec(memory_space=pltpu.VMEM)
    out, cover = pl.pallas_call(
        functools.partial(scale_kernel, inverse, len(far)),
        in_specs=[whole, whole] + [pl.BlockSpec(memory_space=pltpu.HBM)] * len(far) + [whole] * len(near),
        out_specs=[pl.BlockSpec(memory_space=pltpu.HBM), whole],
        out_shape=[
            jax.ShapeDtypeStruct((total, 4, columns * LANES), jnp.bfloat16),
            jax.ShapeDtypeStruct((columns, LANES), jnp.float32),
        ],
        scratch_shapes=[
            pltpu.VMEM((len(far), total * 4, LANES), jnp.float32),
            pltpu.VMEM((total, 4, columns * LANES), jnp.bfloat16),
            pltpu.VMEM((step_rows * 4, LANES), jnp.float32),
            pltpu.VMEM((columns * SUBLANES, LANES), jnp.float32),
            pltpu.SemaphoreType.DMA((steps, len(far))),
            pltpu.SemaphoreType.DMA((steps,)),
        ],
        compiler_params=pltpu.CompilerParams(vmem_limit_bytes=SCALE_LIMIT),
        name="scaled",
    )(mine.reshape(-1, LANES), theirs.reshape(-1, LANES), *far, *near)
    return out, cover.reshape(columns * LANES)


def sum_over_cells(x, shards):
    if shards & (shards - 1):
        return lax.psum(x, "cell"), jnp.zeros_like(x)
    other, unit = jnp.zeros_like(x), 1
    while unit < shards:
        x = x + other
        size = 4 if unit in (4,) and unit * 4 <= shards else 2
        other = sum(lax.ppermute(x, "cell", [(i, i ^ (k * unit)) for i in range(shards)]) for k in range(1, size))
        unit *= size
    return x, other


def coefficients(horiz, vertical, tilt_angle, azimuth):
    sin_t, cos_t = jnp.sin(tilt_angle), jnp.cos(tilt_angle)
    sin_p, cos_p = jnp.sin(azimuth), jnp.cos(azimuth)
    zero = jnp.zeros_like(horiz)
    return jnp.stack(
        [
            sin_t * cos_p,
            sin_t * sin_p,
            cos_t,
            cos_t * cos_p,
            cos_t * sin_p,
            -sin_t,
            -sin_t * sin_p,
            sin_t * cos_p,
            -horiz,
            -vertical,
            horiz - vertical,
        ]
        + [zero] * 5
    )


def scatter_over_cells(x, shards):
    if shards & (shards - 1):
        return lax.psum_scatter(x, "cell", scatter_dimension=0, tiled=False)
    me, bit = lax.axis_index("cell"), 1
    while bit < shards:
        x = x.reshape((x.shape[0] // 2, 2) + x.shape[1:])
        own = (me // bit) % 2
        kept, sent = (lax.dynamic_index_in_dim(x, k, axis=1, keepdims=False) for k in (own, 1 - own))
        x = kept + lax.ppermute(sent, "cell", [(i, i ^ bit) for i in range(shards)])
        bit *= 2
    return x[0]


def cell_parts(fields, shards):
    cell_dev = fields.shape[2] // shards
    if fields.size * fields.dtype.itemsize <= 16 * MIB:
        return (cell_dev - LANES, LANES)
    return (LANES,) * (cell_dev // LANES)


def transfer_and_solve(ready, fields, quads, tables, properties, kept, pool_rows, shards):
    comps, owned, cells = fields.shape
    cell_dev = cells // shards
    total = quads.shape[1]
    coef = coefficients(*properties)
    rank, slot, place = tables or (None, None, None)
    rows = quads * PAD if rank is None else table_rows(quads, place)
    pool = None
    if pool_rows:
        pool = scatter_over_cells(send_order(fields, slot, pool_rows, shards, 0, cell_dev), shards)
    rows = rows.reshape(-1)
    far, near, before = [], [], jnp.zeros((total // GROUP_ROWS, GROUP_ROWS // LANES, LANES), jnp.float32)

    def finish(received, first, before, last):
        width = received.shape[-1]
        here = last and width == LANES and total * 4 * LANES * 4 <= NEAR_BYTES
        for k in range(width // LANES):
            own = coef[:, first + k * LANES : first + (k + 1) * LANES]
            fill_steps, group_rows = (1, total) if here else (FILL_STEPS, GROUP_ROWS)
            before = before.reshape(total // group_rows, group_rows // LANES, LANES)
            block = first // LANES + k
            values, before = sens_block(
                rows, received, pool, k, block, own, before, here, fill_steps, group_rows
            )
            (near if here else far).append(values)
        return before

    first, received = 0, None
    for width in cell_parts(fields, shards):
        if ready is None:
            ready = send_order(fields, rank, kept, shards, first, width)
        if received is not None:
            ready, received, pool, rows, coef = lax.optimization_barrier((ready, received, pool, rows, coef))
        arriving = lax.all_to_all(ready, "cell", split_axis=0, concat_axis=0, tiled=True)
        if received is not None:
            before = finish(received, first - received.shape[-1], before, False)
        received, ready = arriving, None
        first += width
    before = finish(received, first - received.shape[-1], before, True)
    mine, theirs = sum_over_cells(before, shards)
    return scaled(mine, theirs, 1.0 / (4.0 * cell_dev * shards), far, near, SCALE_ROWS)


def local(fields, horiz, vertical, tilt_angle, azimuth, electrode_quads):
    shards = lax.axis_size("cell")
    owned = fields.shape[0]
    fields = fields.transpose(1, 0, 2)
    quads = electrode_quads.T
    properties = (horiz, vertical, tilt_angle, azimuth)
    if owned % LANES or owned > 2 * LANES:
        return transfer_and_solve(None, fields, quads, None, properties, owned, 0, shards)
    keeps = tuple(owned * part // 32 // ROW_TILE * ROW_TILE for part in KEEPS)
    pool = owned * POOL // 32 // ROW_TILE * ROW_TILE
    ready, tables, chosen = send_first(fields, quads, keeps, pool, shards, cell_parts(fields, shards)[0])

    def branch(k):
        if k == len(keeps):
            return lambda ready, tables, fields, quads, *properties: transfer_and_solve(
                None, fields, quads, None, properties, owned, 0, shards
            )
        return lambda ready, tables, fields, quads, *properties: transfer_and_solve(
            ready[k], fields, quads, tables, properties, keeps[k], 0 if k else pool, shards
        )

    branches = [branch(k) for k in range(len(keeps) + 1)]
    return lax.switch(chosen, branches, ready, tables, fields, quads, *properties)


def solution(mesh):
    placed = (
        P(("grp", "cell"), None, None),
        P(("grp", "cell")),
        P(("grp", "cell")),
        P(("grp", "cell")),
        P(("grp", "cell")),
        P("grp", None),
    )
    return jax.shard_map(
        local,
        mesh=mesh,
        in_specs=placed,
        out_specs=(P("grp", None, "cell"), P(("grp", "cell"))),
        check_vma=False,
    )
```

```python
import functools

import jax
import jax.numpy as jnp
from jax import lax
from jax.experimental import pallas as pl
from jax.experimental.pallas import tpu as pltpu
from jax.sharding import PartitionSpec as P

LANES = 128
SUBLANES = 8
UNROLL = 16
FILL_STEPS = 4
GROUP_ROWS = 512
SCALE_ROWS = 512
ROW_TILE = 16
KEEPS = (28, 30)
POOL = 6
PAD = 4
MIB = 1 << 20
VMEM_LIMIT = 60 * MIB
SENS_LIMIT = 32 * MIB
SCALE_LIMIT = 48 * MIB
NEAR_BYTES = 4 * MIB


def one_hots(quads_ref, column, high):
    index = quads_ref[pl.ds(column, 1), :]
    total = index.shape[1]
    upper = lax.broadcasted_iota(jnp.int32, (high, total), 0) == index // LANES
    lower = lax.broadcasted_iota(jnp.int32, (LANES, total), 0) == index % LANES
    return upper.astype(jnp.bfloat16), lower.astype(jnp.bfloat16)


def named_ranks(quads_ref, high, per, base):
    count = jnp.zeros((high, LANES), jnp.float32)
    for column in range(4):
        upper, lower = one_hots(quads_ref, column, high)
        count += lax.dot_general(upper, lower, (((1,), (1,)), ((), ())), preferred_element_type=jnp.float32)
    named = (count > 0).astype(jnp.bfloat16)

    def dot(a, b):
        return jnp.dot(a.astype(jnp.bfloat16), b.astype(jnp.bfloat16), preferred_element_type=jnp.float32)

    i, j = (lax.broadcasted_iota(jnp.int32, (LANES, LANES), d) for d in range(2))
    within = dot(named, i < j)
    lines = dot(named, jnp.ones((LANES, LANES), jnp.bfloat16))
    i, j = (lax.broadcasted_iota(jnp.int32, (high, high), d) for d in range(2))
    rank = jnp.where(count > 0, within + dot((j < i) & (j // per == i // per), lines), -1.0)
    over = jnp.maximum(dot(j // per == i // per, lines) - base, 0.0)
    ahead = dot((j // per < i // per) & (j % per == 0), over)
    slot = jnp.where(rank >= base, rank - base + ahead, -1.0)
    return rank, slot, ahead + over


def table_rows_kernel(quads_ref, place_ref, rows_ref):
    place = place_ref[...]
    coarse = jnp.floor(place * (1.0 / 16.0))
    fine = place - 16.0 * coarse
    for column in range(4):
        upper, lower = one_hots(quads_ref, column, place.shape[0])

        def pick(part):
            spread = lax.dot_general(
                part.astype(jnp.bfloat16), upper, (((0,), (0,)), ((), ())), preferred_element_type=jnp.float32
            )
            return jnp.sum(spread * lower.astype(jnp.float32), axis=0, keepdims=True)

        rows_ref[pl.ds(column, 1), :] = (pick(coarse) * 16.0 + pick(fine)).astype(jnp.int32) * PAD


def table_rows(quads, place):
    whole = pl.BlockSpec(memory_space=pltpu.VMEM)
    return pl.pallas_call(
        table_rows_kernel,
        in_specs=[whole, whole],
        out_specs=whole,
        out_shape=jax.ShapeDtypeStruct(quads.shape, jnp.int32),
        name="table_rows",
    )(quads, place)


def send_order_kernel(first, fields_ref, out_ref, held, in_sems, out_sems):
    shards, _, _, width = held.shape
    cell_dev = fields_ref.shape[2] // shards
    arrive = [
        pltpu.make_async_copy(fields_ref.at[:, :, pl.ds(d * cell_dev + first, width)], held.at[d], in_sems.at[d])
        for d in range(shards)
    ]
    leave = [pltpu.make_async_copy(held.at[d], out_ref.at[d], out_sems.at[d]) for d in range(shards)]
    for copy in arrive:
        copy.start()
    for d in range(shards):
        arrive[d].wait()
        leave[d].start()
    for copy in leave:
        copy.wait()


def choose_rows(choose, rank_ref):
    kept, owned = choose.shape
    me = lax.axis_index("cell")
    place = lax.broadcasted_iota(jnp.int32, (kept, LANES), 0).astype(jnp.float32)
    for k in range(owned // LANES):
        line = rank_ref[pl.ds(me * (owned // LANES) + k, 1), :]
        choose[:, k * LANES : (k + 1) * LANES] = (place == line).astype(choose.dtype)


def send_chosen(arrive, choose, held, packed, out_ref, out_sems):
    shards, comps = held.shape[:2]
    kept = packed.shape[2]

    def leave(d):
        return pltpu.make_async_copy(packed.at[d], out_ref.at[d], out_sems.at[d])

    @pl.loop(0, shards)
    def _(d):
        arrive(d).wait()
        for comp in range(comps):
            rows = jnp.dot(choose[pl.ds(0, kept), :], held[d, comp], preferred_element_type=jnp.float32)
            packed[d, comp] = rows.astype(packed.dtype)
        leave(d).start()

    @pl.loop(0, shards)
    def _(d):
        leave(d).wait()


def arrival(first, fields_ref, held, in_sems):
    shards, _, _, width = held.shape
    cell_dev = fields_ref.shape[2] // shards

    def arrive(d):
        lanes = pl.ds(pl.multiple_of(d * cell_dev + first, LANES), width)
        return pltpu.make_async_copy(fields_ref.at[:, :, lanes], held.at[d], in_sems.at[d])

    return arrive


def send_named_kernel(first, fields_ref, rank_ref, out_ref, held, packed, choose, in_sems, out_sems):
    arrive = arrival(first, fields_ref, held, in_sems)
    for d in range(held.shape[0]):
        arrive(d).start()
    choose_rows(choose, rank_ref)
    send_chosen(arrive, choose, held, packed, out_ref, out_sems)


def send_first_kernel(keeps, pool, fields_ref, quads_ref, *refs):
    out_refs, (rank_ref, slot_ref, place_ref, chosen_ref, held) = refs[: len(keeps)], refs[len(keeps) : len(keeps) + 5]
    packed, (choose, in_sems, out_sems) = refs[len(keeps) + 5 : -3], refs[-3:]
    arrive = arrival(0, fields_ref, held, in_sems)
    for d in range(held.shape[0]):
        arrive(d).start()
    shards, _, owned, _ = held.shape
    high, per = rank_ref.shape[0], owned // LANES
    rank, slot, taken = named_ranks(quads_ref, high, per, float(keeps[0]))
    rank_ref[...] = rank
    slot_ref[...] = slot
    most = (jnp.max(rank) + 1.0).astype(jnp.int32)
    pooled = (jnp.max(taken) <= pool).astype(jnp.int32)
    chosen = sum((most > kept).astype(jnp.int32) for kept in keeps[1:])
    chosen = (1 - pooled) * (1 + chosen)
    chosen_ref[0] = chosen
    owner = (lax.broadcasted_iota(jnp.int32, (high, LANES), 0) // per).astype(jnp.float32)
    place = jnp.where(slot < 0.0, owner * keeps[0] + rank, slot + shards * keeps[0])
    for k, kept in enumerate(keeps[1:]):
        place = jnp.where(chosen == k + 1, owner * kept + rank, place)
    place_ref[...] = place
    choose_rows(choose, rank_ref)
    for k, kept in enumerate(keeps):

        @pl.when(chosen == k)
        def _():
            send_chosen(arrive, choose, held, packed[k], out_refs[k], out_sems)

    @pl.when(chosen == len(keeps))
    def _():
        for d in range(held.shape[0]):
            arrive(d).wait()


def send_first(fields, quads, keeps, pool, shards, width):
    comps, owned, cells = fields.shape
    sent = [(shards, comps, kept, width) for kept in keeps]
    anywhere, whole = pl.BlockSpec(memory_space=pl.ANY), pl.BlockSpec(memory_space=pltpu.VMEM)
    table = jax.ShapeDtypeStruct((shards * owned // LANES, LANES), jnp.float32)
    *ready, rank, slot, place, chosen = pl.pallas_call(
        functools.partial(send_first_kernel, keeps, pool),
        in_specs=[anywhere, whole],
        out_specs=[anywhere] * len(keeps) + [whole] * 3 + [pl.BlockSpec(memory_space=pltpu.SMEM)],
        out_shape=[jax.ShapeDtypeStruct(shape, fields.dtype) for shape in sent]
        + [table] * 3
        + [jax.ShapeDtypeStruct((1,), jnp.int32)],
        scratch_shapes=[pltpu.VMEM((shards, comps, owned, width), fields.dtype)]
        + [pltpu.VMEM(shape, fields.dtype) for shape in sent]
        + [
            pltpu.VMEM((max(keeps), owned), fields.dtype),
            pltpu.SemaphoreType.DMA((shards,)),
            pltpu.SemaphoreType.DMA((shards,)),
        ],
        compiler_params=pltpu.CompilerParams(vmem_limit_bytes=VMEM_LIMIT),
        name="send_first",
    )(fields, quads)
    return ready, (rank, slot, place), chosen[0]


def send_order(fields, rank, kept, shards, first, width):
    comps, owned, cells = fields.shape
    held = (shards, comps, owned, width)
    sent = (shards, comps, kept, width)
    scratch = [pltpu.VMEM(held, fields.dtype)]
    in_specs, args = [pl.BlockSpec(memory_space=pl.ANY)], [fields]
    if rank is not None:
        scratch += [pltpu.VMEM(sent, fields.dtype), pltpu.VMEM((kept, owned), fields.dtype)]
        in_specs.append(pl.BlockSpec(memory_space=pltpu.VMEM))
        args.append(rank)
    return pl.pallas_call(
        functools.partial(send_order_kernel if rank is None else send_named_kernel, first),
        in_specs=in_specs,
        out_specs=pl.BlockSpec(memory_space=pl.ANY),
        out_shape=jax.ShapeDtypeStruct(sent, fields.dtype),
        scratch_shapes=scratch + [pltpu.SemaphoreType.DMA((shards,)), pltpu.SemaphoreType.DMA((shards,))],
        cost_estimate=pl.CostEstimate(flops=0, bytes_accessed=4 * comps * owned * width * shards, transcendentals=0),
        compiler_params=pltpu.CompilerParams(vmem_limit_bytes=VMEM_LIMIT),
        name="send_order",
    )(*args)


def sens_kernel(sources, fill_steps, group_rows, near, all_rows_ref, fields_ref, coef_ref, before_ref, *refs):
    sens_ref, sumsq_ref, table, picked, squares, rows_ref, rows_sem = refs[-7:]
    step = pl.program_id(0)
    rows_copy = pltpu.make_async_copy(all_rows_ref, rows_ref, rows_sem)

    @pl.when(step == 0)
    def _():
        rows_copy.start()

    @pl.when(step == fill_steps)
    def _():
        rows_copy.wait()
        if len(refs) > 7:
            pool_ref = refs[0]
            pool = pool_ref.shape[1]
            for comp in range(pool_ref.shape[0]):
                values = pool_ref[comp].astype(jnp.float32)
                table[pl.ds(table.shape[0] - pool * PAD + comp, pool, stride=PAD), :] = values

    owned = fields_ref.shape[2]
    batch_rows = SUBLANES * UNROLL
    total_rows = rows_ref.shape[0] // 4

    @pl.when(step < fill_steps)
    def _():
        for source in range(sources):
            place = step * sources + source
            for comp in range(fields_ref.shape[1]):
                values = fields_ref[place if near else source, comp].astype(jnp.float32)
                table[pl.ds(place * (owned * PAD) + comp, owned, stride=PAD), :] = values

    @pl.when(step >= fill_steps)
    def _():
        first = (step - fill_steps) * group_rows
        coef = [coef_ref[pl.ds(k, 1), :] for k in range(11)]
        ax, ay, az, tx, ty, tz, ux, uy, nh, nv, nc = coef

        def fetch(index):
            return table[pl.ds(pl.multiple_of(rows_ref[index], PAD), PAD), :]

        def close(batch):
            turned = squares[pl.ds(pl.multiple_of(batch * batch_rows, batch_rows), batch_rows), :].T
            total = jnp.sum(turned, axis=0, keepdims=True)
            sumsq_ref[0, pl.ds(batch, 1), :] = total + before_ref[0, pl.ds(batch, 1), :]

        squares[pl.ds(0, batch_rows), :] = jnp.zeros((batch_rows, LANES), jnp.float32)

        @pl.loop(0, group_rows // batch_rows)
        def _(batch):
            close(jnp.maximum(batch - 1, 0))
            base = first + batch * batch_rows
            for j in range(batch_rows):
                i = base + j
                picked[pl.ds(j * PAD, PAD), :] = fetch(i) - fetch(total_rows + i)
                picked[pl.ds((batch_rows + j) * PAD, PAD), :] = fetch(2 * total_rows + i) - fetch(3 * total_rows + i)
            for g in range(UNROLL):
                start = g * SUBLANES
                sx, sy, sz = (picked[pl.ds(start * PAD + k, SUBLANES, stride=PAD), :] for k in range(3))
                rx, ry, rz = (picked[pl.ds((batch_rows + start) * PAD + k, SUBLANES, stride=PAD), :] for k in range(3))
                sn = sx * ax + sy * ay + sz * az
                rn = rx * ax + ry * ay + rz * az
                st = sx * tx + sy * ty + sz * tz
                rt = rx * tx + ry * ty + rz * tz
                sp = sx * ux + sy * uy
                rp = rx * ux + ry * uy
                dot = sx * rx + sy * ry + sz * rz
                both = sn * rn
                values = (nh * (dot - both), nv * both, nc * (st * rn + sn * rt), nc * (sp * rn + sn * rp))
                place = ((base if near else batch * batch_rows) + start) * 4
                for k in range(4):
                    sens_ref[pl.ds(place + k, SUBLANES, stride=4), :] = values[k]
                squares[pl.ds(batch * batch_rows + start, SUBLANES), :] = (
                    values[0] * values[0] + values[1] * values[1] + values[2] * values[2] + values[3] * values[3]
                )

        close(group_rows // batch_rows - 1)


def sens_block(rows, fields, pool, lane_block, cell_block, coef, before, near, fill_steps, group_rows):
    shards, comps, owned, _ = fields.shape
    total = rows.size // 4
    groups = total // group_rows
    if near:
        fields_spec = sens_spec = pl.BlockSpec(memory_space=pltpu.VMEM)
        sens_shape = pltpu.VMEM((total * 4, LANES), jnp.float32)
    else:
        sens_spec = pl.BlockSpec((group_rows * 4, LANES), lambda i: (jnp.maximum(i - fill_steps, 0), 0))
        sens_shape = pltpu.HBM((total * 4, LANES), jnp.float32)
        fields_spec = pl.BlockSpec(
            (shards // fill_steps, comps, owned, LANES), lambda i: (jnp.minimum(i, fill_steps - 1), 0, 0, lane_block)
        )
    sums = pl.BlockSpec((1, group_rows // LANES, LANES), lambda i: (jnp.maximum(i - fill_steps, 0), 0, 0))
    pools = [] if pool is None else [pool]
    pool_rows = sum(p.shape[1] for p in pools)
    return pl.pallas_call(
        functools.partial(sens_kernel, shards // fill_steps, fill_steps, group_rows, near),
        grid=(fill_steps + groups,),
        in_specs=[
            pl.BlockSpec(memory_space=pl.ANY),
            fields_spec,
            pl.BlockSpec((16, LANES), lambda i: (0, 0)),
            sums,
        ]
        + [pl.BlockSpec((comps, pool_rows, LANES), lambda i: (0, 0, cell_block)) for _ in pools],
        out_specs=[sens_spec, sums],
        out_shape=[
            sens_shape,
            jax.ShapeDtypeStruct((groups, group_rows // LANES, LANES), jnp.float32),
        ],
        scratch_shapes=[
            pltpu.VMEM(((shards * owned + pool_rows) * PAD, LANES), jnp.float32),
            pltpu.VMEM((2 * UNROLL * SUBLANES * PAD, LANES), jnp.float32),
            pltpu.VMEM((group_rows, LANES), jnp.float32),
            pltpu.SMEM(rows.shape, jnp.int32),
            pltpu.SemaphoreType.DMA,
        ],
        cost_estimate=pl.CostEstimate(
            flops=total * LANES * 64,
            bytes_accessed=(shards * comps * owned * LANES * 2 + total * 5 * LANES * 4) * 4,
            transcendentals=0,
        ),
        compiler_params=pltpu.CompilerParams(vmem_limit_bytes=SENS_LIMIT),
        name="sens_block",
    )(rows, fields, coef, before, *pools)


def scale_kernel(inverse, far, mine_ref, theirs_ref, *refs):
    sens_refs, (out_ref, cover_ref, held, ready, spread, cover, in_sems, out_sems) = refs[:-8], refs[-8:]
    far_refs, near_refs = sens_refs[:far], sens_refs[far:]
    rows = spread.shape[0]
    step_rows = rows // 4
    steps = ready.shape[0] // step_rows

    def arrive(step, b):
        part = pl.ds(pl.multiple_of(step * rows, rows), rows)
        return pltpu.make_async_copy(far_refs[b].at[part], held.at[b, part], in_sems.at[step, b])

    def leave(step):
        part = pl.ds(pl.multiple_of(step * step_rows, step_rows), step_rows)
        return pltpu.make_async_copy(ready.at[part], out_ref.at[part], out_sems.at[step])

    for step in range(steps):
        for b in range(far):
            arrive(step, b).start()
    cover[...] = jnp.zeros_like(cover)

    @pl.loop(0, steps)
    def _(step):
        for k in range(step_rows // LANES):
            line = pl.ds(step * (step_rows // LANES) + k, 1)
            meansq = (mine_ref[line, :] + theirs_ref[line, :]) * inverse
            column = jnp.broadcast_to(lax.rsqrt(meansq + 1e-06), (LANES, LANES)).T
            for p in range(4):
                spread[pl.ds(k * 4 * LANES + p, LANES, stride=4), :] = column
        part = pl.ds(pl.multiple_of(step * rows, rows), rows)

        def write(b, values):
            normed = values * spread[...]
            place = pl.ds(pl.multiple_of(step * step_rows, step_rows), step_rows)
            lanes = slice(b * LANES, (b + 1) * LANES)
            ready[place, :, lanes] = normed.astype(ready.dtype).reshape(step_rows, 4, LANES)
            squares = (normed * normed).reshape(rows // SUBLANES, SUBLANES, LANES)
            cover[pl.ds(b * SUBLANES, SUBLANES), :] += jnp.sum(squares, axis=0)

        for b, ref in enumerate(near_refs):
            write(far + b, ref[part, :])
        for b in range(far):
            arrive(step, b).wait()
            write(b, held[b, part, :])
        leave(step).start()

    for b in range(len(sens_refs)):
        cover_ref[pl.ds(b, 1), :] = jnp.sum(cover[pl.ds(b * SUBLANES, SUBLANES), :], axis=0, keepdims=True)
    for step in range(steps):
        leave(step).wait()


def scaled(mine, theirs, inverse, far, near, step_rows):
    columns, total = len(far) + len(near), (far + near)[0].shape[0] // 4
    steps = total // step_rows
    near = [pltpu.with_memory_space_constraint(s, pltpu.VMEM) for s in near]
    whole = pl.BlockSpec(memory_space=pltpu.VMEM)
    out, cover = pl.pallas_call(
        functools.partial(scale_kernel, inverse, len(far)),
        in_specs=[whole, whole] + [pl.BlockSpec(memory_space=pltpu.HBM)] * len(far) + [whole] * len(near),
        out_specs=[pl.BlockSpec(memory_space=pltpu.HBM), whole],
        out_shape=[
            jax.ShapeDtypeStruct((total, 4, columns * LANES), jnp.bfloat16),
            jax.ShapeDtypeStruct((columns, LANES), jnp.float32),
        ],
        scratch_shapes=[
            pltpu.VMEM((len(far), total * 4, LANES), jnp.float32),
            pltpu.VMEM((total, 4, columns * LANES), jnp.bfloat16),
            pltpu.VMEM((step_rows * 4, LANES), jnp.float32),
            pltpu.VMEM((columns * SUBLANES, LANES), jnp.float32),
            pltpu.SemaphoreType.DMA((steps, len(far))),
            pltpu.SemaphoreType.DMA((steps,)),
        ],
        compiler_params=pltpu.CompilerParams(vmem_limit_bytes=SCALE_LIMIT),
        name="scaled",
    )(mine.reshape(-1, LANES), theirs.reshape(-1, LANES), *far, *near)
    return out, cover.reshape(columns * LANES)


def sum_over_cells(x, shards):
    if shards & (shards - 1):
        return lax.psum(x, "cell"), jnp.zeros_like(x)
    other, unit = jnp.zeros_like(x), 1
    while unit < shards:
        x = x + other
        size = 4 if unit in (4,) and unit * 4 <= shards else 2
        other = sum(lax.ppermute(x, "cell", [(i, i ^ (k * unit)) for i in range(shards)]) for k in range(1, size))
        unit *= size
    return x, other


def coefficients(horiz, vertical, tilt_angle, azimuth):
    sin_t, cos_t = jnp.sin(tilt_angle), jnp.cos(tilt_angle)
    sin_p, cos_p = jnp.sin(azimuth), jnp.cos(azimuth)
    zero = jnp.zeros_like(horiz)
    return jnp.stack(
        [
            sin_t * cos_p,
            sin_t * sin_p,
            cos_t,
            cos_t * cos_p,
            cos_t * sin_p,
            -sin_t,
            -sin_t * sin_p,
            sin_t * cos_p,
            -horiz,
            -vertical,
            horiz - vertical,
        ]
        + [zero] * 5
    )


def scatter_over_cells(x, shards):
    if shards & (shards - 1):
        return lax.psum_scatter(x, "cell", scatter_dimension=0, tiled=False)
    me, bit = lax.axis_index("cell"), 1
    while bit < shards:
        x = x.reshape((x.shape[0] // 2, 2) + x.shape[1:])
        own = (me // bit) % 2
        kept, sent = (lax.dynamic_index_in_dim(x, k, axis=1, keepdims=False) for k in (own, 1 - own))
        x = kept + lax.ppermute(sent, "cell", [(i, i ^ bit) for i in range(shards)])
        bit *= 2
    return x[0]


def cell_parts(fields, shards):
    cell_dev = fields.shape[2] // shards
    if fields.size * fields.dtype.itemsize <= 16 * MIB:
        return (cell_dev - LANES, LANES)
    return (LANES,) * (cell_dev // LANES)


def transfer_and_solve(ready, fields, quads, tables, properties, kept, pool_rows, shards):
    comps, owned, cells = fields.shape
    cell_dev = cells // shards
    total = quads.shape[1]
    coef = coefficients(*properties)
    rank, slot, place = tables or (None, None, None)
    rows = quads * PAD if rank is None else table_rows(quads, place)
    pool = None
    if pool_rows:
        pool = scatter_over_cells(send_order(fields, slot, pool_rows, shards, 0, cell_dev), shards)
    rows = rows.reshape(-1)
    far, near, before = [], [], jnp.zeros((total // GROUP_ROWS, GROUP_ROWS // LANES, LANES), jnp.float32)

    def finish(received, first, before, last):
        width = received.shape[-1]
        here = last and width == LANES and total * 4 * LANES * 4 <= NEAR_BYTES
        for k in range(width // LANES):
            own = coef[:, first + k * LANES : first + (k + 1) * LANES]
            fill_steps, group_rows = (1, total) if here else (FILL_STEPS, GROUP_ROWS)
            before = before.reshape(total // group_rows, group_rows // LANES, LANES)
            block = first // LANES + k
            values, before = sens_block(
                rows, received, pool, k, block, own, before, here, fill_steps, group_rows
            )
            (near if here else far).append(values)
        return before

    first, received = 0, None
    for width in cell_parts(fields, shards):
        if ready is None:
            ready = send_order(fields, rank, kept, shards, first, width)
        if received is not None:
            ready, received, pool, rows, coef = lax.optimization_barrier((ready, received, pool, rows, coef))
        arriving = lax.all_to_all(ready, "cell", split_axis=0, concat_axis=0, tiled=True)
        if received is not None:
            before = finish(received, first - received.shape[-1], before, False)
        received, ready = arriving, None
        first += width
    before = finish(received, first - received.shape[-1], before, True)
    mine, theirs = sum_over_cells(before, shards)
    return scaled(mine, theirs, 1.0 / (4.0 * cell_dev * shards), far, near, SCALE_ROWS)


def local(fields, horiz, vertical, tilt_angle, azimuth, electrode_quads):
    shards = lax.axis_size("cell")
    owned = fields.shape[0]
    fields = fields.transpose(1, 0, 2)
    quads = electrode_quads.T
    properties = (horiz, vertical, tilt_angle, azimuth)
    if owned % LANES or owned > 2 * LANES:
        return transfer_and_solve(None, fields, quads, None, properties, owned, 0, shards)
    keeps = tuple(owned * part // 32 // ROW_TILE * ROW_TILE for part in KEEPS)
    pool = owned * POOL // 32 // ROW_TILE * ROW_TILE
    ready, tables, chosen = send_first(fields, quads, keeps, pool, shards, cell_parts(fields, shards)[0])

    def branch(k):
        if k == len(keeps):
            return lambda ready, tables, fields, quads, *properties: transfer_and_solve(
                None, fields, quads, None, properties, owned, 0, shards
            )
        return lambda ready, tables, fields, quads, *properties: transfer_and_solve(
            ready[k], fields, quads, tables, properties, keeps[k], 0 if k else pool, shards
        )

    branches = [branch(k) for k in range(len(keeps) + 1)]
    return lax.switch(chosen, branches, ready, tables, fields, quads, *properties)


def solution(mesh):
    placed = (
        P(("grp", "cell"), None, None),
        P(("grp", "cell")),
        P(("grp", "cell")),
        P(("grp", "cell")),
        P(("grp", "cell")),
        P("grp", None),
    )
    return jax.shard_map(
        local,
        mesh=mesh,
        in_specs=placed,
        out_specs=(P("grp", None, "cell"), P(("grp", "cell"))),
        check_vma=False,
    )
```
